256 devices in a mesh: dp: 16 (over x_lo, y, core), pipe: 16 (over x_hi, z).
Axes of the slice: x: 4 (x_hi: 2, x_lo: 2; x = x_hi * 2 + x_lo), y: 4, z: 8, core: 2. Of those that a mesh axis runs over, the one named last changes fastest.
Arguments:
- hidden: bfloat16 [512, 4608], P(('dp', 'pipe')), may hold values from -6 to 6
- norm_gain: float32 [4608], replicated, may hold values from 0.5 to 1.5
- weight: bfloat16 [131072, 4608], P(('dp', 'pipe')), may hold values from -0.25 to 0.25
- targets: int32 [512], replicated, may hold values from 0 to 131071
Outputs:
- token_loss: float32 [512], P(('dp', 'pipe'))
- grad_hidden: float32 [512, 4608], P(('dp', 'pipe'))
- grad_weight: bfloat16 [131072, 4608], P(('dp', 'pipe'))
- grad_gain: float32 [4608], replicated
The draws below stay inside these ranges and needn't reach their ends.
All inputs are finite; a program needn't handle non-finite values.
Results may differ from the reference program's by a relative error of at most 0.0055.
Values may be sent and summed in bfloat16 or wider, within the bound.
No kernel may reach another device: no remote copies, remote signals or barrier semaphores. Data moves between devices by JAX's collectives and lax.ppermute only.
A program may use at most 128 MiB of HBM per device.

```python
import math
import jax
import jax.numpy as jnp
import numpy as np
from jax import lax

D = 4608
TOKENS = 512
VOCAB = 131072


def plant(values, key, low, top_value):
    longest = values.shape.index(max(values.shape))
    spots = []
    for shift in (0, 1):
        where = [jax.random.randint(jax.random.fold_in(key, axis), (), 0, length) for axis, length in enumerate(values.shape)]
        where[longest] = (where[longest] + shift) % values.shape[longest]
        spots.append(tuple(where))
    return values.at[spots[0]].set(low).at[spots[1]].set(top_value)


def level_of(key, shape, shards, least, largest):
    def one(position, blocks):
        heights = jax.random.uniform(jax.random.fold_in(jax.random.fold_in(key, 6), position), (blocks,), jnp.float32, least / len(shards), largest / len(shards))
        return jnp.repeat(jnp.exp(heights), shape[position] // blocks).reshape((-1,) + (1,) * (len(shape) - position - 1))

    factor_of = one(*shards[0])
    for cut in shards[1:]:
        factor_of = factor_of * one(*cut)
    return factor_of


def ranked_wide(own_key, shape, amount, lean):
    loads = [min(1 << octave, amount + 1 - (1 << octave)) * (1 << 20) // math.isqrt((1 << octave) ** lean) + 1 for octave in range((amount + 1).bit_length()) if 1 << octave <= amount]
    width = 1 + sum(loads) // (1 << 30)
    table = np.cumsum(np.array([max(1, weight // width) for weight in loads]))
    lot = jax.random.randint(jax.random.fold_in(own_key, 1), shape, 0, int(table[len(loads) - 1]))
    start = jnp.left_shift(1, jnp.searchsorted(jnp.asarray(table, jnp.int32), lot, side="right").astype(jnp.int32))
    rank = start - 1 + jax.random.randint(jax.random.fold_in(own_key, 4), shape, 0, 1 << 30) % jnp.minimum(start, amount + 1 - start)
    return jax.random.permutation(jax.random.fold_in(own_key, 2), amount)[rank].astype(jnp.int32)


def bell_draw(rng, dims, deviation, reach, pieces=(), held_as=jnp.bfloat16):
    result = deviation * jax.random.normal(rng, dims, jnp.float32)
    if pieces:
        result = result * level_of(rng, dims, pieces, -0.22, 0.18)
    return jnp.clip(result, -reach, reach).astype(held_as)


def setup_inputs(seed: int = 0) -> dict:
    streams_of = jax.random.split(jax.random.key(seed), 5)
    hidden = bell_draw(streams_of[0], (TOKENS, D), 1.0, 6.0, ((0, 256),))
    norm_gain = jnp.clip(1.0 + 0.1 * jax.random.normal(streams_of[1], (D,), jnp.float32), 0.5, 1.5)
    weight = bell_draw(streams_of[2], (VOCAB, D), (D // 9) ** -0.5, 0.25, ((0, 256),))
    targets = plant(ranked_wide(streams_of[3], (TOKENS,), VOCAB, 2), jax.random.fold_in(streams_of[3], 3), 0, VOCAB - 1).astype(jnp.int32)
    return dict(hidden=hidden, norm_gain=norm_gain, weight=weight, targets=targets)


epsilon = 1e-06
cap_value = 30.0
entropy_weight = 0.2

def reference(hidden, norm_gain, weight, targets):
    values = hidden.astype(jnp.float32)
    inverse = lax.rsqrt(lax.optimization_barrier(jnp.mean(values * values, axis=-1, keepdims=True)) + epsilon)
    unit_rows = values * inverse
    normed = (unit_rows * norm_gain).astype(jnp.bfloat16)
    logits = lax.dot_general(normed, weight, (((1,), (1,)), ((), ())), preferred_element_type=jnp.float32)
    capped = cap_value * jnp.tanh(logits / cap_value)
    powers = jnp.exp(capped - cap_value)
    total_exp = lax.optimization_barrier(jnp.sum(powers, axis=-1))
    total_weighted = lax.optimization_barrier(jnp.sum(powers * capped, axis=-1))
    columns = jnp.arange(VOCAB, dtype=jnp.int32)
    target_hit = targets[:, None] == columns[None, :]
    target_logit = lax.optimization_barrier(jnp.sum(jnp.where(target_hit, capped, 0.0), axis=-1))
    log_total = cap_value + jnp.log(total_exp)
    mean_logit = total_weighted / total_exp
    token_loss = log_total - target_logit - entropy_weight * (log_total - mean_logit)
    probs = jnp.exp(capped - log_total[:, None])
    raw_grad = probs - target_hit.astype(probs.dtype) + entropy_weight * probs * (capped - mean_logit[:, None])
    ratio = capped / cap_value
    logit_grad = (raw_grad * (1.0 - ratio * ratio)).astype(jnp.bfloat16)
    grad_weight = lax.dot_general(logit_grad, normed, (((0,), (0,)), ((), ())), preferred_element_type=jnp.float32).astype(jnp.bfloat16)
    grad_normed = jnp.dot(logit_grad, weight, preferred_element_type=jnp.float32)
    grad_gain = lax.optimization_barrier(jnp.sum(grad_normed * unit_rows, axis=0))
    scaled = norm_gain * grad_normed
    grad_hidden = (scaled - unit_rows * lax.optimization_barrier(jnp.mean(scaled * unit_rows, axis=-1, keepdims=True))) * inverse
    return (token_loss, grad_hidden, grad_weight, grad_gain)
```

```python
import jax
import jax.numpy as jnp
from jax import lax
from jax.sharding import Mesh, PartitionSpec as P

epsilon = 1e-06
cap_value = 30.0
entropy_weight = 0.2

AXES = ("x_lo", "y", "core", "x_hi", "z")
PLANE = ("x_lo", "y", "x_hi")


def gather_over(block, axes, size):
    copies = jnp.broadcast_to(block[None], (size,) + block.shape)
    return lax.all_to_all(copies, axes, 0, 0, tiled=True)


def sum_over(block, axes, size):
    return jnp.sum(gather_over(block, axes, size), axis=0)


def swap_cores(block):
    return lax.ppermute(block, "core", [(0, 1), (1, 0)])


def on_device(hidden, norm_gain, weight, targets):
    own_rows, width = hidden.shape
    vocab_rows = weight.shape[0]
    values = hidden.astype(jnp.float32)
    inverse = lax.rsqrt(jnp.mean(values * values, axis=-1, keepdims=True) + epsilon)
    unit_rows = values * inverse
    normed = (unit_rows * norm_gain).astype(jnp.bfloat16)

    line = gather_over(normed, "z", 8).reshape(16, width)
    near = gather_over(line, PLANE, 16).reshape(256, width)
    far = swap_cores(near)

    position = lax.axis_index(AXES)
    core = lax.axis_index("core")
    columns = position * vocab_rows + lax.iota(jnp.int32, vocab_rows)
    by_core = targets.reshape(8, 2, 32)
    near_targets = lax.dynamic_index_in_dim(by_core, core, 1, False).reshape(256)
    far_targets = lax.dynamic_index_in_dim(by_core, 1 - core, 1, False).reshape(256)

    def forward(rows, ids):
        logits = lax.dot_general(
            rows, weight, (((1,), (1,)), ((), ())), preferred_element_type=jnp.float32
        )
        capped = cap_value * jnp.tanh(logits / cap_value)
        powers = jnp.exp(capped - cap_value)
        hit = ids[:, None] == columns[None, :]
        sums = jnp.stack([
            jnp.sum(powers, axis=-1),
            jnp.sum(powers * capped, axis=-1),
            jnp.sum(jnp.where(hit, capped, 0.0), axis=-1),
        ])
        return capped, hit, sums

    near_capped, near_hit, near_sums = forward(near, near_targets)
    far_capped, far_hit, far_sums = forward(far, far_targets)
    stats = jnp.stack([near_sums, far_sums], axis=1)
    stats = stats + swap_cores(stats)[:, ::-1]
    stats = sum_over(stats, PLANE, 16)
    stats = sum_over(stats, "z", 8)
    total_exp, total_weighted, target_logit = stats
    log_total = cap_value + jnp.log(total_exp)
    mean_logit = total_weighted / total_exp
    every_loss = log_total - target_logit - entropy_weight * (log_total - mean_logit)
    place = (lax.axis_index(PLANE) * 8 + lax.axis_index("z")) * own_rows
    token_loss = lax.dynamic_slice_in_dim(every_loss[0], place, own_rows, 0)

    def backward(capped, hit, half):
        probs = jnp.exp(capped - log_total[half][:, None])
        raw_grad = (
            probs
            - hit.astype(jnp.float32)
            + entropy_weight * probs * (capped - mean_logit[half][:, None])
        )
        ratio = capped / cap_value
        return (raw_grad * (1.0 - ratio * ratio)).astype(jnp.bfloat16)

    far_grad = backward(far_capped, far_hit, 1)
    far_part = jnp.dot(far_grad, weight, preferred_element_type=jnp.float32).astype(jnp.bfloat16)
    arrived = swap_cores(far_part)
    near_grad = backward(near_capped, near_hit, 0)
    near_part = jnp.dot(near_grad, weight, preferred_element_type=jnp.float32)
    pair_part = (near_part + arrived.astype(jnp.float32)).astype(jnp.bfloat16)
    grad_weight = (
        lax.dot_general(near_grad, near, (((0,), (0,)), ((), ())), preferred_element_type=jnp.float32)
        + lax.dot_general(far_grad, far, (((0,), (0,)), ((), ())), preferred_element_type=jnp.float32)
    ).astype(jnp.bfloat16)
    plane_parts = lax.all_to_all(pair_part.reshape(16, 16, width), PLANE, 0, 0, tiled=True)
    line_part = jnp.sum(plane_parts.astype(jnp.float32), axis=0).astype(jnp.bfloat16)
    line_parts = lax.all_to_all(line_part.reshape(8, 2, width), "z", 0, 0, tiled=True)
    grad_normed = jnp.sum(line_parts.astype(jnp.float32), axis=0)

    gain_part = jnp.sum(grad_normed * unit_rows, axis=0)
    gain_part = sum_over(gain_part, "z", 8)
    gain_part = sum_over(gain_part, PLANE, 16)
    grad_gain = gain_part + swap_cores(gain_part)
    scaled = norm_gain * grad_normed
    grad_hidden = (
        scaled - unit_rows * jnp.mean(scaled * unit_rows, axis=-1, keepdims=True)
    ) * inverse
    return (token_loss, grad_hidden, grad_weight, grad_gain)


def solution(mesh):
    fine = Mesh(mesh.devices.reshape(2, 4, 2, 2, 8), AXES)
    rows = P(AXES, None)
    return jax.shard_map(
        on_device,
        mesh=fine,
        in_specs=(rows, P(), rows, P()),
        out_specs=(P(AXES), rows, rows, P()),
        check_vma=False,
    )
```

```python
import jax
import jax.numpy as jnp
from jax import lax
from jax.experimental import pallas as pl
from jax.experimental.pallas import tpu as pltpu
from jax.sharding import Mesh, PartitionSpec as P

epsilon = 1e-06
cap_value = 30.0
entropy_weight = 0.2

AXES = ("x_lo", "y", "core", "x_hi", "z")
PLANE = ("x_lo", "y", "x_hi")
WIDTH = 4608
HALF = WIDTH // 2
TOKENS = 512
NEAR = TOKENS // 2
VOCAB_ROWS = 512
PIECE = 16
STEP = 768
STEPS = WIDTH // STEP
HALF_STEPS = HALF // STEP
VMEM_BYTES = 40 * 1024 * 1024

RING = (0, 2, 1, 3)


def shift_y(block, step):
    return lax.ppermute(block, "y", [(p, (p + step) % 4) for p in range(4)])


def shift_x(block, step):
    pairs = [(RING[p], RING[(p + step) % 4]) for p in range(4)]
    return lax.ppermute(block, ("x_lo", "x_hi"), pairs)


def swap_cores(block):
    return lax.ppermute(block, "core", [(0, 1), (1, 0)])


def gather_over(block, axes, size):
    copies = jnp.broadcast_to(block[None], (size,) + block.shape)
    return lax.all_to_all(copies, axes, 0, 0, tiled=True)


def sum_over(block, axes, size):
    return jnp.sum(gather_over(block, axes, size), axis=0)


def gather_ring(block, shift):
    up, down, across = shift(block, 3), shift(block, 1), shift(block, 2)
    return [block, up, across, down]


def scatter_ring(blocks, shift):
    up, down, across = shift(blocks[1], 1), shift(blocks[3], 3), shift(blocks[2], 2)
    return (
        blocks[0].astype(jnp.float32)
        + up.astype(jnp.float32)
        + down.astype(jnp.float32)
        + across.astype(jnp.float32)
    )


def piece_row(core, y, x):
    return pl.multiple_of((core * 16 + y * 4 + x) * PIECE, PIECE)


def forward_kernel(place, targets, weight, *rest):
    blocks = rest[:16]
    gathered, capped_out, stats_out, weight_held, rows_held, weight_sems, row_sems, out_sem = rest[16:]
    core, y, x, position = place[0], place[1], place[2], place[3]

    def half_columns(half):
        return pl.ds(half * HALF, HALF)

    weight_copies = []
    row_copies = ([], [])
    for half in range(2):
        copy = pltpu.make_async_copy(
            weight.at[:, half_columns(half)],
            weight_held.at[:, half_columns(half)],
            weight_sems.at[half],
        )
        copy.start()
        weight_copies.append(copy)
        for far in range(2):
            owner = core if far == 0 else 1 - core
            for outer in range(4):
                block = blocks[far * 8 + half * 4 + outer]
                for inner in range(4):
                    up_y, up_x = (outer, inner) if half == 0 else (inner, outer)
                    row = piece_row(owner, lax.rem(y + up_y, 4), lax.rem(x + up_x, 4))
                    copy = pltpu.make_async_copy(
                        block.at[pl.ds(inner * PIECE, PIECE), :],
                        rows_held.at[pl.ds(row, PIECE), half_columns(half)],
                        row_sems.at[half * 32 + far * 16 + outer * 4 + inner],
                    )
                    copy.start()
                    row_copies[half].append(copy)

    logits = None
    for half in range(2):
        weight_copies[half].wait()
        for copy in row_copies[half]:
            copy.wait()
        columns = slice(half * HALF, (half + 1) * HALF)
        part = lax.dot_general(
            weight_held[:, columns],
            rows_held[:, columns],
            (((1,), (1,)), ((), ())),
            preferred_element_type=jnp.float32,
        )
        logits = part if logits is None else logits + part
    out_copy = pltpu.make_async_copy(rows_held, gathered, out_sem)
    out_copy.start()
    capped = cap_value * jnp.tanh(logits / cap_value)
    capped_out[...] = capped
    powers = jnp.exp(capped - cap_value)
    entry = position * VOCAB_ROWS + lax.broadcasted_iota(jnp.int32, capped.shape, 0)
    hit = targets[...] == entry
    stats_out[0:1, :] = jnp.sum(powers, axis=0, keepdims=True)
    stats_out[1:2, :] = jnp.sum(powers * capped, axis=0, keepdims=True)
    stats_out[2:3, :] = jnp.sum(jnp.where(hit, capped, 0.0), axis=0, keepdims=True)
    out_copy.wait()


def forward(place, targets, weight, blocks):
    vmem, hbm = pl.BlockSpec(memory_space=pltpu.VMEM), pl.BlockSpec(memory_space=pl.ANY)
    return pl.pallas_call(
        forward_kernel,
        out_shape=(
            jax.ShapeDtypeStruct((TOKENS, WIDTH), jnp.bfloat16),
            jax.ShapeDtypeStruct((VOCAB_ROWS, TOKENS), jnp.float32),
            jax.ShapeDtypeStruct((3, TOKENS), jnp.float32),
        ),
        in_specs=[pl.BlockSpec(memory_space=pltpu.SMEM), vmem] + [hbm] * 17,
        out_specs=(hbm, vmem, vmem),
        scratch_shapes=[
            pltpu.VMEM((VOCAB_ROWS, WIDTH), jnp.bfloat16),
            pltpu.VMEM((TOKENS, WIDTH), jnp.bfloat16),
            pltpu.SemaphoreType.DMA((2,)),
            pltpu.SemaphoreType.DMA((64,)),
            pltpu.SemaphoreType.DMA,
        ],
        compiler_params=pltpu.CompilerParams(vmem_limit_bytes=VMEM_BYTES),
        cost_estimate=pl.CostEstimate(
            flops=2 * VOCAB_ROWS * TOKENS * WIDTH, bytes_accessed=16 << 20, transcendentals=1 << 19
        ),
        name="forward",
    )(place, targets, weight, *blocks)


def far_kernel(place, targets, capped, totals, weight, grad_out, turned_out, far_out):
    core, position = place[0], place[3]

    @pl.when(pl.program_id(0) == 0)
    def _():
        log_total = cap_value + jnp.log(totals[0:1, :])
        mean_logit = totals[1:2, :] / totals[0:1, :]
        values = capped[...]
        probs = jnp.exp(values - log_total)
        entry = position * VOCAB_ROWS + lax.broadcasted_iota(jnp.int32, values.shape, 0)
        hit = (targets[...] == entry).astype(jnp.float32)
        raw_grad = probs - hit + entropy_weight * probs * (values - mean_logit)
        ratio = values / cap_value
        grad = raw_grad * (1.0 - ratio * ratio)
        grad_out[...] = grad.astype(jnp.bfloat16)
        turned_out[...] = grad.T.astype(jnp.bfloat16)

    far = pl.multiple_of((1 - core) * NEAR, NEAR)
    far_out[...] = jnp.dot(
        turned_out[pl.ds(far, NEAR), :], weight[...], preferred_element_type=jnp.float32
    ).astype(jnp.bfloat16)


def far_gradient(place, targets, capped, totals, weight):
    whole = lambda rows, columns: pl.BlockSpec((rows, columns), lambda j, place: (0, 0))
    return pl.pallas_call(
        far_kernel,
        out_shape=(
            jax.ShapeDtypeStruct((VOCAB_ROWS, TOKENS), jnp.bfloat16),
            jax.ShapeDtypeStruct((TOKENS, VOCAB_ROWS), jnp.bfloat16),
            jax.ShapeDtypeStruct((NEAR, WIDTH), jnp.bfloat16),
        ),
        grid_spec=pltpu.PrefetchScalarGridSpec(
            num_scalar_prefetch=1,
            grid=(STEPS,),
            in_specs=[
                whole(1, TOKENS),
                whole(VOCAB_ROWS, TOKENS),
                whole(3, TOKENS),
                pl.BlockSpec((VOCAB_ROWS, STEP), lambda j, place: (0, j)),
            ],
            out_specs=[
                whole(VOCAB_ROWS, TOKENS),
                whole(TOKENS, VOCAB_ROWS),
                pl.BlockSpec((NEAR, STEP), lambda j, place: (0, j)),
            ],
        ),
        compiler_params=pltpu.CompilerParams(vmem_limit_bytes=VMEM_BYTES),
        cost_estimate=pl.CostEstimate(
            flops=2 * VOCAB_ROWS * NEAR * WIDTH, bytes_accessed=9 << 20, transcendentals=1 << 18
        ),
        name="far_gradient",
    )(place, targets, capped, totals, weight)


def near_kernel(place, turned, weight, arrived, rows, *rest):
    sends, gain_out, held = rest[:8], rest[8], rest[9]
    y, x = place[1], place[2]
    j = pl.program_id(0)
    part = jnp.dot(turned[...], weight[...], preferred_element_type=jnp.float32)
    part = part + arrived[...].astype(jnp.float32)
    gain_out[...] = jnp.sum(part * rows[...].astype(jnp.float32), axis=0, keepdims=True)
    held[...] = part.reshape(16, PIECE, STEP)

    def store(half):
        for outer in range(4):
            for inner in range(4):
                up_y, up_x = (outer, inner) if half == 0 else (inner, outer)
                piece = held[lax.rem(y + up_y, 4) * 4 + lax.rem(x + up_x, 4)]
                sends[half * 4 + outer][inner * PIECE : (inner + 1) * PIECE, :] = piece.astype(jnp.bfloat16)

    pl.when(j < HALF_STEPS)(lambda: store(0))
    pl.when(j >= HALF_STEPS)(lambda: store(1))


def near_gradient(place, turned, weight, arrived, rows):
    first = pl.BlockSpec((64, STEP), lambda j, place: (0, jnp.minimum(j, HALF_STEPS - 1)))
    second = pl.BlockSpec((64, STEP), lambda j, place: (0, jnp.maximum(j - HALF_STEPS, 0)))
    outs = pl.pallas_call(
        near_kernel,
        out_shape=[jax.ShapeDtypeStruct((64, HALF), jnp.bfloat16)] * 8
        + [jax.ShapeDtypeStruct((1, WIDTH), jnp.float32)],
        grid_spec=pltpu.PrefetchScalarGridSpec(
            num_scalar_prefetch=1,
            grid=(STEPS,),
            in_specs=[
                pl.BlockSpec((NEAR, VOCAB_ROWS), lambda j, place: (place[0], 0)),
                pl.BlockSpec((VOCAB_ROWS, STEP), lambda j, place: (0, j)),
                pl.BlockSpec((NEAR, STEP), lambda j, place: (0, j)),
                pl.BlockSpec((NEAR, STEP), lambda j, place: (place[0], j)),
            ],
            out_specs=[first] * 4 + [second] * 4 + [pl.BlockSpec((1, STEP), lambda j, place: (0, j))],
            scratch_shapes=[pltpu.VMEM((16, PIECE, STEP), jnp.float32)],
        ),
        compiler_params=pltpu.CompilerParams(vmem_limit_bytes=VMEM_BYTES),
        cost_estimate=pl.CostEstimate(
            flops=2 * VOCAB_ROWS * NEAR * WIDTH, bytes_accessed=12 << 20, transcendentals=0
        ),
        name="near_gradient",
    )(place, turned, weight, arrived, rows)
    return outs[:4], outs[4:8], outs[8]


def weight_kernel(grad, rows, out):
    out[...] = jnp.dot(grad[...], rows[...], preferred_element_type=jnp.float32).astype(jnp.bfloat16)


def weight_gradient(grad, rows):
    return pl.pallas_call(
        weight_kernel,
        out_shape=jax.ShapeDtypeStruct((VOCAB_ROWS, WIDTH), jnp.bfloat16),
        grid=(STEPS,),
        in_specs=[
            pl.BlockSpec((VOCAB_ROWS, TOKENS), lambda j: (0, 0)),
            pl.BlockSpec((TOKENS, STEP), lambda j: (0, j)),
        ],
        out_specs=pl.BlockSpec((VOCAB_ROWS, STEP), lambda j: (0, j)),
        compiler_params=pltpu.CompilerParams(vmem_limit_bytes=VMEM_BYTES),
        cost_estimate=pl.CostEstimate(
            flops=2 * VOCAB_ROWS * TOKENS * WIDTH, bytes_accessed=10 << 20, transcendentals=0
        ),
        name="weight_gradient",
    )(grad, rows)


def on_device(hidden, norm_gain, weight, targets):
    core, y, z = lax.axis_index("core"), lax.axis_index("y"), lax.axis_index("z")
    x = lax.axis_index("x_hi") * 2 + lax.axis_index("x_lo")
    place = jnp.stack([core, y, x, lax.axis_index(AXES)]).astype(jnp.int32)
    ids = targets.reshape(2, 4, 2, 2, 16).transpose(2, 1, 3, 0, 4).reshape(1, TOKENS)

    values = hidden.astype(jnp.float32)
    inverse = lax.rsqrt(jnp.mean(values * values, axis=-1, keepdims=True) + epsilon)
    unit_rows = values * inverse
    normed = (unit_rows * norm_gain).astype(jnp.bfloat16)

    line = gather_over(normed, "z", 8).reshape(PIECE, WIDTH)
    first_row = jnp.concatenate(gather_ring(line[:, :HALF], shift_x), axis=0)
    second_row = jnp.concatenate(gather_ring(line[:, HALF:], shift_y), axis=0)
    near_blocks = gather_ring(first_row, shift_y) + gather_ring(second_row, shift_x)
    far_blocks = [swap_cores(block) for block in near_blocks]

    gathered, capped, stats = forward(place, ids, weight, near_blocks + far_blocks)
    stats = stats + swap_cores(stats)
    stats = sum_over(stats, PLANE, 16)
    stats = sum_over(stats, "z", 8)

    grad, turned, far_part = far_gradient(place, ids, capped, stats, weight)
    arrived = swap_cores(far_part)
    first_sends, second_sends, gain_part = near_gradient(place, turned, weight, arrived, gathered)
    first_half = scatter_ring(first_sends, shift_y).astype(jnp.bfloat16)
    second_half = scatter_ring(second_sends, shift_x).astype(jnp.bfloat16)
    grad_weight = weight_gradient(grad, gathered)
    gain_part = sum_over(gain_part, PLANE, 16)

    def pieces(block):
        return [block[k * PIECE : (k + 1) * PIECE] for k in range(4)]

    first_line = scatter_ring(pieces(first_half), shift_x)
    second_line = scatter_ring(pieces(second_half), shift_y)
    line_part = jnp.concatenate([first_line, second_line], axis=1).astype(jnp.bfloat16)
    line_parts = lax.all_to_all(line_part.reshape(8, 2, WIDTH), "z", 0, 0, tiled=True)
    grad_normed = jnp.sum(line_parts.astype(jnp.float32), axis=0)
    gain_part = sum_over(gain_part, "z", 8)
    grad_gain = (gain_part + swap_cores(gain_part)).reshape(WIDTH) / norm_gain

    total_exp, total_weighted, target_logit = stats
    log_total = cap_value + jnp.log(total_exp)
    mean_logit = total_weighted / total_exp
    every_loss = log_total - target_logit - entropy_weight * (log_total - mean_logit)
    row = (core * 16 + y * 4 + x) * PIECE + z * 2
    token_loss = lax.dynamic_slice_in_dim(every_loss, row, 2, 0)
    scaled = norm_gain * grad_normed
    grad_hidden = (
        scaled - unit_rows * jnp.mean(scaled * unit_rows, axis=-1, keepdims=True)
    ) * inverse
    return (token_loss, grad_hidden, grad_weight, grad_gain)


def solution(mesh):
    fine = Mesh(mesh.devices.reshape(2, 4, 2, 2, 8), AXES)
    rows = P(AXES, None)
    return jax.shard_map(
        on_device,
        mesh=fine,
        in_specs=(rows, P(), rows, P()),
        out_specs=(P(AXES), rows, rows, P()),
        check_vma=False,
    )
```

```python
import jax
import jax.numpy as jnp
from jax import lax
from jax.experimental import pallas as pl
from jax.experimental.pallas import tpu as pltpu
from jax.sharding import Mesh, PartitionSpec as P

epsilon = 1e-06
cap_value = 30.0
entropy_weight = 0.2

AXES = ("x_lo", "y", "core", "x_hi", "z")
PLANE = ("x_lo", "y", "x_hi")
WIDTH = 4608
HALF = WIDTH // 2
TOKENS = 512
NEAR = TOKENS // 2
VOCAB_ROWS = 512
PIECE = 16
STEP = 768
STEPS = WIDTH // STEP
HALF_STEPS = HALF // STEP

RING = (0, 2, 1, 3)


def shift_y(block, step):
    return lax.ppermute(block, "y", [(p, (p + step) % 4) for p in range(4)])


def shift_x(block, step):
    pairs = [(RING[p], RING[(p + step) % 4]) for p in range(4)]
    return lax.ppermute(block, ("x_lo", "x_hi"), pairs)


def swap_cores(block):
    return lax.ppermute(block, "core", [(0, 1), (1, 0)])


def gather_over(block, axes, size):
    copies = jnp.broadcast_to(block[None], (size,) + block.shape)
    return lax.all_to_all(copies, axes, 0, 0, tiled=True)


def sum_over(block, axes, size):
    return jnp.sum(gather_over(block, axes, size), axis=0)


def gather_ring(block, shift):
    across, up, down = shift(block, 2), shift(block, 3), shift(block, 1)
    return [block, up, across, down]


def send_ring(blocks, shift):
    across, up, down = shift(blocks[2], 2), shift(blocks[1], 1), shift(blocks[3], 3)
    return [blocks[0], up, across, down]


def total(blocks):
    return sum(block.astype(jnp.float32) for block in blocks)


def piece_row(core, y, x):
    return pl.multiple_of((core * 16 + y * 4 + x) * PIECE, PIECE)


def step_columns(step):
    return pl.ds(step * STEP, STEP)


def start(copies):
    for copy in copies:
        copy.start()
    return copies


def forward_kernel(place, targets, weight, *rest):
    blocks = rest[:16]
    gathered, capped_out, stats_out, weight_held, rows_held, weight_sems, row_sems, out_sem = rest[16:]
    core, y, x, position = place[0], place[1], place[2], place[3]

    def half_columns(half):
        return pl.ds(half * HALF, HALF)

    weight_copies = []
    row_copies = ([], [])
    for half in range(2):
        copy = pltpu.make_async_copy(
            weight.at[:, half_columns(half)],
            weight_held.at[:, half_columns(half)],
            weight_sems.at[half],
        )
        copy.start()
        weight_copies.append(copy)
        for far in range(2):
            owner = core if far == 0 else 1 - core
            for outer in range(4):
                block = blocks[far * 8 + half * 4 + outer]
                for inner in range(4):
                    up_y, up_x = (outer, inner) if half == 0 else (inner, outer)
                    row = piece_row(owner, lax.rem(y + up_y, 4), lax.rem(x + up_x, 4))
                    copy = pltpu.make_async_copy(
                        block.at[inner],
                        rows_held.at[pl.ds(row, PIECE), half_columns(half)],
                        row_sems.at[half * 32 + far * 16 + outer * 4 + inner],
                    )
                    copy.start()
                    row_copies[half].append(copy)

    logits = None
    for half in range(2):
        weight_copies[half].wait()
        for copy in row_copies[half]:
            copy.wait()
        columns = slice(half * HALF, (half + 1) * HALF)
        part = lax.dot_general(
            weight_held[:, columns],
            rows_held[:, columns],
            (((1,), (1,)), ((), ())),
            preferred_element_type=jnp.float32,
        )
        logits = part if logits is None else logits + part
    out_copy = pltpu.make_async_copy(rows_held, gathered, out_sem)
    out_copy.start()
    capped = cap_value * jnp.tanh(logits / cap_value)
    capped_out[...] = capped
    powers = jnp.exp(capped - cap_value)
    entry = position * VOCAB_ROWS + lax.broadcasted_iota(jnp.int32, capped.shape, 0)
    hit = targets[...] == entry
    stats_out[0:1, :] = jnp.sum(powers, axis=0, keepdims=True)
    stats_out[1:2, :] = jnp.sum(powers * capped, axis=0, keepdims=True)
    stats_out[2:3, :] = jnp.sum(jnp.where(hit, capped, 0.0), axis=0, keepdims=True)
    out_copy.wait()


SCALARS = pl.BlockSpec(memory_space=pltpu.SMEM)
IN_VMEM = pl.BlockSpec(memory_space=pltpu.VMEM)
IN_HBM = pl.BlockSpec(memory_space=pltpu.HBM)
ANYWHERE = pl.BlockSpec(memory_space=pl.ANY)


def forward(place, targets, weight, blocks):
    return pl.pallas_call(
        forward_kernel,
        out_shape=(
            jax.ShapeDtypeStruct((TOKENS, WIDTH), jnp.bfloat16),
            jax.ShapeDtypeStruct((VOCAB_ROWS, TOKENS), jnp.float32),
            jax.ShapeDtypeStruct((3, TOKENS), jnp.float32),
        ),
        in_specs=[SCALARS, IN_VMEM, IN_HBM] + [ANYWHERE] * 16,
        out_specs=(IN_HBM, IN_VMEM, IN_VMEM),
        scratch_shapes=[
            pltpu.VMEM((VOCAB_ROWS, WIDTH), jnp.bfloat16),
            pltpu.VMEM((TOKENS, WIDTH), jnp.bfloat16),
            pltpu.SemaphoreType.DMA((2,)),
            pltpu.SemaphoreType.DMA((64,)),
            pltpu.SemaphoreType.DMA,
        ],
        compiler_params=pltpu.CompilerParams(vmem_limit_bytes=22 << 20),
        cost_estimate=pl.CostEstimate(
            flops=2 * VOCAB_ROWS * TOKENS * WIDTH, bytes_accessed=16 << 20, transcendentals=1 << 19
        ),
        name="forward",
    )(place, targets, weight, *blocks)


def far_kernel(
    place, targets, capped, totals, weight, grad_out, turned_out, far_out,
    weight_held, far_held, weight_sems, out_sems,
):
    core, position = place[0], place[3]
    arrivals = start([
        pltpu.make_async_copy(
            weight.at[:, step_columns(j)], weight_held.at[:, step_columns(j)], weight_sems.at[j]
        )
        for j in range(STEPS)
    ])
    log_total = cap_value + jnp.log(totals[0:1, :])
    mean_logit = totals[1:2, :] / totals[0:1, :]
    values = capped[...]
    probs = jnp.exp(values - log_total)
    entry = position * VOCAB_ROWS + lax.broadcasted_iota(jnp.int32, values.shape, 0)
    hit = (targets[...] == entry).astype(jnp.float32)
    raw_grad = probs - hit + entropy_weight * probs * (values - mean_logit)
    ratio = values / cap_value
    grad = raw_grad * (1.0 - ratio * ratio)
    grad_out[...] = grad.astype(jnp.bfloat16)
    turned_out[...] = grad.T.astype(jnp.bfloat16)
    far = pl.multiple_of((1 - core) * NEAR, NEAR)
    rows = turned_out[pl.ds(far, NEAR), :]
    leaving = []
    for j in range(STEPS):
        arrivals[j].wait()
        columns = slice(j * STEP, (j + 1) * STEP)
        far_held[:, columns] = jnp.dot(
            rows, weight_held[:, columns], preferred_element_type=jnp.float32
        ).astype(jnp.bfloat16)
        copy = pltpu.make_async_copy(
            far_held.at[:, step_columns(j)], far_out.at[:, step_columns(j)], out_sems.at[j]
        )
        leaving += start([copy])
    for copy in leaving:
        copy.wait()


def far_gradient(place, targets, capped, totals, weight):
    return pl.pallas_call(
        far_kernel,
        out_shape=(
            jax.ShapeDtypeStruct((VOCAB_ROWS, TOKENS), jnp.bfloat16),
            jax.ShapeDtypeStruct((TOKENS, VOCAB_ROWS), jnp.bfloat16),
            jax.ShapeDtypeStruct((NEAR, WIDTH), jnp.bfloat16),
        ),
        in_specs=[SCALARS, IN_VMEM, IN_VMEM, IN_VMEM, IN_HBM],
        out_specs=(IN_VMEM, IN_VMEM, ANYWHERE),
        scratch_shapes=[
            pltpu.VMEM((VOCAB_ROWS, WIDTH), jnp.bfloat16),
            pltpu.VMEM((NEAR, WIDTH), jnp.bfloat16),
            pltpu.SemaphoreType.DMA((STEPS,)),
            pltpu.SemaphoreType.DMA((STEPS,)),
        ],
        compiler_params=pltpu.CompilerParams(vmem_limit_bytes=20 << 20),
        cost_estimate=pl.CostEstimate(
            flops=2 * VOCAB_ROWS * NEAR * WIDTH, bytes_accessed=9 << 20, transcendentals=1 << 18
        ),
        name="far_gradient",
    )(place, targets, capped, totals, weight)


def near_kernel(place, turned, weight, arrived, gathered, *rest):
    sends, gain_out = rest[:8], rest[8]
    weight_held, arrived_held, rows_held, first_held, second_held, in_sems, out_sems = rest[9:]
    core, y, x = place[0], place[1], place[2]
    near = pl.multiple_of(core * NEAR, NEAR)
    arrivals = []
    for j in range(STEPS):
        columns = step_columns(j)
        arrivals.append(start([
            pltpu.make_async_copy(weight.at[:, columns], weight_held.at[:, columns], in_sems.at[0, j]),
            pltpu.make_async_copy(arrived.at[:, columns], arrived_held.at[:, columns], in_sems.at[1, j]),
            pltpu.make_async_copy(
                gathered.at[pl.ds(near, NEAR), columns], rows_held.at[:, columns], in_sems.at[2, j]
            ),
        ]))
    rows = turned[pl.ds(near, NEAR), :]
    leaving = []
    for j in range(STEPS):
        for copy in arrivals[j]:
            copy.wait()
        columns = slice(j * STEP, (j + 1) * STEP)
        part = jnp.dot(rows, weight_held[:, columns], preferred_element_type=jnp.float32)
        part = part + arrived_held[:, columns].astype(jnp.float32)
        gain_out[:, columns] = jnp.sum(
            part * rows_held[:, columns].astype(jnp.float32), axis=0, keepdims=True
        )
        rounded = part.astype(jnp.bfloat16)
        half = j // HALF_STEPS
        held = (first_held, second_held)[half]
        own = slice((j - half * HALF_STEPS) * STEP, (j - half * HALF_STEPS + 1) * STEP)
        for to_y in range(4):
            for to_x in range(4):
                up_y, up_x = lax.rem(to_y + 4 - y, 4), lax.rem(to_x + 4 - x, 4)
                outer, inner = (up_y, up_x) if half == 0 else (up_x, up_y)
                row = (to_y * 4 + to_x) * PIECE
                held[outer, inner, :, own] = rounded[row : row + PIECE]
        if j % HALF_STEPS == HALF_STEPS - 1:
            leaving += start([
                pltpu.make_async_copy(held.at[k], sends[half * 4 + k], out_sems.at[half * 4 + k])
                for k in range(4)
            ])
    for copy in leaving:
        copy.wait()


def near_gradient(place, turned, weight, arrived, gathered):
    outs = pl.pallas_call(
        near_kernel,
        out_shape=[jax.ShapeDtypeStruct((4, PIECE, HALF), jnp.bfloat16)] * 8
        + [jax.ShapeDtypeStruct((1, WIDTH), jnp.float32)],
        in_specs=[SCALARS, IN_VMEM, IN_HBM, ANYWHERE, IN_HBM],
        out_specs=[ANYWHERE] * 8 + [IN_VMEM],
        scratch_shapes=[
            pltpu.VMEM((VOCAB_ROWS, WIDTH), jnp.bfloat16),
            pltpu.VMEM((NEAR, WIDTH), jnp.bfloat16),
            pltpu.VMEM((NEAR, WIDTH), jnp.bfloat16),
            pltpu.VMEM((4, 4, PIECE, HALF), jnp.bfloat16),
            pltpu.VMEM((4, 4, PIECE, HALF), jnp.bfloat16),
            pltpu.SemaphoreType.DMA((3, STEPS)),
            pltpu.SemaphoreType.DMA((8,)),
        ],
        compiler_params=pltpu.CompilerParams(vmem_limit_bytes=22 << 20),
        cost_estimate=pl.CostEstimate(
            flops=2 * VOCAB_ROWS * NEAR * WIDTH, bytes_accessed=12 << 20, transcendentals=0
        ),
        name="near_gradient",
    )(place, turned, weight, arrived, gathered)
    return outs[:4], outs[4:8], outs[8]


def weight_kernel(grad, gathered, out, rows_held, out_held, in_sems, out_sems):
    arrivals = start([
        pltpu.make_async_copy(
            gathered.at[:, step_columns(j)], rows_held.at[:, step_columns(j)], in_sems.at[j]
        )
        for j in range(STEPS)
    ])
    leaving = []
    for j in range(STEPS):
        arrivals[j].wait()
        columns = slice(j * STEP, (j + 1) * STEP)
        out_held[:, columns] = jnp.dot(
            grad[...], rows_held[:, columns], preferred_element_type=jnp.float32
        ).astype(jnp.bfloat16)
        copy = pltpu.make_async_copy(
            out_held.at[:, step_columns(j)], out.at[:, step_columns(j)], out_sems.at[j]
        )
        leaving += start([copy])
    for copy in leaving:
        copy.wait()


def weight_gradient(grad, gathered):
    return pl.pallas_call(
        weight_kernel,
        out_shape=jax.ShapeDtypeStruct((VOCAB_ROWS, WIDTH), jnp.bfloat16),
        in_specs=[IN_VMEM, IN_HBM],
        out_specs=IN_HBM,
        scratch_shapes=[
            pltpu.VMEM((TOKENS, WIDTH), jnp.bfloat16),
            pltpu.VMEM((VOCAB_ROWS, WIDTH), jnp.bfloat16),
            pltpu.SemaphoreType.DMA((STEPS,)),
            pltpu.SemaphoreType.DMA((STEPS,)),
        ],
        compiler_params=pltpu.CompilerParams(vmem_limit_bytes=16 << 20),
        cost_estimate=pl.CostEstimate(
            flops=2 * VOCAB_ROWS * TOKENS * WIDTH, bytes_accessed=10 << 20, transcendentals=0
        ),
        name="weight_gradient",
    )(grad, gathered)


def on_device(hidden, norm_gain, weight, targets):
    core, y, z = lax.axis_index("core"), lax.axis_index("y"), lax.axis_index("z")
    x = lax.axis_index("x_hi") * 2 + lax.axis_index("x_lo")
    place = jnp.stack([core, y, x, lax.axis_index(AXES)]).astype(jnp.int32)
    ids = targets.reshape(2, 4, 2, 2, 16).transpose(2, 1, 3, 0, 4).reshape(1, TOKENS)

    values = hidden.astype(jnp.float32)
    inverse = lax.rsqrt(jnp.mean(values * values, axis=-1, keepdims=True) + epsilon)
    unit_rows = values * inverse
    normed = (unit_rows * norm_gain).astype(jnp.bfloat16)

    line = gather_over(normed, "z", 8).reshape(PIECE, WIDTH)
    first_row = jnp.stack(gather_ring(line[:, :HALF], shift_x))
    second_row = jnp.stack(gather_ring(line[:, HALF:], shift_y))
    near_blocks = gather_ring(first_row, shift_y) + gather_ring(second_row, shift_x)
    far_blocks = [swap_cores(block) for block in near_blocks]

    gathered, capped, stats = forward(place, ids, weight, near_blocks + far_blocks)
    stats = stats + swap_cores(stats)
    stats = sum_over(stats, PLANE, 16)
    stats = sum_over(stats, "z", 8)

    grad, turned, far_part = far_gradient(place, ids, capped, stats, weight)
    arrived = swap_cores(far_part)
    first_sends, second_sends, gain_part = near_gradient(place, turned, weight, arrived, gathered)
    first_parts = send_ring(first_sends, shift_y)
    second_parts = send_ring(second_sends, shift_x)
    gain_part, first_parts[2] = lax.optimization_barrier((gain_part, first_parts[2]))
    gain_part = sum_over(gain_part, PLANE, 16)
    first_half = total(first_parts).astype(jnp.bfloat16)
    second_half = total(second_parts).astype(jnp.bfloat16)
    first_line = total(send_ring([first_half[k] for k in range(4)], shift_x))
    second_line = total(send_ring([second_half[k] for k in range(4)], shift_y))
    line_part = jnp.concatenate([first_line, second_line], axis=1).astype(jnp.bfloat16)
    gain_high = lax.reduce_precision(gain_part, 8, 7)
    gain_rows = jnp.concatenate([gain_high, gain_part - gain_high], axis=0).astype(jnp.bfloat16)
    message = jnp.concatenate(
        [line_part.reshape(8, 2, WIDTH), jnp.broadcast_to(gain_rows[None], (8, 2, WIDTH))], axis=1
    )
    message, grad = lax.optimization_barrier((message, grad))
    line_parts = lax.all_to_all(message, "z", 0, 0, tiled=True)
    grad_weight = weight_gradient(grad, gathered)
    line_sum = jnp.sum(line_parts.astype(jnp.float32), axis=0)
    grad_normed = line_sum[:2]
    gain_part = line_sum[2] + line_sum[3]
    grad_gain = (gain_part + swap_cores(gain_part)) / norm_gain

    total_exp, total_weighted, target_logit = stats
    log_total = cap_value + jnp.log(total_exp)
    mean_logit = total_weighted / total_exp
    every_loss = log_total - target_logit - entropy_weight * (log_total - mean_logit)
    row = (core * 16 + y * 4 + x) * PIECE + z * 2
    token_loss = lax.dynamic_slice_in_dim(every_loss, row, 2, 0)
    scaled = norm_gain * grad_normed
    grad_hidden = (
        scaled - unit_rows * jnp.mean(scaled * unit_rows, axis=-1, keepdims=True)
    ) * inverse
    return (token_loss, grad_hidden, grad_weight, grad_gain)


def solution(mesh):
    fine = Mesh(mesh.devices.reshape(2, 4, 2, 2, 8), AXES)
    rows = P(AXES, None)
    return jax.shard_map(
        on_device,
        mesh=fine,
        in_specs=(rows, P(), rows, P()),
        out_specs=(P(AXES), rows, rows, P()),
        check_vma=False,
    )
```

```python
import jax
import jax.numpy as jnp
from jax import lax
from jax.experimental import pallas as pl
from jax.experimental.pallas import tpu as pltpu
from jax.sharding import Mesh, PartitionSpec as P

epsilon = 1e-06
cap_value = 30.0
entropy_weight = 0.2

AXES = ("x_lo", "y", "core", "x_hi", "z")
PLANE = ("x_lo", "y", "x_hi")
WIDTH = 4608
HALF = WIDTH // 2
TOKENS = 512
NEAR = TOKENS // 2
VOCAB_ROWS = 512
PIECE = 16
STEP = 768
STEPS = WIDTH // STEP
HALF_STEPS = HALF // STEP

RING = (0, 2, 1, 3)


def shift_y(block, step):
    return lax.ppermute(block, "y", [(p, (p + step) % 4) for p in range(4)])


def shift_x(block, step):
    pairs = [(RING[p], RING[(p + step) % 4]) for p in range(4)]
    return lax.ppermute(block, ("x_lo", "x_hi"), pairs)


def swap_cores(block):
    return lax.ppermute(block, "core", [(0, 1), (1, 0)])


def gather_over(block, axes, size):
    copies = jnp.broadcast_to(block[None], (size,) + block.shape)
    return lax.all_to_all(copies, axes, 0, 0, tiled=True)


def sum_over(block, axes, size):
    return jnp.sum(gather_over(block, axes, size), axis=0)


def gather_ring(block, shift):
    across, up, down = shift(block, 2), shift(block, 3), shift(block, 1)
    return [block, up, across, down]


def send_ring(blocks, shift):
    across, up, down = shift(blocks[2], 2), shift(blocks[1], 1), shift(blocks[3], 3)
    return [blocks[0], up, across, down]


def total(blocks):
    return sum(block.astype(jnp.float32) for block in blocks)


def piece_row(core, y, x):
    piece = ((lax.rem(x, 2) * 4 + y) * 2 + core) * 2 + lax.div(x, 2)
    return pl.multiple_of(piece * PIECE, PIECE)


def step_columns(step):
    return pl.ds(step * STEP, STEP)


def start(copies):
    for copy in copies:
        copy.start()
    return copies


def forward_kernel(place, targets, weight, *rest):
    blocks = rest[:16]
    gathered, capped_out, stats_out, weight_held, rows_held, weight_sems, row_sems, out_sem = rest[16:]
    core, y, x, position = place[0], place[1], place[2], place[3]

    def half_columns(half):
        return pl.ds(half * HALF, HALF)

    weight_copies = []
    row_copies = ([], [])
    for half in range(2):
        copy = pltpu.make_async_copy(
            weight.at[:, half_columns(half)],
            weight_held.at[:, half_columns(half)],
            weight_sems.at[half],
        )
        copy.start()
        weight_copies.append(copy)
        for far in range(2):
            owner = core if far == 0 else 1 - core
            for outer in range(4):
                block = blocks[far * 8 + half * 4 + outer]
                for inner in range(4):
                    up_y, up_x = (outer, inner) if half == 0 else (inner, outer)
                    row = piece_row(owner, lax.rem(y + up_y, 4), lax.rem(x + up_x, 4))
                    copy = pltpu.make_async_copy(
                        block.at[inner],
                        rows_held.at[pl.ds(row, PIECE), half_columns(half)],
                        row_sems.at[half * 32 + far * 16 + outer * 4 + inner],
                    )
                    copy.start()
                    row_copies[half].append(copy)

    logits = None
    for half in range(2):
        weight_copies[half].wait()
        for copy in row_copies[half]:
            copy.wait()
        columns = slice(half * HALF, (half + 1) * HALF)
        part = lax.dot_general(
            weight_held[:, columns],
            rows_held[:, columns],
            (((1,), (1,)), ((), ())),
            preferred_element_type=jnp.float32,
        )
        logits = part if logits is None else logits + part
    out_copy = pltpu.make_async_copy(rows_held, gathered, out_sem)
    out_copy.start()
    capped = cap_value * jnp.tanh(logits / cap_value)
    capped_out[...] = capped
    powers = jnp.exp(capped - cap_value)
    entry = position * VOCAB_ROWS + lax.broadcasted_iota(jnp.int32, capped.shape, 0)
    hit = targets[...] == entry
    stats_out[0:1, :] = jnp.sum(powers, axis=0, keepdims=True)
    stats_out[1:2, :] = jnp.sum(powers * capped, axis=0, keepdims=True)
    stats_out[2:3, :] = jnp.sum(jnp.where(hit, capped, 0.0), axis=0, keepdims=True)
    out_copy.wait()


SCALARS = pl.BlockSpec(memory_space=pltpu.SMEM)
IN_VMEM = pl.BlockSpec(memory_space=pltpu.VMEM)
IN_HBM = pl.BlockSpec(memory_space=pltpu.HBM)
ANYWHERE = pl.BlockSpec(memory_space=pl.ANY)


def forward(place, targets, weight, blocks):
    return pl.pallas_call(
        forward_kernel,
        out_shape=(
            jax.ShapeDtypeStruct((TOKENS, WIDTH), jnp.bfloat16),
            jax.ShapeDtypeStruct((VOCAB_ROWS, TOKENS), jnp.float32),
            jax.ShapeDtypeStruct((3, TOKENS), jnp.float32),
        ),
        in_specs=[SCALARS, IN_VMEM, IN_HBM] + [ANYWHERE] * 16,
        out_specs=(IN_HBM, IN_VMEM, IN_VMEM),
        scratch_shapes=[
            pltpu.VMEM((VOCAB_ROWS, WIDTH), jnp.bfloat16),
            pltpu.VMEM((TOKENS, WIDTH), jnp.bfloat16),
            pltpu.SemaphoreType.DMA((2,)),
            pltpu.SemaphoreType.DMA((64,)),
            pltpu.SemaphoreType.DMA,
        ],
        compiler_params=pltpu.CompilerParams(vmem_limit_bytes=50 << 20),
        cost_estimate=pl.CostEstimate(
            flops=2 * VOCAB_ROWS * TOKENS * WIDTH, bytes_accessed=16 << 20, transcendentals=1 << 19
        ),
        name="forward",
    )(place, targets, weight, *blocks)


def far_kernel(
    place, targets, capped, totals, weight, grad_out, turned_out, far_out,
    weight_held, far_held, weight_sems, out_sems,
):
    core, position = place[0], place[3]
    arrivals = start([
        pltpu.make_async_copy(
            weight.at[:, step_columns(j)], weight_held.at[:, step_columns(j)], weight_sems.at[j]
        )
        for j in range(STEPS)
    ])
    log_total = cap_value + jnp.log(totals[0:1, :])
    mean_logit = totals[1:2, :] / totals[0:1, :]
    values = capped[...]
    probs = jnp.exp(values - log_total)
    entry = position * VOCAB_ROWS + lax.broadcasted_iota(jnp.int32, values.shape, 0)
    hit = (targets[...] == entry).astype(jnp.float32)
    raw_grad = probs - hit + entropy_weight * probs * (values - mean_logit)
    ratio = values / cap_value
    grad = raw_grad * (1.0 - ratio * ratio)
    grad_out[...] = grad.astype(jnp.bfloat16)
    turned_out[...] = grad.T.astype(jnp.bfloat16).reshape(8, 2, 32, VOCAB_ROWS)
    rows = turned_out[:, 1 - core].reshape(NEAR, VOCAB_ROWS)
    leaving = []
    for j in range(STEPS):
        arrivals[j].wait()
        columns = slice(j * STEP, (j + 1) * STEP)
        far_held[:, columns] = jnp.dot(
            rows, weight_held[:, columns], preferred_element_type=jnp.float32
        ).astype(jnp.bfloat16)
        copy = pltpu.make_async_copy(
            far_held.at[:, step_columns(j)], far_out.at[:, step_columns(j)], out_sems.at[j]
        )
        leaving += start([copy])
    for copy in leaving:
        copy.wait()


def far_gradient(place, targets, capped, totals, weight):
    return pl.pallas_call(
        far_kernel,
        out_shape=(
            jax.ShapeDtypeStruct((VOCAB_ROWS, TOKENS), jnp.bfloat16),
            jax.ShapeDtypeStruct((8, 2, 32, VOCAB_ROWS), jnp.bfloat16),
            jax.ShapeDtypeStruct((NEAR, WIDTH), jnp.bfloat16),
        ),
        in_specs=[SCALARS, IN_VMEM, IN_VMEM, IN_VMEM, IN_HBM],
        out_specs=(IN_VMEM, IN_VMEM, ANYWHERE),
        scratch_shapes=[
            pltpu.VMEM((VOCAB_ROWS, WIDTH), jnp.bfloat16),
            pltpu.VMEM((NEAR, WIDTH), jnp.bfloat16),
            pltpu.SemaphoreType.DMA((STEPS,)),
            pltpu.SemaphoreType.DMA((STEPS,)),
        ],
        compiler_params=pltpu.CompilerParams(vmem_limit_bytes=52 << 20),
        cost_estimate=pl.CostEstimate(
            flops=2 * VOCAB_ROWS * NEAR * WIDTH, bytes_accessed=9 << 20, transcendentals=1 << 18
        ),
        name="far_gradient",
    )(place, targets, capped, totals, weight)


def near_kernel(place, turned, weight, arrived, gathered, *rest):
    sends, gain_out = rest[:8], rest[8]
    weight_held, arrived_held, rows_held, first_held, second_held, in_sems, out_sems = rest[9:]
    core, y, x = place[0], place[1], place[2]
    arrivals = []
    for j in range(STEPS):
        columns = step_columns(j)
        arrivals.append(start([
            pltpu.make_async_copy(weight.at[:, columns], weight_held.at[:, columns], in_sems.at[0, j]),
            pltpu.make_async_copy(arrived.at[:, columns], arrived_held.at[:, columns], in_sems.at[1, j]),
            pltpu.make_async_copy(
                gathered.at[:, core, :, columns], rows_held.at[:, :, columns], in_sems.at[2, j]
            ),
        ]))
    rows = turned[:, core].reshape(NEAR, VOCAB_ROWS)
    leaving = []
    for j in range(STEPS):
        for copy in arrivals[j]:
            copy.wait()
        columns = slice(j * STEP, (j + 1) * STEP)
        part = jnp.dot(rows, weight_held[:, columns], preferred_element_type=jnp.float32)
        part = part + arrived_held[:, columns].astype(jnp.float32)
        gain_out[:, columns] = jnp.sum(
            part * rows_held[:, :, columns].reshape(NEAR, STEP).astype(jnp.float32), axis=0, keepdims=True
        )
        rounded = part.astype(jnp.bfloat16)
        half = j // HALF_STEPS
        held = (first_held, second_held)[half]
        own = slice((j - half * HALF_STEPS) * STEP, (j - half * HALF_STEPS + 1) * STEP)
        for to_y in range(4):
            for to_x in range(4):
                up_y, up_x = lax.rem(to_y + 4 - y, 4), lax.rem(to_x + 4 - x, 4)
                outer, inner = (up_y, up_x) if half == 0 else (up_x, up_y)
                row = ((to_x % 2 * 4 + to_y) * 2 + to_x // 2) * PIECE
                held[outer, inner, :, own] = rounded[row : row + PIECE]
        if j % HALF_STEPS == HALF_STEPS - 1:
            leaving += start([
                pltpu.make_async_copy(held.at[k], sends[half * 4 + k], out_sems.at[half * 4 + k])
                for k in range(4)
            ])
    for copy in leaving:
        copy.wait()


def near_gradient(place, turned, weight, arrived, gathered):
    outs = pl.pallas_call(
        near_kernel,
        out_shape=[jax.ShapeDtypeStruct((4, PIECE, HALF), jnp.bfloat16)] * 8
        + [jax.ShapeDtypeStruct((1, WIDTH), jnp.float32)],
        in_specs=[SCALARS, IN_VMEM, IN_HBM, ANYWHERE, IN_HBM],
        out_specs=[ANYWHERE] * 8 + [IN_VMEM],
        scratch_shapes=[
            pltpu.VMEM((VOCAB_ROWS, WIDTH), jnp.bfloat16),
            pltpu.VMEM((NEAR, WIDTH), jnp.bfloat16),
            pltpu.VMEM((8, 32, WIDTH), jnp.bfloat16),
            pltpu.VMEM((4, 4, PIECE, HALF), jnp.bfloat16),
            pltpu.VMEM((4, 4, PIECE, HALF), jnp.bfloat16),
            pltpu.SemaphoreType.DMA((3, STEPS)),
            pltpu.SemaphoreType.DMA((8,)),
        ],
        compiler_params=pltpu.CompilerParams(vmem_limit_bytes=45 << 20),
        cost_estimate=pl.CostEstimate(
            flops=2 * VOCAB_ROWS * NEAR * WIDTH, bytes_accessed=12 << 20, transcendentals=0
        ),
        name="near_gradient",
    )(place, turned, weight, arrived, gathered)
    return outs[:4], outs[4:8], outs[8]


def weight_kernel(grad, gathered, out, rows_held, out_held, in_sems, out_sems):
    arrivals = start([
        pltpu.make_async_copy(
            gathered.at[:, step_columns(j)], rows_held.at[:, step_columns(j)], in_sems.at[j]
        )
        for j in range(STEPS)
    ])
    leaving = []
    for j in range(STEPS):
        arrivals[j].wait()
        columns = slice(j * STEP, (j + 1) * STEP)
        out_held[:, columns] = jnp.dot(
            grad[...], rows_held[:, columns], preferred_element_type=jnp.float32
        ).astype(jnp.bfloat16)
        copy = pltpu.make_async_copy(
            out_held.at[:, step_columns(j)], out.at[:, step_columns(j)], out_sems.at[j]
        )
        leaving += start([copy])
    for copy in leaving:
        copy.wait()


def weight_gradient(grad, gathered):
    return pl.pallas_call(
        weight_kernel,
        out_shape=jax.ShapeDtypeStruct((VOCAB_ROWS, WIDTH), jnp.bfloat16),
        in_specs=[IN_VMEM, IN_HBM],
        out_specs=IN_HBM,
        scratch_shapes=[
            pltpu.VMEM((TOKENS, WIDTH), jnp.bfloat16),
            pltpu.VMEM((VOCAB_ROWS, WIDTH), jnp.bfloat16),
            pltpu.SemaphoreType.DMA((STEPS,)),
            pltpu.SemaphoreType.DMA((STEPS,)),
        ],
        compiler_params=pltpu.CompilerParams(vmem_limit_bytes=58 << 20),
        cost_estimate=pl.CostEstimate(
            flops=2 * VOCAB_ROWS * TOKENS * WIDTH, bytes_accessed=10 << 20, transcendentals=0
        ),
        name="weight_gradient",
    )(grad, gathered)


def on_device(hidden, norm_gain, weight, targets):
    core, y, position = lax.axis_index("core"), lax.axis_index("y"), lax.axis_index(AXES)
    x = lax.axis_index("x_hi") * 2 + lax.axis_index("x_lo")
    place = jnp.stack([core, y, x, position]).astype(jnp.int32)
    ids = targets.reshape(1, TOKENS)

    values = hidden.astype(jnp.float32)
    inverse = lax.rsqrt(jnp.mean(values * values, axis=-1, keepdims=True) + epsilon)
    unit_rows = values * inverse
    normed = (unit_rows * norm_gain).astype(jnp.bfloat16)

    line = gather_over(normed, "z", 8).reshape(PIECE, WIDTH)
    first_row = jnp.stack(gather_ring(line[:, :HALF], shift_x))
    second_row = jnp.stack(gather_ring(line[:, HALF:], shift_y))
    near_blocks = gather_ring(first_row, shift_y) + gather_ring(second_row, shift_x)
    far_blocks = [swap_cores(block) for block in near_blocks]

    gathered, capped, stats = forward(place, ids, weight, near_blocks + far_blocks)
    stats = stats + swap_cores(stats)
    stats = sum_over(stats, PLANE, 16)
    stats = sum_over(stats, "z", 8)

    grad, turned, far_part = far_gradient(place, ids, capped, stats, weight)
    arrived = swap_cores(far_part)
    first_sends, second_sends, gain_part = near_gradient(
        place, turned, weight, arrived, gathered.reshape(8, 2, 32, WIDTH)
    )
    first_parts = send_ring(first_sends, shift_y)
    second_parts = send_ring(second_sends, shift_x)
    gain_part, first_parts[2] = lax.optimization_barrier((gain_part, first_parts[2]))
    gain_part = sum_over(gain_part, PLANE, 16)
    first_half = total(first_parts).astype(jnp.bfloat16)
    second_half = total(second_parts).astype(jnp.bfloat16)
    first_line = total(send_ring([first_half[k] for k in range(4)], shift_x))
    second_line = total(send_ring([second_half[k] for k in range(4)], shift_y))
    line_part = jnp.concatenate([first_line, second_line], axis=1).astype(jnp.bfloat16)
    gain_high = lax.reduce_precision(gain_part, 8, 7)
    gain_rows = jnp.concatenate([gain_high, gain_part - gain_high], axis=0).astype(jnp.bfloat16)
    message = jnp.concatenate(
        [line_part.reshape(8, 2, WIDTH), jnp.broadcast_to(gain_rows[None], (8, 2, WIDTH))], axis=1
    )
    message, grad = lax.optimization_barrier((message, grad))
    line_parts = lax.all_to_all(message, "z", 0, 0, tiled=True)
    grad_weight = weight_gradient(grad, gathered)
    line_sum = jnp.sum(line_parts.astype(jnp.float32), axis=0)
    grad_normed = line_sum[:2]
    gain_part = line_sum[2] + line_sum[3]
    grad_gain = (gain_part + swap_cores(gain_part)) / norm_gain

    total_exp, total_weighted, target_logit = stats
    log_total = cap_value + jnp.log(total_exp)
    mean_logit = total_weighted / total_exp
    every_loss = log_total - target_logit - entropy_weight * (log_total - mean_logit)
    token_loss = lax.dynamic_slice_in_dim(every_loss, position * 2, 2, 0)
    scaled = norm_gain * grad_normed
    grad_hidden = (
        scaled - unit_rows * jnp.mean(scaled * unit_rows, axis=-1, keepdims=True)
    ) * inverse
    return (token_loss, grad_hidden, grad_weight, grad_gain)


def solution(mesh):
    fine = Mesh(mesh.devices.reshape(2, 4, 2, 2, 8), AXES)
    rows = P(AXES, None)
    return jax.shard_map(
        on_device,
        mesh=fine,
        in_specs=(rows, P(), rows, P()),
        out_specs=(P(AXES), rows, rows, P()),
        check_vma=False,
    )
```

```python
import jax
import jax.numpy as jnp
from jax import lax
from jax.experimental import pallas as pl
from jax.experimental.pallas import tpu as pltpu
from jax.sharding import Mesh, PartitionSpec as P

epsilon = 1e-06
cap_value = 30.0
entropy_weight = 0.2

AXES = ("x_lo", "y", "core", "x_hi", "z")
PLANE = ("x_lo", "y", "x_hi")
WIDTH = 4608
HALF = WIDTH // 2
TOKENS = 512
NEAR = TOKENS // 2
VOCAB_ROWS = 512
PIECE = 16
STEP = 768
STEPS = WIDTH // STEP
HALF_STEPS = HALF // STEP

RING = (0, 2, 1, 3)


def shift_y(block, step):
    return lax.ppermute(block, "y", [(p, (p + step) % 4) for p in range(4)])


def shift_x(block, step):
    pairs = [(RING[p], RING[(p + step) % 4]) for p in range(4)]
    return lax.ppermute(block, ("x_lo", "x_hi"), pairs)


def swap_cores(block):
    return lax.ppermute(block, "core", [(0, 1), (1, 0)])


def gather_over(block, axes, size):
    copies = jnp.broadcast_to(block[None], (size,) + block.shape)
    return lax.all_to_all(copies, axes, 0, 0, tiled=True)


def sum_over(block, axes, size):
    return jnp.sum(gather_over(block, axes, size), axis=0)


def gather_ring(block, shift):
    across, up, down = shift(block, 2), shift(block, 3), shift(block, 1)
    return [block, up, across, down]


def send_ring(blocks, shift):
    across, up, down = shift(blocks[2], 2), shift(blocks[1], 1), shift(blocks[3], 3)
    return [blocks[0], up, across, down]


def total(blocks):
    return sum(block.astype(jnp.float32) for block in blocks)


def piece_row(core, y, x):
    piece = ((lax.rem(x, 2) * 4 + y) * 2 + core) * 2 + lax.div(x, 2)
    return pl.multiple_of(piece * PIECE, PIECE)


def step_columns(step):
    return pl.ds(pl.multiple_of(step * STEP, STEP), STEP)


def steps(body, first=0, last=STEPS):
    lax.fori_loop(first, last, lambda j, carry: (body(j), carry)[1], 0)


def forward_kernel(place, targets, weight, *rest):
    blocks = rest[:16]
    gathered, capped_out, stats_out, weight_held, rows_held, logits, weight_sems, row_sems, out_sem = rest[16:]
    core, y, x, position = place[0], place[1], place[2], place[3]

    def half_rows(half):
        return rows_held.at[:, half * HALF : (half + 1) * HALF]

    def weight_copy(j):
        columns = step_columns(j)
        return pltpu.make_async_copy(weight.at[:, columns], weight_held.at[:, columns], weight_sems.at[j])

    def place_blocks(half):
        def pieces(inner, carry):
            for far in range(2):
                owner = core if far == 0 else 1 - core
                for outer in range(4):
                    up_y, up_x = (outer, inner) if half == 0 else (inner, outer)
                    row = piece_row(owner, lax.rem(y + up_y, 4), lax.rem(x + up_x, 4))
                    pltpu.make_async_copy(
                        blocks[far * 8 + half * 4 + outer].at[inner],
                        half_rows(half).at[pl.ds(row, PIECE), :],
                        row_sems.at[half],
                    ).start()
            return carry

        lax.fori_loop(0, 4, pieces, 0)

    def multiply(j):
        weight_copy(j).wait()
        columns = step_columns(j)
        logits[...] += lax.dot_general(
            weight_held[:, columns],
            rows_held[:, columns],
            (((1,), (1,)), ((), ())),
            preferred_element_type=jnp.float32,
        )

    steps(lambda j: weight_copy(j).start(), 0, HALF_STEPS)
    place_blocks(0)
    steps(lambda j: weight_copy(j).start(), HALF_STEPS, STEPS)
    place_blocks(1)
    logits[...] = jnp.zeros_like(logits)
    pltpu.make_async_copy(half_rows(0), half_rows(0), row_sems.at[0]).wait()
    steps(multiply, 0, HALF_STEPS)
    pltpu.make_async_copy(half_rows(1), half_rows(1), row_sems.at[1]).wait()
    out_copy = pltpu.make_async_copy(rows_held, gathered, out_sem)
    out_copy.start()
    steps(multiply, HALF_STEPS, STEPS)

    def finish(k, carry):
        rows = pl.ds(pl.multiple_of(k * 64, 64), 64)
        capped = cap_value * jnp.tanh(logits[rows, :] / cap_value)
        capped_out[rows, :] = capped
        powers = jnp.exp(capped - cap_value)
        entry = position * VOCAB_ROWS + k * 64 + lax.broadcasted_iota(jnp.int32, capped.shape, 0)
        hit = targets[...] == entry
        return (
            carry[0] + jnp.sum(powers, axis=0, keepdims=True),
            carry[1] + jnp.sum(powers * capped, axis=0, keepdims=True),
            carry[2] + jnp.sum(jnp.where(hit, capped, 0.0), axis=0, keepdims=True),
        )

    sums = lax.fori_loop(0, VOCAB_ROWS // 64, finish, (jnp.zeros((1, TOKENS), jnp.float32),) * 3)
    for k in range(3):
        stats_out[k : k + 1, :] = sums[k]
    out_copy.wait()


SCALARS = pl.BlockSpec(memory_space=pltpu.SMEM)
IN_VMEM = pl.BlockSpec(memory_space=pltpu.VMEM)
IN_HBM = pl.BlockSpec(memory_space=pltpu.HBM)
ANYWHERE = pl.BlockSpec(memory_space=pl.ANY)


def forward(place, targets, weight, blocks):
    return pl.pallas_call(
        forward_kernel,
        out_shape=(
            jax.ShapeDtypeStruct((TOKENS, WIDTH), jnp.bfloat16),
            jax.ShapeDtypeStruct((VOCAB_ROWS, TOKENS), jnp.float32),
            jax.ShapeDtypeStruct((3, TOKENS), jnp.float32),
        ),
        in_specs=[SCALARS, IN_VMEM, IN_HBM] + [ANYWHERE] * 16,
        out_specs=(IN_HBM, IN_VMEM, IN_VMEM),
        scratch_shapes=[
            pltpu.VMEM((VOCAB_ROWS, WIDTH), jnp.bfloat16),
            pltpu.VMEM((TOKENS, WIDTH), jnp.bfloat16),
            pltpu.VMEM((VOCAB_ROWS, TOKENS), jnp.float32),
            pltpu.SemaphoreType.DMA((STEPS,)),
            pltpu.SemaphoreType.DMA((2,)),
            pltpu.SemaphoreType.DMA,
        ],
        compiler_params=pltpu.CompilerParams(vmem_limit_bytes=50 << 20),
        cost_estimate=pl.CostEstimate(
            flops=2 * VOCAB_ROWS * TOKENS * WIDTH, bytes_accessed=16 << 20, transcendentals=1 << 19
        ),
        name="forward",
    )(place, targets, weight, *blocks)


def far_kernel(
    place, targets, capped, totals, weight, grad_out, turned_out, far_out,
    weight_held, far_held, weight_sems, out_sems,
):
    core, position = place[0], place[3]

    def arrival(j):
        columns = step_columns(j)
        return pltpu.make_async_copy(weight.at[:, columns], weight_held.at[:, columns], weight_sems.at[j])

    def leaving(j):
        columns = step_columns(j)
        return pltpu.make_async_copy(far_held.at[:, columns], far_out.at[:, columns], out_sems.at[j])

    steps(lambda j: arrival(j).start())
    log_total = cap_value + jnp.log(totals[0:1, :])
    mean_logit = totals[1:2, :] / totals[0:1, :]

    def gradient(k):
        rows = pl.ds(pl.multiple_of(k * 128, 128), 128)
        values = capped[rows, :]
        probs = jnp.exp(values - log_total)
        entry = position * VOCAB_ROWS + k * 128 + lax.broadcasted_iota(jnp.int32, values.shape, 0)
        hit = (targets[...] == entry).astype(jnp.float32)
        raw_grad = probs - hit + entropy_weight * probs * (values - mean_logit)
        ratio = values / cap_value
        grad = raw_grad * (1.0 - ratio * ratio)
        grad_out[rows, :] = grad.astype(jnp.bfloat16)
        turned_out[:, :, :, rows] = grad.T.astype(jnp.bfloat16).reshape(8, 2, 32, 128)

    steps(gradient, 0, VOCAB_ROWS // 128)

    def multiply(j):
        arrival(j).wait()
        columns = step_columns(j)
        rows = turned_out[:, 1 - core].reshape(NEAR, VOCAB_ROWS)
        far_held[:, columns] = jnp.dot(
            rows, weight_held[:, columns], preferred_element_type=jnp.float32
        ).astype(jnp.bfloat16)
        leaving(j).start()

    steps(multiply)
    steps(lambda j: leaving(j).wait())


def far_gradient(place, targets, capped, totals, weight):
    return pl.pallas_call(
        far_kernel,
        out_shape=(
            jax.ShapeDtypeStruct((VOCAB_ROWS, TOKENS), jnp.bfloat16),
            jax.ShapeDtypeStruct((8, 2, 32, VOCAB_ROWS), jnp.bfloat16),
            jax.ShapeDtypeStruct((NEAR, WIDTH), jnp.bfloat16),
        ),
        in_specs=[SCALARS, IN_VMEM, IN_VMEM, IN_VMEM, IN_HBM],
        out_specs=(IN_VMEM, IN_VMEM, ANYWHERE),
        scratch_shapes=[
            pltpu.VMEM((VOCAB_ROWS, WIDTH), jnp.bfloat16),
            pltpu.VMEM((NEAR, WIDTH), jnp.bfloat16),
            pltpu.SemaphoreType.DMA((STEPS,)),
            pltpu.SemaphoreType.DMA((STEPS,)),
        ],
        compiler_params=pltpu.CompilerParams(vmem_limit_bytes=55 << 20),
        cost_estimate=pl.CostEstimate(
            flops=2 * VOCAB_ROWS * NEAR * WIDTH, bytes_accessed=9 << 20, transcendentals=1 << 18
        ),
        name="far_gradient",
    )(place, targets, capped, totals, weight)


def near_kernel(place, turned, weight, arrived, gathered, *rest):
    sends, gain_out = rest[:8], rest[8]
    weight_held, arrived_held, rows_held, first_held, second_held, in_sems, out_sems = rest[9:]
    core, y, x = place[0], place[1], place[2]

    def arrivals(j):
        columns = step_columns(j)
        return [
            pltpu.make_async_copy(weight.at[:, columns], weight_held.at[:, columns], in_sems.at[0, j]),
            pltpu.make_async_copy(arrived.at[:, columns], arrived_held.at[:, columns], in_sems.at[1, j]),
            pltpu.make_async_copy(
                gathered.at[:, core, :, columns], rows_held.at[:, :, columns], in_sems.at[2, j]
            ),
        ]

    def begin(j):
        for copy in arrivals(j):
            copy.start()

    def multiply(half, held, j):
        for copy in arrivals(j):
            copy.wait()
        columns = step_columns(j)
        rows = turned[:, core].reshape(NEAR, VOCAB_ROWS)
        part = jnp.dot(rows, weight_held[:, columns], preferred_element_type=jnp.float32)
        part = part + arrived_held[:, columns].astype(jnp.float32)
        gain_out[:, columns] = jnp.sum(
            part * rows_held[:, :, columns].reshape(NEAR, STEP).astype(jnp.float32), axis=0, keepdims=True
        )
        rounded = part.astype(jnp.bfloat16)
        own = step_columns(j - half * HALF_STEPS)
        for to_y in range(4):
            for to_x in range(4):
                up_y, up_x = lax.rem(to_y + 4 - y, 4), lax.rem(to_x + 4 - x, 4)
                outer, inner = (up_y, up_x) if half == 0 else (up_x, up_y)
                row = ((to_x % 2 * 4 + to_y) * 2 + to_x // 2) * PIECE
                held[outer, inner, :, own] = rounded[row : row + PIECE]

    steps(begin)
    leaving = []
    for half, held in ((0, first_held), (1, second_held)):
        first = half * HALF_STEPS
        steps(lambda j, half=half, held=held: multiply(half, held, j), first, first + HALF_STEPS)
        for k in range(4):
            copy = pltpu.make_async_copy(held.at[k], sends[half * 4 + k], out_sems.at[half * 4 + k])
            copy.start()
            leaving.append(copy)
    for copy in leaving:
        copy.wait()


def near_gradient(place, turned, weight, arrived, gathered):
    outs = pl.pallas_call(
        near_kernel,
        out_shape=[jax.ShapeDtypeStruct((4, PIECE, HALF), jnp.bfloat16)] * 8
        + [jax.ShapeDtypeStruct((1, WIDTH), jnp.float32)],
        in_specs=[SCALARS, IN_VMEM, IN_HBM, ANYWHERE, IN_HBM],
        out_specs=[ANYWHERE] * 8 + [IN_VMEM],
        scratch_shapes=[
            pltpu.VMEM((VOCAB_ROWS, WIDTH), jnp.bfloat16),
            pltpu.VMEM((NEAR, WIDTH), jnp.bfloat16),
            pltpu.VMEM((8, 32, WIDTH), jnp.bfloat16),
            pltpu.VMEM((4, 4, PIECE, HALF), jnp.bfloat16),
            pltpu.VMEM((4, 4, PIECE, HALF), jnp.bfloat16),
            pltpu.SemaphoreType.DMA((3, STEPS)),
            pltpu.SemaphoreType.DMA((8,)),
        ],
        compiler_params=pltpu.CompilerParams(vmem_limit_bytes=45 << 20),
        cost_estimate=pl.CostEstimate(
            flops=2 * VOCAB_ROWS * NEAR * WIDTH, bytes_accessed=12 << 20, transcendentals=0
        ),
        name="near_gradient",
    )(place, turned, weight, arrived, gathered)
    return outs[:4], outs[4:8], outs[8]


def weight_kernel(grad, gathered, out, rows_held, out_held, in_sems, out_sems):
    def arrival(j):
        columns = step_columns(j)
        return pltpu.make_async_copy(gathered.at[:, columns], rows_held.at[:, columns], in_sems.at[j])

    def leaving(j):
        columns = step_columns(j)
        return pltpu.make_async_copy(out_held.at[:, columns], out.at[:, columns], out_sems.at[j])

    def multiply(j):
        arrival(j).wait()
        columns = step_columns(j)
        out_held[:, columns] = jnp.dot(
            grad[...], rows_held[:, columns], preferred_element_type=jnp.float32
        ).astype(jnp.bfloat16)
        leaving(j).start()

    steps(lambda j: arrival(j).start())
    steps(multiply)
    steps(lambda j: leaving(j).wait())


def weight_gradient(grad, gathered):
    return pl.pallas_call(
        weight_kernel,
        out_shape=jax.ShapeDtypeStruct((VOCAB_ROWS, WIDTH), jnp.bfloat16),
        in_specs=[IN_VMEM, IN_HBM],
        out_specs=IN_HBM,
        scratch_shapes=[
            pltpu.VMEM((TOKENS, WIDTH), jnp.bfloat16),
            pltpu.VMEM((VOCAB_ROWS, WIDTH), jnp.bfloat16),
            pltpu.SemaphoreType.DMA((STEPS,)),
            pltpu.SemaphoreType.DMA((STEPS,)),
        ],
        compiler_params=pltpu.CompilerParams(vmem_limit_bytes=58 << 20),
        cost_estimate=pl.CostEstimate(
            flops=2 * VOCAB_ROWS * TOKENS * WIDTH, bytes_accessed=10 << 20, transcendentals=0
        ),
        name="weight_gradient",
    )(grad, gathered)


def on_device(hidden, norm_gain, weight, targets):
    core, y, position = lax.axis_index("core"), lax.axis_index("y"), lax.axis_index(AXES)
    x = lax.axis_index("x_hi") * 2 + lax.axis_index("x_lo")
    place = jnp.stack([core, y, x, position]).astype(jnp.int32)
    ids = targets.reshape(1, TOKENS)

    values = hidden.astype(jnp.float32)
    inverse = lax.rsqrt(jnp.mean(values * values, axis=-1, keepdims=True) + epsilon)
    unit_rows = values * inverse
    normed = (unit_rows * norm_gain).astype(jnp.bfloat16)

    line = gather_over(normed, "z", 8).reshape(PIECE, WIDTH)
    first_row = jnp.stack(gather_ring(line[:, :HALF], shift_x))
    second_row = jnp.stack(gather_ring(line[:, HALF:], shift_y))
    near_blocks = gather_ring(first_row, shift_y) + gather_ring(second_row, shift_x)
    arrived_blocks = lax.optimization_barrier(near_blocks[1:4] + near_blocks[5:])
    near_blocks = [near_blocks[0], *arrived_blocks[:3], near_blocks[4], *arrived_blocks[3:]]
    far_blocks = [swap_cores(block) for block in near_blocks]

    gathered, capped, stats = forward(place, ids, weight, near_blocks + far_blocks)
    stats = stats + swap_cores(stats)
    stats = sum_over(stats, PLANE, 16)
    stats = sum_over(stats, "z", 8)

    grad, turned, far_part = far_gradient(place, ids, capped, stats, weight)
    arrived = swap_cores(far_part)
    first_sends, second_sends, gain_part = near_gradient(
        place, turned, weight, arrived, gathered.reshape(8, 2, 32, WIDTH)
    )
    first_parts = send_ring(first_sends, shift_y)
    second_parts = send_ring(second_sends, shift_x)
    gain_part, second_parts[3] = lax.optimization_barrier((gain_part, second_parts[3]))
    gain_part = sum_over(gain_part, PLANE, 16)
    first_half = total(first_parts).astype(jnp.bfloat16)
    second_half = total(second_parts).astype(jnp.bfloat16)
    first_line = total(send_ring([first_half[k] for k in range(4)], shift_x))
    second_line = total(send_ring([second_half[k] for k in range(4)], shift_y))
    line_part = jnp.concatenate([first_line, second_line], axis=1).astype(jnp.bfloat16)
    gain_high = lax.reduce_precision(gain_part, 8, 7)
    gain_rows = jnp.concatenate([gain_high, gain_part - gain_high], axis=0).astype(jnp.bfloat16)
    message = jnp.concatenate(
        [line_part.reshape(8, 2, WIDTH), jnp.broadcast_to(gain_rows[None], (8, 2, WIDTH))], axis=1
    )
    message, grad = lax.optimization_barrier((message, grad))
    line_parts = lax.all_to_all(message, "z", 0, 0, tiled=True)
    grad_weight = weight_gradient(grad, gathered)
    line_sum = jnp.sum(line_parts.astype(jnp.float32), axis=0)
    grad_normed = line_sum[:2]
    gain_part = line_sum[2] + line_sum[3]
    grad_gain = (gain_part + swap_cores(gain_part)) / norm_gain

    total_exp, total_weighted, target_logit = stats
    log_total = cap_value + jnp.log(total_exp)
    mean_logit = total_weighted / total_exp
    every_loss = log_total - target_logit - entropy_weight * (log_total - mean_logit)
    token_loss = lax.dynamic_slice_in_dim(every_loss, position * 2, 2, 0)
    scaled = norm_gain * grad_normed
    grad_hidden = (
        scaled - unit_rows * jnp.mean(scaled * unit_rows, axis=-1, keepdims=True)
    ) * inverse
    return (token_loss, grad_hidden, grad_weight, grad_gain)


def solution(mesh):
    fine = Mesh(mesh.devices.reshape(2, 4, 2, 2, 8), AXES)
    rows = P(AXES, None)
    return jax.shard_map(
        on_device,
        mesh=fine,
        in_specs=(rows, P(), rows, P()),
        out_specs=(P(AXES), rows, rows, P()),
        check_vma=False,
    )
```

```python
import jax
import jax.numpy as jnp
from jax import lax
from jax.experimental import pallas as pl
from jax.experimental.pallas import tpu as pltpu
from jax.sharding import Mesh, PartitionSpec as P

epsilon = 1e-06
cap_value = 30.0
entropy_weight = 0.2

AXES = ("x_lo", "y", "core", "x_hi", "z")
PLANE = ("x_lo", "y", "x_hi")
WIDTH = 4608
HALF = WIDTH // 2
TOKENS = 512
NEAR = TOKENS // 2
VOCAB_ROWS = 512
PIECE = 16
STEP = 768
STEPS = WIDTH // STEP
HALF_STEPS = HALF // STEP

RING = (0, 2, 1, 3)


def shift_y(block, step):
    return lax.ppermute(block, "y", [(p, (p + step) % 4) for p in range(4)])


def shift_x(block, step):
    pairs = [(RING[p], RING[(p + step) % 4]) for p in range(4)]
    return lax.ppermute(block, ("x_lo", "x_hi"), pairs)


def swap_cores(block):
    return lax.ppermute(block, "core", [(0, 1), (1, 0)])


def gather_over(block, axes, size):
    copies = jnp.broadcast_to(block[None], (size,) + block.shape)
    return lax.all_to_all(copies, axes, 0, 0, tiled=True)


def sum_over(block, axes, size):
    return jnp.sum(gather_over(block, axes, size), axis=0)


def gather_ring(block, shift):
    across, up, down = shift(block, 2), shift(block, 3), shift(block, 1)
    return [block, up, across, down]


def send_ring(blocks, shift):
    across, up, down = shift(blocks[2], 2), shift(blocks[1], 1), shift(blocks[3], 3)
    return [blocks[0], up, across, down]


def total(blocks):
    return sum(block.astype(jnp.float32) for block in blocks)


def piece_row(core, y, x):
    piece = ((lax.rem(x, 2) * 4 + y) * 2 + core) * 2 + lax.div(x, 2)
    return pl.multiple_of(piece * PIECE, PIECE)


def step_columns(step):
    return pl.ds(pl.multiple_of(step * STEP, STEP), STEP)


def steps(body, first=0, last=STEPS):
    lax.fori_loop(first, last, lambda j, carry: (body(j), carry)[1], 0)


def forward_kernel(place, targets, weight, *rest):
    blocks = rest[:16]
    gathered, capped_out, stats_out, weight_held, rows_held, logits, weight_sems, row_sems, out_sem = rest[16:]
    core, y, x, position = place[0], place[1], place[2], place[3]

    def half_rows(half):
        return rows_held.at[:, half * HALF : (half + 1) * HALF]

    def weight_copy(j):
        columns = step_columns(j)
        return pltpu.make_async_copy(weight.at[:, columns], weight_held.at[:, columns], weight_sems.at[j])

    def place_blocks(half):
        def pieces(inner, carry):
            for far in range(2):
                owner = core if far == 0 else 1 - core
                for outer in range(4):
                    up_y, up_x = (outer, inner) if half == 0 else (inner, outer)
                    row = piece_row(owner, lax.rem(y + up_y, 4), lax.rem(x + up_x, 4))
                    pltpu.make_async_copy(
                        blocks[far * 8 + half * 4 + outer].at[inner],
                        half_rows(half).at[pl.ds(row, PIECE), :],
                        row_sems.at[half],
                    ).start()
            return carry

        lax.fori_loop(0, 4, pieces, 0)

    def multiply(j):
        weight_copy(j).wait()
        columns = step_columns(j)
        logits[...] += lax.dot_general(
            weight_held[:, columns],
            rows_held[:, columns],
            (((1,), (1,)), ((), ())),
            preferred_element_type=jnp.float32,
        )

    steps(lambda j: weight_copy(j).start(), 0, HALF_STEPS)
    place_blocks(0)
    steps(lambda j: weight_copy(j).start(), HALF_STEPS, STEPS)
    place_blocks(1)
    logits[...] = jnp.zeros_like(logits)
    pltpu.make_async_copy(half_rows(0), half_rows(0), row_sems.at[0]).wait()
    steps(multiply, 0, HALF_STEPS)
    pltpu.make_async_copy(half_rows(1), half_rows(1), row_sems.at[1]).wait()
    out_copy = pltpu.make_async_copy(rows_held, gathered, out_sem)
    out_copy.start()
    steps(multiply, HALF_STEPS, STEPS)

    def finish(k, carry):
        rows = pl.ds(pl.multiple_of(k * 64, 64), 64)
        capped = cap_value * jnp.tanh(logits[rows, :] / cap_value)
        capped_out[rows, :] = capped
        powers = jnp.exp(capped - cap_value)
        entry = position * VOCAB_ROWS + k * 64 + lax.broadcasted_iota(jnp.int32, capped.shape, 0)
        hit = targets[...] == entry
        return (
            carry[0] + jnp.sum(powers, axis=0, keepdims=True),
            carry[1] + jnp.sum(powers * capped, axis=0, keepdims=True),
            carry[2] + jnp.sum(jnp.where(hit, capped, 0.0), axis=0, keepdims=True),
        )

    sums = lax.fori_loop(0, VOCAB_ROWS // 64, finish, (jnp.zeros((1, TOKENS), jnp.float32),) * 3)
    for k in range(3):
        stats_out[k : k + 1, :] = sums[k]
    out_copy.wait()


SCALARS = pl.BlockSpec(memory_space=pltpu.SMEM)
IN_VMEM = pl.BlockSpec(memory_space=pltpu.VMEM)
IN_HBM = pl.BlockSpec(memory_space=pltpu.HBM)
ANYWHERE = pl.BlockSpec(memory_space=pl.ANY)


def forward(place, targets, weight, blocks):
    return pl.pallas_call(
        forward_kernel,
        out_shape=(
            jax.ShapeDtypeStruct((TOKENS, WIDTH), jnp.bfloat16),
            jax.ShapeDtypeStruct((VOCAB_ROWS, TOKENS), jnp.float32),
            jax.ShapeDtypeStruct((3, TOKENS), jnp.float32),
        ),
        in_specs=[SCALARS, IN_VMEM, IN_HBM] + [ANYWHERE] * 16,
        out_specs=(IN_HBM, IN_VMEM, IN_VMEM),
        scratch_shapes=[
            pltpu.VMEM((VOCAB_ROWS, WIDTH), jnp.bfloat16),
            pltpu.VMEM((TOKENS, WIDTH), jnp.bfloat16),
            pltpu.VMEM((VOCAB_ROWS, TOKENS), jnp.float32),
            pltpu.SemaphoreType.DMA((STEPS,)),
            pltpu.SemaphoreType.DMA((2,)),
            pltpu.SemaphoreType.DMA,
        ],
        compiler_params=pltpu.CompilerParams(vmem_limit_bytes=50 << 20),
        cost_estimate=pl.CostEstimate(
            flops=2 * VOCAB_ROWS * TOKENS * WIDTH, bytes_accessed=16 << 20, transcendentals=1 << 19
        ),
        name="forward",
    )(place, targets, weight, *blocks)


def far_kernel(
    place, targets, capped, totals, weight, grad_out, turned_out, far_out,
    weight_held, far_held, weight_sems, out_sems,
):
    core, position = place[0], place[3]

    def arrival(j):
        columns = step_columns(j)
        return pltpu.make_async_copy(weight.at[:, columns], weight_held.at[:, columns], weight_sems.at[j])

    def leaving(j):
        columns = step_columns(j)
        return pltpu.make_async_copy(far_held.at[:, columns], far_out.at[:, columns], out_sems.at[j])

    steps(lambda j: arrival(j).start())
    log_total = cap_value + jnp.log(totals[0:1, :])
    mean_logit = totals[1:2, :] / totals[0:1, :]

    def gradient(k):
        rows = pl.ds(pl.multiple_of(k * 128, 128), 128)
        values = capped[rows, :]
        probs = jnp.exp(values - log_total)
        entry = position * VOCAB_ROWS + k * 128 + lax.broadcasted_iota(jnp.int32, values.shape, 0)
        hit = (targets[...] == entry).astype(jnp.float32)
        raw_grad = probs - hit + entropy_weight * probs * (values - mean_logit)
        ratio = values / cap_value
        grad = raw_grad * (1.0 - ratio * ratio)
        grad_out[rows, :] = grad.astype(jnp.bfloat16)
        turned_out[:, :, :, rows] = grad.T.astype(jnp.bfloat16).reshape(8, 2, 32, 128)

    steps(gradient, 0, VOCAB_ROWS // 128)

    def multiply(j):
        arrival(j).wait()
        columns = step_columns(j)
        rows = turned_out[:, 1 - core].reshape(NEAR, VOCAB_ROWS)
        far_held[:, columns] = jnp.dot(
            rows, weight_held[:, columns], preferred_element_type=jnp.float32
        ).astype(jnp.bfloat16)
        leaving(j).start()

    steps(multiply)
    steps(lambda j: leaving(j).wait())


def far_gradient(place, targets, capped, totals, weight):
    return pl.pallas_call(
        far_kernel,
        out_shape=(
            jax.ShapeDtypeStruct((VOCAB_ROWS, TOKENS), jnp.bfloat16),
            jax.ShapeDtypeStruct((8, 2, 32, VOCAB_ROWS), jnp.bfloat16),
            jax.ShapeDtypeStruct((NEAR, WIDTH), jnp.bfloat16),
        ),
        in_specs=[SCALARS, IN_VMEM, IN_VMEM, IN_VMEM, IN_HBM],
        out_specs=(IN_VMEM, IN_VMEM, ANYWHERE),
        scratch_shapes=[
            pltpu.VMEM((VOCAB_ROWS, WIDTH), jnp.bfloat16),
            pltpu.VMEM((NEAR, WIDTH), jnp.bfloat16),
            pltpu.SemaphoreType.DMA((STEPS,)),
            pltpu.SemaphoreType.DMA((STEPS,)),
        ],
        compiler_params=pltpu.CompilerParams(vmem_limit_bytes=52 << 20),
        cost_estimate=pl.CostEstimate(
            flops=2 * VOCAB_ROWS * NEAR * WIDTH, bytes_accessed=9 << 20, transcendentals=1 << 18
        ),
        name="far_gradient",
    )(place, targets, capped, totals, weight)


def near_kernel(place, turned, weight, arrived, gathered, *rest):
    sends, gain_out = rest[:8], rest[8]
    weight_held, arrived_held, rows_held, first_held, second_held, in_sems, out_sems = rest[9:]
    core, y, x = place[0], place[1], place[2]

    def arrivals(j):
        columns = step_columns(j)
        return [
            pltpu.make_async_copy(weight.at[:, columns], weight_held.at[:, columns], in_sems.at[0, j]),
            pltpu.make_async_copy(arrived.at[:, columns], arrived_held.at[:, columns], in_sems.at[1, j]),
            pltpu.make_async_copy(
                gathered.at[:, core, :, columns], rows_held.at[:, :, columns], in_sems.at[2, j]
            ),
        ]

    def begin(j):
        for copy in arrivals(j):
            copy.start()

    def multiply(half, held, j):
        for copy in arrivals(j):
            copy.wait()
        columns = step_columns(j)
        rows = turned[:, core].reshape(NEAR, VOCAB_ROWS)
        part = jnp.dot(rows, weight_held[:, columns], preferred_element_type=jnp.float32)
        part = part + arrived_held[:, columns].astype(jnp.float32)
        gain_out[:, columns] = jnp.sum(
            part * rows_held[:, :, columns].reshape(NEAR, STEP).astype(jnp.float32), axis=0, keepdims=True
        )
        rounded = part.astype(jnp.bfloat16)
        own = step_columns(j - half * HALF_STEPS)
        for to_y in range(4):
            for to_x in range(4):
                up_y, up_x = lax.rem(to_y + 4 - y, 4), lax.rem(to_x + 4 - x, 4)
                outer, inner = (up_y, up_x) if half == 0 else (up_x, up_y)
                row = ((to_x % 2 * 4 + to_y) * 2 + to_x // 2) * PIECE
                held[outer, inner, :, own] = rounded[row : row + PIECE]

    steps(begin)
    leaving = []
    for half, held in ((0, first_held), (1, second_held)):
        first = half * HALF_STEPS
        steps(lambda j, half=half, held=held: multiply(half, held, j), first, first + HALF_STEPS)
        for k in range(4):
            copy = pltpu.make_async_copy(held.at[k], sends[half * 4 + k], out_sems.at[half * 4 + k])
            copy.start()
            leaving.append(copy)
    for copy in leaving:
        copy.wait()


def near_gradient(place, turned, weight, arrived, gathered):
    outs = pl.pallas_call(
        near_kernel,
        out_shape=[jax.ShapeDtypeStruct((4, PIECE, HALF), jnp.bfloat16)] * 8
        + [jax.ShapeDtypeStruct((1, WIDTH), jnp.float32)],
        in_specs=[SCALARS, IN_VMEM, IN_HBM, ANYWHERE, IN_HBM],
        out_specs=[ANYWHERE] * 8 + [IN_VMEM],
        scratch_shapes=[
            pltpu.VMEM((VOCAB_ROWS, WIDTH), jnp.bfloat16),
            pltpu.VMEM((NEAR, WIDTH), jnp.bfloat16),
            pltpu.VMEM((8, 32, WIDTH), jnp.bfloat16),
            pltpu.VMEM((4, 4, PIECE, HALF), jnp.bfloat16),
            pltpu.VMEM((4, 4, PIECE, HALF), jnp.bfloat16),
            pltpu.SemaphoreType.DMA((3, STEPS)),
            pltpu.SemaphoreType.DMA((8,)),
        ],
        compiler_params=pltpu.CompilerParams(vmem_limit_bytes=45 << 20),
        cost_estimate=pl.CostEstimate(
            flops=2 * VOCAB_ROWS * NEAR * WIDTH, bytes_accessed=12 << 20, transcendentals=0
        ),
        name="near_gradient",
    )(place, turned, weight, arrived, gathered)
    return outs[:4], outs[4:8], outs[8]


def weight_kernel(grad, gathered, out, rows_held, out_held, in_sems, out_sems):
    def arrival(j):
        columns = step_columns(j)
        return pltpu.make_async_copy(gathered.at[:, columns], rows_held.at[:, columns], in_sems.at[j])

    def leaving(j):
        columns = step_columns(j)
        return pltpu.make_async_copy(out_held.at[:, columns], out.at[:, columns], out_sems.at[j])

    def multiply(j):
        arrival(j).wait()
        columns = step_columns(j)
        out_held[:, columns] = jnp.dot(
            grad[...], rows_held[:, columns], preferred_element_type=jnp.float32
        ).astype(jnp.bfloat16)
        leaving(j).start()

    steps(lambda j: arrival(j).start())
    steps(multiply)
    steps(lambda j: leaving(j).wait())


def weight_gradient(grad, gathered):
    return pl.pallas_call(
        weight_kernel,
        out_shape=jax.ShapeDtypeStruct((VOCAB_ROWS, WIDTH), jnp.bfloat16),
        in_specs=[IN_VMEM, IN_HBM],
        out_specs=IN_HBM,
        scratch_shapes=[
            pltpu.VMEM((TOKENS, WIDTH), jnp.bfloat16),
            pltpu.VMEM((VOCAB_ROWS, WIDTH), jnp.bfloat16),
            pltpu.SemaphoreType.DMA((STEPS,)),
            pltpu.SemaphoreType.DMA((STEPS,)),
        ],
        compiler_params=pltpu.CompilerParams(vmem_limit_bytes=50 << 20),
        cost_estimate=pl.CostEstimate(
            flops=2 * VOCAB_ROWS * TOKENS * WIDTH, bytes_accessed=10 << 20, transcendentals=0
        ),
        name="weight_gradient",
    )(grad, gathered)


def on_device(hidden, norm_gain, weight, targets):
    core, y, position = lax.axis_index("core"), lax.axis_index("y"), lax.axis_index(AXES)
    x = lax.axis_index("x_hi") * 2 + lax.axis_index("x_lo")
    place = jnp.stack([core, y, x, position]).astype(jnp.int32)
    ids = targets.reshape(1, TOKENS)

    values = hidden.astype(jnp.float32)
    inverse = lax.rsqrt(jnp.mean(values * values, axis=-1, keepdims=True) + epsilon)
    unit_rows = values * inverse
    normed = (unit_rows * norm_gain).astype(jnp.bfloat16)

    line = gather_over(normed, "z", 8).reshape(PIECE, WIDTH)
    first_row = jnp.stack(gather_ring(line[:, :HALF], shift_x))
    second_row = jnp.stack(gather_ring(line[:, HALF:], shift_y))
    near_blocks = gather_ring(first_row, shift_y) + gather_ring(second_row, shift_x)
    arrived_blocks = lax.optimization_barrier(near_blocks[1:4] + near_blocks[5:])
    near_blocks = [near_blocks[0], *arrived_blocks[:3], near_blocks[4], *arrived_blocks[3:]]
    far_blocks = [swap_cores(block) for block in near_blocks]

    gathered, capped, stats = forward(place, ids, weight, near_blocks + far_blocks)
    stats = stats + swap_cores(stats)
    stats = sum_over(stats, PLANE, 16)
    stats = sum_over(stats, "z", 8)

    grad, turned, far_part = far_gradient(place, ids, capped, stats, weight)
    arrived = swap_cores(far_part)
    first_sends, second_sends, gain_part = near_gradient(
        place, turned, weight, arrived, gathered.reshape(8, 2, 32, WIDTH)
    )
    first_parts = send_ring(first_sends, shift_y)
    second_parts = send_ring(second_sends, shift_x)
    gain_part, first_parts[2] = lax.optimization_barrier((gain_part, first_parts[2]))
    gain_part = sum_over(gain_part, PLANE, 16)
    gain_part = gain_part + swap_cores(gain_part)
    first_half = total(first_parts).astype(jnp.bfloat16)
    second_half = total(second_parts).astype(jnp.bfloat16)
    first_line = total(send_ring([first_half[k] for k in range(4)], shift_x))
    second_line = total(send_ring([second_half[k] for k in range(4)], shift_y))
    line_part = jnp.concatenate([first_line, second_line], axis=1).astype(jnp.bfloat16)
    gain_high = lax.reduce_precision(gain_part, 8, 7)
    gain_rows = jnp.concatenate([gain_high, gain_part - gain_high], axis=0).astype(jnp.bfloat16)
    message = jnp.concatenate(
        [line_part.reshape(8, 2, WIDTH), jnp.broadcast_to(gain_rows[None], (8, 2, WIDTH))], axis=1
    )
    message, grad = lax.optimization_barrier((message, grad))
    line_parts = lax.all_to_all(message, "z", 0, 0, tiled=True)
    grad_weight = weight_gradient(grad, gathered)
    line_sum = jnp.sum(line_parts.astype(jnp.float32), axis=0)
    grad_normed = line_sum[:2]
    grad_gain = (line_sum[2] + line_sum[3]) / norm_gain

    total_exp, total_weighted, target_logit = stats
    log_total = cap_value + jnp.log(total_exp)
    mean_logit = total_weighted / total_exp
    every_loss = log_total - target_logit - entropy_weight * (log_total - mean_logit)
    token_loss = lax.dynamic_slice_in_dim(every_loss, position * 2, 2, 0)
    scaled = norm_gain * grad_normed
    grad_hidden = (
        scaled - unit_rows * jnp.mean(scaled * unit_rows, axis=-1, keepdims=True)
    ) * inverse
    return (token_loss, grad_hidden, grad_weight, grad_gain)


def solution(mesh):
    fine = Mesh(mesh.devices.reshape(2, 4, 2, 2, 8), AXES)
    rows = P(AXES, None)
    return jax.shard_map(
        on_device,
        mesh=fine,
        in_specs=(rows, P(), rows, P()),
        out_specs=(P(AXES), rows, rows, P()),
        check_vma=False,
    )
```

```python
import jax
import jax.numpy as jnp
from jax import lax
from jax.experimental import pallas as pl
from jax.experimental.pallas import tpu as pltpu
from jax.sharding import Mesh, PartitionSpec as P

epsilon = 1e-06
cap_value = 30.0
entropy_weight = 0.2

AXES = ("x_lo", "y", "core", "x_hi", "z")
PLANE = ("x_lo", "y", "x_hi")
WIDTH = 4608
HALF = WIDTH // 2
TOKENS = 512
VOCAB_ROWS = 512
PIECE = 16
STEP = 768
STEPS = WIDTH // STEP
HALF_STEPS = HALF // STEP

CROSS = ("x_lo", "y", "core", "x_hi")


def cross_pairs(step, x_core):
    index = lambda x, y, core: ((x % 2 * 4 + y) * 2 + core) * 2 + x // 2
    pairs = []
    for x in range(4):
        for y in range(4):
            for core in range(2):
                to = ((x + step) % 4, y) if core == x_core else (x, (y + step) % 4)
                pairs.append((index(x, y, core), index(*to, core)))
    return pairs


def shift_first(block, step):
    return lax.ppermute(block, CROSS, cross_pairs(step, 0))


def shift_second(block, step):
    return lax.ppermute(block, CROSS, cross_pairs(step, 1))


def swap_cores(block):
    return lax.ppermute(block, "core", [(0, 1), (1, 0)])


def gather_over(block, axes, size):
    copies = jnp.broadcast_to(block[None], (size,) + block.shape)
    return lax.all_to_all(copies, axes, 0, 0, tiled=True)


def sum_over(block, axes, size):
    return jnp.sum(gather_over(block, axes, size), axis=0)


def gather_ring(block, shift):
    across, up, down = shift(block, 2), shift(block, 3), shift(block, 1)
    return [block, up, across, down]


def send_ring(blocks, shift):
    across, up, down = shift(blocks[2], 2), shift(blocks[1], 1), shift(blocks[3], 3)
    return [blocks[0], up, across, down]


def total(blocks):
    return sum(block.astype(jnp.float32) for block in blocks)


def piece_row(core, y, x):
    piece = ((lax.rem(x, 2) * 4 + y) * 2 + core) * 2 + lax.div(x, 2)
    return pl.multiple_of(piece * PIECE, PIECE)


def step_columns(step):
    return pl.ds(pl.multiple_of(step * STEP, STEP), STEP)


def steps(body, first=0, last=STEPS):
    lax.fori_loop(first, last, lambda j, carry: (body(j), carry)[1], 0)


def forward_kernel(place, targets, weight, *rest):
    blocks = rest[:8]
    gathered, capped_out, stats_out, weight_held, rows_held, logits, weight_sems, row_sems, out_sem = rest[8:]
    core, y, x, position = place[0], place[1], place[2], place[3]

    def half_columns(half):
        return pl.ds(pl.multiple_of(half * HALF, HALF), HALF)

    def half_rows(half):
        return rows_held.at[:, half_columns(half)]

    def weight_copy(j):
        columns = step_columns(j)
        return pltpu.make_async_copy(weight.at[:, columns], weight_held.at[:, columns], weight_sems.at[j])

    def place_blocks(half, held):
        def pieces(inner, carry):
            for outer in range(4):
                up_y = jnp.where(half == 0, outer, inner)
                up_x = jnp.where(half == 0, inner, outer)
                for owner in range(2):
                    row = piece_row(owner, lax.rem(y + up_y, 4), lax.rem(x + up_x, 4))
                    pltpu.make_async_copy(
                        held[outer].at[inner, owner],
                        rows_held.at[pl.ds(row, PIECE), half_columns(half)],
                        row_sems.at[half],
                    ).start()
            return carry

        lax.fori_loop(0, 4, pieces, 0)

    def multiply(j):
        weight_copy(j).wait()
        columns = step_columns(j)
        logits[...] += lax.dot_general(
            weight_held[:, columns],
            rows_held[:, columns],
            (((1,), (1,)), ((), ())),
            preferred_element_type=jnp.float32,
        )

    steps(lambda j: weight_copy(j).start(), 0, HALF_STEPS)
    place_blocks(core, blocks[:4])
    steps(lambda j: weight_copy(j).start(), HALF_STEPS, STEPS)
    place_blocks(1 - core, blocks[4:])
    logits[...] = jnp.zeros_like(logits)
    pltpu.make_async_copy(half_rows(0), half_rows(0), row_sems.at[0]).wait()
    steps(multiply, 0, HALF_STEPS)
    pltpu.make_async_copy(half_rows(1), half_rows(1), row_sems.at[1]).wait()
    out_copy = pltpu.make_async_copy(rows_held, gathered, out_sem)
    out_copy.start()
    steps(multiply, HALF_STEPS, STEPS)

    def finish(k, carry):
        rows = pl.ds(pl.multiple_of(k * 64, 64), 64)
        capped = cap_value * jnp.tanh(logits[rows, :] / cap_value)
        capped_out[rows, :] = capped
        powers = jnp.exp(capped - cap_value)
        entry = position * VOCAB_ROWS + k * 64 + lax.broadcasted_iota(jnp.int32, capped.shape, 0)
        hit = targets[...] == entry
        return (
            carry[0] + jnp.sum(powers, axis=0, keepdims=True),
            carry[1] + jnp.sum(powers * capped, axis=0, keepdims=True),
            carry[2] + jnp.sum(jnp.where(hit, capped, 0.0), axis=0, keepdims=True),
        )

    sums = lax.fori_loop(0, VOCAB_ROWS // 64, finish, (jnp.zeros((1, TOKENS), jnp.float32),) * 3)
    for k in range(3):
        stats_out[k : k + 1, :] = sums[k]
    out_copy.wait()


SCALARS = pl.BlockSpec(memory_space=pltpu.SMEM)
IN_VMEM = pl.BlockSpec(memory_space=pltpu.VMEM)
IN_HBM = pl.BlockSpec(memory_space=pltpu.HBM)
ANYWHERE = pl.BlockSpec(memory_space=pl.ANY)


def forward(place, targets, weight, blocks):
    return pl.pallas_call(
        forward_kernel,
        out_shape=(
            jax.ShapeDtypeStruct((TOKENS, WIDTH), jnp.bfloat16),
            jax.ShapeDtypeStruct((VOCAB_ROWS, TOKENS), jnp.float32),
            jax.ShapeDtypeStruct((3, TOKENS), jnp.float32),
        ),
        in_specs=[SCALARS, IN_VMEM, IN_HBM] + [ANYWHERE] * 8,
        out_specs=(IN_HBM, IN_VMEM, IN_VMEM),
        scratch_shapes=[
            pltpu.VMEM((VOCAB_ROWS, WIDTH), jnp.bfloat16),
            pltpu.VMEM((TOKENS, WIDTH), jnp.bfloat16),
            pltpu.VMEM((VOCAB_ROWS, TOKENS), jnp.float32),
            pltpu.SemaphoreType.DMA((STEPS,)),
            pltpu.SemaphoreType.DMA((2,)),
            pltpu.SemaphoreType.DMA,
        ],
        compiler_params=pltpu.CompilerParams(vmem_limit_bytes=50 << 20),
        cost_estimate=pl.CostEstimate(
            flops=2 * VOCAB_ROWS * TOKENS * WIDTH, bytes_accessed=16 << 20, transcendentals=1 << 19
        ),
        name="forward",
    )(place, targets, weight, *blocks)


def far_kernel(
    place, targets, capped, totals, weight, grad_out, turned_out, far_out,
    weight_held, far_held, weight_sems, out_sems,
):
    core, position = place[0], place[3]

    def arrival(j):
        columns = step_columns((1 - core) * HALF_STEPS + j)
        return pltpu.make_async_copy(
            weight.at[:, columns], weight_held.at[:, step_columns(j)], weight_sems.at[j]
        )

    def leaving(j):
        columns = step_columns(j)
        return pltpu.make_async_copy(far_held.at[:, columns], far_out.at[:, columns], out_sems.at[j])

    steps(lambda j: arrival(j).start(), 0, HALF_STEPS)
    log_total = cap_value + jnp.log(totals[0:1, :])
    mean_logit = totals[1:2, :] / totals[0:1, :]

    def gradient(k):
        rows = pl.ds(pl.multiple_of(k * 128, 128), 128)
        values = capped[rows, :]
        probs = jnp.exp(values - log_total)
        entry = position * VOCAB_ROWS + k * 128 + lax.broadcasted_iota(jnp.int32, values.shape, 0)
        hit = (targets[...] == entry).astype(jnp.float32)
        raw_grad = probs - hit + entropy_weight * probs * (values - mean_logit)
        ratio = values / cap_value
        grad = raw_grad * (1.0 - ratio * ratio)
        grad_out[rows, :] = grad.astype(jnp.bfloat16)
        turned_out[:, rows] = grad.T.astype(jnp.bfloat16)

    steps(gradient, 0, VOCAB_ROWS // 128)

    def multiply(j):
        arrival(j).wait()
        columns = step_columns(j)
        far_held[:, columns] = jnp.dot(
            turned_out[...], weight_held[:, columns], preferred_element_type=jnp.float32
        ).astype(jnp.bfloat16)
        leaving(j).start()

    steps(multiply, 0, HALF_STEPS)
    steps(lambda j: leaving(j).wait(), 0, HALF_STEPS)


def far_gradient(place, targets, capped, totals, weight):
    return pl.pallas_call(
        far_kernel,
        out_shape=(
            jax.ShapeDtypeStruct((VOCAB_ROWS, TOKENS), jnp.bfloat16),
            jax.ShapeDtypeStruct((TOKENS, VOCAB_ROWS), jnp.bfloat16),
            jax.ShapeDtypeStruct((TOKENS, HALF), jnp.bfloat16),
        ),
        in_specs=[SCALARS, IN_VMEM, IN_VMEM, IN_VMEM, IN_HBM],
        out_specs=(IN_VMEM, IN_VMEM, ANYWHERE),
        scratch_shapes=[
            pltpu.VMEM((VOCAB_ROWS, HALF), jnp.bfloat16),
            pltpu.VMEM((TOKENS, HALF), jnp.bfloat16),
            pltpu.SemaphoreType.DMA((HALF_STEPS,)),
            pltpu.SemaphoreType.DMA((HALF_STEPS,)),
        ],
        compiler_params=pltpu.CompilerParams(vmem_limit_bytes=52 << 20),
        cost_estimate=pl.CostEstimate(
            flops=VOCAB_ROWS * TOKENS * WIDTH, bytes_accessed=9 << 20, transcendentals=1 << 18
        ),
        name="far_gradient",
    )(place, targets, capped, totals, weight)


def near_kernel(place, turned, weight, arrived, gathered, *rest):
    sends, gain_out = rest[:4], rest[4]
    weight_held, arrived_held, rows_held, held, in_sems, out_sems = rest[5:]
    core, y, x = place[0], place[1], place[2]

    def arrivals(j):
        columns, own = step_columns(core * HALF_STEPS + j), step_columns(j)
        return [
            pltpu.make_async_copy(weight.at[:, columns], weight_held.at[:, own], in_sems.at[0, j]),
            pltpu.make_async_copy(arrived.at[:, own], arrived_held.at[:, own], in_sems.at[1, j]),
            pltpu.make_async_copy(gathered.at[:, columns], rows_held.at[:, own], in_sems.at[2, j]),
        ]

    def begin(j):
        for copy in arrivals(j):
            copy.start()

    def multiply(j):
        for copy in arrivals(j):
            copy.wait()
        columns = step_columns(j)
        part = jnp.dot(turned[...], weight_held[:, columns], preferred_element_type=jnp.float32)
        part = part + arrived_held[:, columns].astype(jnp.float32)
        gain_out[:, columns] = jnp.sum(
            part * rows_held[:, columns].astype(jnp.float32), axis=0, keepdims=True
        )
        rounded = part.astype(jnp.bfloat16)
        for to_y in range(4):
            for to_x in range(4):
                up_y, up_x = lax.rem(to_y + 4 - y, 4), lax.rem(to_x + 4 - x, 4)
                outer, inner = jnp.where(core == 0, up_y, up_x), jnp.where(core == 0, up_x, up_y)
                for owner in range(2):
                    row = (((to_x % 2 * 4 + to_y) * 2 + owner) * 2 + to_x // 2) * PIECE
                    held[outer, inner, owner, :, columns] = rounded[row : row + PIECE]

    steps(begin, 0, HALF_STEPS)
    steps(multiply, 0, HALF_STEPS)
    leaving = [pltpu.make_async_copy(held.at[k], sends[k], out_sems.at[k]) for k in range(4)]
    for copy in leaving:
        copy.start()
    for copy in leaving:
        copy.wait()


def near_gradient(place, turned, weight, arrived, gathered):
    outs = pl.pallas_call(
        near_kernel,
        out_shape=[jax.ShapeDtypeStruct((4, 2, PIECE, HALF), jnp.bfloat16)] * 4
        + [jax.ShapeDtypeStruct((1, HALF), jnp.float32)],
        in_specs=[SCALARS, IN_VMEM, IN_HBM, ANYWHERE, IN_HBM],
        out_specs=[ANYWHERE] * 4 + [IN_VMEM],
        scratch_shapes=[
            pltpu.VMEM((VOCAB_ROWS, HALF), jnp.bfloat16),
            pltpu.VMEM((TOKENS, HALF), jnp.bfloat16),
            pltpu.VMEM((TOKENS, HALF), jnp.bfloat16),
            pltpu.VMEM((4, 4, 2, PIECE, HALF), jnp.bfloat16),
            pltpu.SemaphoreType.DMA((3, HALF_STEPS)),
            pltpu.SemaphoreType.DMA((4,)),
        ],
        compiler_params=pltpu.CompilerParams(vmem_limit_bytes=45 << 20),
        cost_estimate=pl.CostEstimate(
            flops=VOCAB_ROWS * TOKENS * WIDTH, bytes_accessed=12 << 20, transcendentals=0
        ),
        name="near_gradient",
    )(place, turned, weight, arrived, gathered)
    return outs[:4], outs[4]


def weight_kernel(grad, gathered, out, rows_held, out_held, in_sems, out_sems):
    def arrival(j):
        columns = step_columns(j)
        return pltpu.make_async_copy(gathered.at[:, columns], rows_held.at[:, columns], in_sems.at[j])

    def leaving(j):
        columns = step_columns(j)
        return pltpu.make_async_copy(out_held.at[:, columns], out.at[:, columns], out_sems.at[j])

    def multiply(j):
        arrival(j).wait()
        columns = step_columns(j)
        out_held[:, columns] = jnp.dot(
            grad[...], rows_held[:, columns], preferred_element_type=jnp.float32
        ).astype(jnp.bfloat16)
        leaving(j).start()

    steps(lambda j: arrival(j).start())
    steps(multiply)
    steps(lambda j: leaving(j).wait())


def weight_gradient(grad, gathered):
    return pl.pallas_call(
        weight_kernel,
        out_shape=jax.ShapeDtypeStruct((VOCAB_ROWS, WIDTH), jnp.bfloat16),
        in_specs=[IN_VMEM, IN_HBM],
        out_specs=IN_HBM,
        scratch_shapes=[
            pltpu.VMEM((TOKENS, WIDTH), jnp.bfloat16),
            pltpu.VMEM((VOCAB_ROWS, WIDTH), jnp.bfloat16),
            pltpu.SemaphoreType.DMA((STEPS,)),
            pltpu.SemaphoreType.DMA((STEPS,)),
        ],
        compiler_params=pltpu.CompilerParams(vmem_limit_bytes=50 << 20),
        cost_estimate=pl.CostEstimate(
            flops=2 * VOCAB_ROWS * TOKENS * WIDTH, bytes_accessed=10 << 20, transcendentals=0
        ),
        name="weight_gradient",
    )(grad, gathered)


def on_device(hidden, norm_gain, weight, targets):
    core, y, position = lax.axis_index("core"), lax.axis_index("y"), lax.axis_index(AXES)
    x = lax.axis_index("x_hi") * 2 + lax.axis_index("x_lo")
    place = jnp.stack([core, y, x, position]).astype(jnp.int32)
    ids = targets.reshape(1, TOKENS)

    values = hidden.astype(jnp.float32)
    inverse = lax.rsqrt(jnp.mean(values * values, axis=-1, keepdims=True) + epsilon)
    unit_rows = values * inverse
    normed = (unit_rows * norm_gain).astype(jnp.bfloat16)

    def by_core(mine, other, axis):
        return jnp.where(
            core == 0, jnp.concatenate([mine, other], axis), jnp.concatenate([other, mine], axis)
        )

    mine = lax.dynamic_slice_in_dim(normed, core * HALF, HALF, 1)
    other = swap_cores(lax.dynamic_slice_in_dim(normed, (1 - core) * HALF, HALF, 1))
    line = gather_over(by_core(mine, other, 0), "z", 8)
    line = line.reshape(8, 2, 2, HALF).transpose(1, 0, 2, 3).reshape(2, PIECE, HALF)
    blocks = gather_ring(jnp.stack(gather_ring(line, shift_first)), shift_second)
    blocks = blocks + [swap_cores(block) for block in blocks]

    gathered, capped, stats = forward(place, ids, weight, blocks)
    stats = stats + swap_cores(stats)
    stats = sum_over(stats, PLANE, 16)
    stats = sum_over(stats, "z", 8)

    grad, turned, far_part = far_gradient(place, ids, capped, stats, weight)
    arrived = swap_cores(far_part)
    sends, gain_part = near_gradient(place, turned, weight, arrived, gathered)
    parts = send_ring(sends, shift_second)
    gain_part, parts[1] = lax.optimization_barrier((gain_part, parts[1]))
    gain_part = sum_over(gain_part, PLANE, 16)
    half_sum = total(parts).astype(jnp.bfloat16)
    line_part = total(send_ring([half_sum[k] for k in range(4)], shift_first)).astype(jnp.bfloat16)
    line_part = line_part.reshape(2, 8, 2, HALF).transpose(1, 0, 2, 3).reshape(8, 4, HALF)
    gain_high = lax.reduce_precision(gain_part, 8, 7)
    gain_rows = jnp.concatenate([gain_high, gain_part - gain_high], axis=0).astype(jnp.bfloat16)
    message = jnp.concatenate([line_part, jnp.broadcast_to(gain_rows[None], (8, 2, HALF))], axis=1)
    message, grad = lax.optimization_barrier((message, grad))
    line_parts = lax.all_to_all(message, "z", 0, 0, tiled=True)
    grad_weight = weight_gradient(grad, gathered)
    line_parts, grad_weight = lax.optimization_barrier((line_parts, grad_weight))
    line_sum = jnp.sum(line_parts.astype(jnp.float32), axis=0)
    gain_sum = line_sum[4:5] + line_sum[5:6]
    first_core, second_core = line_sum[0:2], line_sum[2:4]
    mine = jnp.concatenate([jnp.where(core == 0, first_core, second_core), gain_sum], axis=0)
    theirs = jnp.concatenate([jnp.where(core == 0, second_core, first_core), gain_sum], axis=0)
    whole = by_core(mine, swap_cores(theirs), 1)
    grad_normed = whole[:2]
    grad_gain = whole[2] / norm_gain

    total_exp, total_weighted, target_logit = stats
    log_total = cap_value + jnp.log(total_exp)
    mean_logit = total_weighted / total_exp
    every_loss = log_total - target_logit - entropy_weight * (log_total - mean_logit)
    token_loss = lax.dynamic_slice_in_dim(every_loss, position * 2, 2, 0)
    scaled = norm_gain * grad_normed
    grad_hidden = (
        scaled - unit_rows * jnp.mean(scaled * unit_rows, axis=-1, keepdims=True)
    ) * inverse
    return (token_loss, grad_hidden, grad_weight, grad_gain)


def solution(mesh):
    fine = Mesh(mesh.devices.reshape(2, 4, 2, 2, 8), AXES)
    rows = P(AXES, None)
    return jax.shard_map(
        on_device,
        mesh=fine,
        in_specs=(rows, P(), rows, P()),
        out_specs=(P(AXES), rows, rows, P()),
        check_vma=False,
    )
```

```python
import jax
import jax.numpy as jnp
from jax import lax
from jax.experimental import pallas as pl
from jax.experimental.pallas import tpu as pltpu
from jax.sharding import Mesh, PartitionSpec as P

epsilon = 1e-06
cap_value = 30.0
entropy_weight = 0.2

AXES = ("x_lo", "y", "core", "x_hi", "z")
PLANE = ("x_lo", "y", "x_hi")
WIDTH = 4608
HALF = WIDTH // 2
TOKENS = 512
VOCAB_ROWS = 512
PIECE = 16
STEP = 768
STEPS = WIDTH // STEP
HALF_STEPS = HALF // STEP

CROSS = ("x_lo", "y", "core", "x_hi")


def cross_pairs(step, x_core):
    index = lambda x, y, core: ((x % 2 * 4 + y) * 2 + core) * 2 + x // 2
    pairs = []
    for x in range(4):
        for y in range(4):
            for core in range(2):
                to = ((x + step) % 4, y) if core == x_core else (x, (y + step) % 4)
                pairs.append((index(x, y, core), index(*to, core)))
    return pairs


def shift_first(block, step):
    return lax.ppermute(block, CROSS, cross_pairs(step, 0))


def shift_second(block, step):
    return lax.ppermute(block, CROSS, cross_pairs(step, 1))


def swap_cores(block):
    return lax.ppermute(block, "core", [(0, 1), (1, 0)])


def gather_over(block, axes, size):
    copies = jnp.broadcast_to(block[None], (size,) + block.shape)
    return lax.all_to_all(copies, axes, 0, 0, tiled=True)


def sum_over(block, axes, size):
    return jnp.sum(gather_over(block, axes, size), axis=0)


def gather_ring(block, shift):
    across, up, down = shift(block, 2), shift(block, 3), shift(block, 1)
    return [block, up, across, down]


def send_ring(blocks, shift):
    across, up, down = shift(blocks[2], 2), shift(blocks[1], 1), shift(blocks[3], 3)
    return [blocks[0], up, across, down]


def total(blocks):
    return sum(block.astype(jnp.float32) for block in blocks)


def piece_row(core, y, x):
    piece = ((lax.rem(x, 2) * 4 + y) * 2 + core) * 2 + lax.div(x, 2)
    return pl.multiple_of(piece * PIECE, PIECE)


def step_columns(step):
    return pl.ds(pl.multiple_of(step * STEP, STEP), STEP)


def steps(body, first=0, last=STEPS):
    lax.fori_loop(first, last, lambda j, carry: (body(j), carry)[1], 0)


def forward_kernel(place, targets, weight, *rest):
    blocks = rest[:8]
    gathered, capped_out, stats_out, weight_held, rows_held, logits, weight_sems, row_sems, out_sem = rest[8:]
    core, y, x, position = place[0], place[1], place[2], place[3]

    def half_columns(half):
        return pl.ds(pl.multiple_of(half * HALF, HALF), HALF)

    def half_rows(half):
        return rows_held.at[:, half_columns(half)]

    def weight_copy(j):
        columns = step_columns(j)
        return pltpu.make_async_copy(weight.at[:, columns], weight_held.at[:, columns], weight_sems.at[j])

    def place_blocks(half, held):
        def pieces(inner, carry):
            for outer in range(4):
                up_y = jnp.where(half == 0, outer, inner)
                up_x = jnp.where(half == 0, inner, outer)
                for owner in range(2):
                    row = piece_row(owner, lax.rem(y + up_y, 4), lax.rem(x + up_x, 4))
                    pltpu.make_async_copy(
                        held[outer].at[inner, owner],
                        rows_held.at[pl.ds(row, PIECE), half_columns(half)],
                        row_sems.at[half],
                    ).start()
            return carry

        lax.fori_loop(0, 4, pieces, 0)

    def multiply(j):
        weight_copy(j).wait()
        columns = step_columns(j)
        logits[...] += lax.dot_general(
            weight_held[:, columns],
            rows_held[:, columns],
            (((1,), (1,)), ((), ())),
            preferred_element_type=jnp.float32,
        )

    steps(lambda j: weight_copy(j).start(), 0, HALF_STEPS)
    place_blocks(core, blocks[:4])
    steps(lambda j: weight_copy(j).start(), HALF_STEPS, STEPS)
    place_blocks(1 - core, blocks[4:])
    logits[...] = jnp.zeros_like(logits)
    pltpu.make_async_copy(half_rows(0), half_rows(0), row_sems.at[0]).wait()
    steps(multiply, 0, HALF_STEPS)
    pltpu.make_async_copy(half_rows(1), half_rows(1), row_sems.at[1]).wait()
    out_copy = pltpu.make_async_copy(rows_held, gathered, out_sem)
    out_copy.start()
    steps(multiply, HALF_STEPS, STEPS)

    def finish(k, carry):
        rows = pl.ds(pl.multiple_of(k * 64, 64), 64)
        capped = cap_value * jnp.tanh(logits[rows, :] / cap_value)
        capped_out[rows, :] = capped
        powers = jnp.exp(capped - cap_value)
        entry = position * VOCAB_ROWS + k * 64 + lax.broadcasted_iota(jnp.int32, capped.shape, 0)
        hit = targets[...] == entry
        return (
            carry[0] + jnp.sum(powers, axis=0, keepdims=True),
            carry[1] + jnp.sum(powers * capped, axis=0, keepdims=True),
            carry[2] + jnp.sum(jnp.where(hit, capped, 0.0), axis=0, keepdims=True),
        )

    sums = lax.fori_loop(0, VOCAB_ROWS // 64, finish, (jnp.zeros((1, TOKENS), jnp.float32),) * 3)
    for k in range(3):
        stats_out[k : k + 1, :] = sums[k]
    out_copy.wait()


SCALARS = pl.BlockSpec(memory_space=pltpu.SMEM)
IN_VMEM = pl.BlockSpec(memory_space=pltpu.VMEM)
IN_HBM = pl.BlockSpec(memory_space=pltpu.HBM)
ANYWHERE = pl.BlockSpec(memory_space=pl.ANY)


def forward(place, targets, weight, blocks):
    return pl.pallas_call(
        forward_kernel,
        out_shape=(
            jax.ShapeDtypeStruct((TOKENS, WIDTH), jnp.bfloat16),
            jax.ShapeDtypeStruct((VOCAB_ROWS, TOKENS), jnp.float32),
            jax.ShapeDtypeStruct((3, TOKENS), jnp.float32),
        ),
        in_specs=[SCALARS, IN_VMEM, IN_HBM] + [ANYWHERE] * 8,
        out_specs=(IN_HBM, IN_VMEM, IN_VMEM),
        scratch_shapes=[
            pltpu.VMEM((VOCAB_ROWS, WIDTH), jnp.bfloat16),
            pltpu.VMEM((TOKENS, WIDTH), jnp.bfloat16),
            pltpu.VMEM((VOCAB_ROWS, TOKENS), jnp.float32),
            pltpu.SemaphoreType.DMA((STEPS,)),
            pltpu.SemaphoreType.DMA((2,)),
            pltpu.SemaphoreType.DMA,
        ],
        compiler_params=pltpu.CompilerParams(vmem_limit_bytes=50 << 20),
        cost_estimate=pl.CostEstimate(
            flops=2 * VOCAB_ROWS * TOKENS * WIDTH, bytes_accessed=16 << 20, transcendentals=1 << 19
        ),
        name="forward",
    )(place, targets, weight, *blocks)


def far_kernel(
    place, targets, capped, totals, weight, grad_out, turned_out, far_out,
    weight_held, far_held, weight_sems, out_sems,
):
    core, position = place[0], place[3]

    def arrival(j):
        columns = step_columns((1 - core) * HALF_STEPS + j)
        return pltpu.make_async_copy(
            weight.at[:, columns], weight_held.at[:, step_columns(j)], weight_sems.at[j]
        )

    def leaving(j):
        columns = step_columns(j)
        return pltpu.make_async_copy(far_held.at[:, columns], far_out.at[:, columns], out_sems.at[j])

    steps(lambda j: arrival(j).start(), 0, HALF_STEPS)
    log_total = cap_value + jnp.log(totals[0:1, :])
    mean_logit = totals[1:2, :] / totals[0:1, :]

    def gradient(k):
        rows = pl.ds(pl.multiple_of(k * 128, 128), 128)
        values = capped[rows, :]
        probs = jnp.exp(values - log_total)
        entry = position * VOCAB_ROWS + k * 128 + lax.broadcasted_iota(jnp.int32, values.shape, 0)
        hit = (targets[...] == entry).astype(jnp.float32)
        raw_grad = probs - hit + entropy_weight * probs * (values - mean_logit)
        ratio = values / cap_value
        grad = raw_grad * (1.0 - ratio * ratio)
        grad_out[rows, :] = grad.astype(jnp.bfloat16)
        turned_out[:, rows] = grad.T.astype(jnp.bfloat16)

    steps(gradient, 0, VOCAB_ROWS // 128)

    def multiply(j):
        arrival(j).wait()
        columns = step_columns(j)
        far_held[:, columns] = jnp.dot(
            turned_out[...], weight_held[:, columns], preferred_element_type=jnp.float32
        ).astype(jnp.bfloat16)
        leaving(j).start()

    steps(multiply, 0, HALF_STEPS)
    steps(lambda j: leaving(j).wait(), 0, HALF_STEPS)


def far_gradient(place, targets, capped, totals, weight):
    return pl.pallas_call(
        far_kernel,
        out_shape=(
            jax.ShapeDtypeStruct((VOCAB_ROWS, TOKENS), jnp.bfloat16),
            jax.ShapeDtypeStruct((TOKENS, VOCAB_ROWS), jnp.bfloat16),
            jax.ShapeDtypeStruct((TOKENS, HALF), jnp.bfloat16),
        ),
        in_specs=[SCALARS, IN_VMEM, IN_VMEM, IN_VMEM, IN_HBM],
        out_specs=(IN_VMEM, IN_VMEM, ANYWHERE),
        scratch_shapes=[
            pltpu.VMEM((VOCAB_ROWS, HALF), jnp.bfloat16),
            pltpu.VMEM((TOKENS, HALF), jnp.bfloat16),
            pltpu.SemaphoreType.DMA((HALF_STEPS,)),
            pltpu.SemaphoreType.DMA((HALF_STEPS,)),
        ],
        compiler_params=pltpu.CompilerParams(vmem_limit_bytes=52 << 20),
        cost_estimate=pl.CostEstimate(
            flops=VOCAB_ROWS * TOKENS * WIDTH, bytes_accessed=9 << 20, transcendentals=1 << 18
        ),
        name="far_gradient",
    )(place, targets, capped, totals, weight)


def near_kernel(place, turned, weight, arrived, gathered, *rest):
    sends = rest[:4]
    weight_held, arrived_held, rows_held, held, in_sems, out_sems = rest[4:]
    core, y, x = place[0], place[1], place[2]

    def arrivals(j):
        columns, own = step_columns(core * HALF_STEPS + j), step_columns(j)
        return [
            pltpu.make_async_copy(weight.at[:, columns], weight_held.at[:, own], in_sems.at[0, j]),
            pltpu.make_async_copy(arrived.at[:, own], arrived_held.at[:, own], in_sems.at[1, j]),
            pltpu.make_async_copy(gathered.at[:, columns], rows_held.at[:, own], in_sems.at[2, j]),
        ]

    def begin(j):
        for copy in arrivals(j):
            copy.start()

    def multiply(j):
        for copy in arrivals(j):
            copy.wait()
        columns = step_columns(j)
        part = jnp.dot(turned[...], weight_held[:, columns], preferred_element_type=jnp.float32)
        part = part + arrived_held[:, columns].astype(jnp.float32)
        gain = jnp.sum(part * rows_held[:, columns].astype(jnp.float32), axis=0, keepdims=True)
        high = gain.astype(jnp.bfloat16).astype(jnp.float32)
        row = lax.broadcasted_iota(jnp.int32, (PIECE, STEP), 0)
        gain_piece = jnp.where(row == 0, high, jnp.where(row == 1, gain - high, 0.0)).astype(jnp.bfloat16)
        for k in range(4):
            held[k, 8, :, columns] = gain_piece
        rounded = part.astype(jnp.bfloat16)
        for to_y in range(4):
            for to_x in range(4):
                up_y, up_x = lax.rem(to_y + 4 - y, 4), lax.rem(to_x + 4 - x, 4)
                outer, inner = jnp.where(core == 0, up_y, up_x), jnp.where(core == 0, up_x, up_y)
                for owner in range(2):
                    row = (((to_x % 2 * 4 + to_y) * 2 + owner) * 2 + to_x // 2) * PIECE
                    held[outer, inner * 2 + owner, :, columns] = rounded[row : row + PIECE]

    steps(begin, 0, HALF_STEPS)
    steps(multiply, 0, HALF_STEPS)
    leaving = [pltpu.make_async_copy(held.at[k], sends[k], out_sems.at[k]) for k in range(4)]
    for copy in leaving:
        copy.start()
    for copy in leaving:
        copy.wait()


def near_gradient(place, turned, weight, arrived, gathered):
    return pl.pallas_call(
        near_kernel,
        out_shape=[jax.ShapeDtypeStruct((9, PIECE, HALF), jnp.bfloat16)] * 4,
        in_specs=[SCALARS, IN_VMEM, IN_HBM, ANYWHERE, IN_HBM],
        out_specs=[ANYWHERE] * 4,
        scratch_shapes=[
            pltpu.VMEM((VOCAB_ROWS, HALF), jnp.bfloat16),
            pltpu.VMEM((TOKENS, HALF), jnp.bfloat16),
            pltpu.VMEM((TOKENS, HALF), jnp.bfloat16),
            pltpu.VMEM((4, 9, PIECE, HALF), jnp.bfloat16),
            pltpu.SemaphoreType.DMA((3, HALF_STEPS)),
            pltpu.SemaphoreType.DMA((4,)),
        ],
        compiler_params=pltpu.CompilerParams(vmem_limit_bytes=45 << 20),
        cost_estimate=pl.CostEstimate(
            flops=VOCAB_ROWS * TOKENS * WIDTH, bytes_accessed=12 << 20, transcendentals=0
        ),
        name="near_gradient",
    )(place, turned, weight, arrived, gathered)


def weight_kernel(grad, gathered, out, rows_held, out_held, in_sems, out_sems):
    def arrival(j):
        columns = step_columns(j)
        return pltpu.make_async_copy(gathered.at[:, columns], rows_held.at[:, columns], in_sems.at[j])

    def leaving(j):
        columns = step_columns(j)
        return pltpu.make_async_copy(out_held.at[:, columns], out.at[:, columns], out_sems.at[j])

    def multiply(j):
        arrival(j).wait()
        columns = step_columns(j)
        out_held[:, columns] = jnp.dot(
            grad[...], rows_held[:, columns], preferred_element_type=jnp.float32
        ).astype(jnp.bfloat16)
        leaving(j).start()

    steps(lambda j: arrival(j).start())
    steps(multiply)
    steps(lambda j: leaving(j).wait())


def weight_gradient(grad, gathered):
    return pl.pallas_call(
        weight_kernel,
        out_shape=jax.ShapeDtypeStruct((VOCAB_ROWS, WIDTH), jnp.bfloat16),
        in_specs=[IN_VMEM, IN_HBM],
        out_specs=IN_HBM,
        scratch_shapes=[
            pltpu.VMEM((TOKENS, WIDTH), jnp.bfloat16),
            pltpu.VMEM((VOCAB_ROWS, WIDTH), jnp.bfloat16),
            pltpu.SemaphoreType.DMA((STEPS,)),
            pltpu.SemaphoreType.DMA((STEPS,)),
        ],
        compiler_params=pltpu.CompilerParams(vmem_limit_bytes=50 << 20),
        cost_estimate=pl.CostEstimate(
            flops=2 * VOCAB_ROWS * TOKENS * WIDTH, bytes_accessed=10 << 20, transcendentals=0
        ),
        name="weight_gradient",
    )(grad, gathered)


def on_device(hidden, norm_gain, weight, targets):
    core, y, position = lax.axis_index("core"), lax.axis_index("y"), lax.axis_index(AXES)
    x = lax.axis_index("x_hi") * 2 + lax.axis_index("x_lo")
    place = jnp.stack([core, y, x, position]).astype(jnp.int32)
    ids = targets.reshape(1, TOKENS)

    values = hidden.astype(jnp.float32)
    inverse = lax.rsqrt(jnp.mean(values * values, axis=-1, keepdims=True) + epsilon)
    unit_rows = values * inverse
    normed = (unit_rows * norm_gain).astype(jnp.bfloat16)

    def by_core(mine, other, axis):
        return jnp.where(
            core == 0, jnp.concatenate([mine, other], axis), jnp.concatenate([other, mine], axis)
        )

    mine = lax.dynamic_slice_in_dim(normed, core * HALF, HALF, 1)
    other = swap_cores(lax.dynamic_slice_in_dim(normed, (1 - core) * HALF, HALF, 1))
    line = gather_over(by_core(mine, other, 0), "z", 8)
    line = line.reshape(8, 2, 2, HALF).transpose(1, 0, 2, 3).reshape(2, PIECE, HALF)
    blocks = gather_ring(jnp.stack(gather_ring(line, shift_first)), shift_second)
    blocks = blocks + [swap_cores(block) for block in blocks]

    gathered, capped, stats = forward(place, ids, weight, blocks)
    stats = stats + swap_cores(stats)
    stats = sum_over(stats, PLANE, 16)
    stats = sum_over(stats, "z", 8)

    grad, turned, far_part = far_gradient(place, ids, capped, stats, weight)
    arrived = swap_cores(far_part)
    sends = near_gradient(place, turned, weight, arrived, gathered)

    def gain_rows(piece):
        gain = piece[0:1] + piece[1:2]
        high = lax.reduce_precision(gain, 8, 7)
        return jnp.concatenate([high, gain - high], axis=0).astype(jnp.bfloat16)

    parts = send_ring(sends, shift_second)
    grad, parts[1] = lax.optimization_barrier((grad, parts[1]))
    grad_weight = weight_gradient(grad, gathered)
    grad_weight, *parts = lax.optimization_barrier((grad_weight, *parts))
    half_sum = total(parts)
    half_rows = half_sum[:8].astype(jnp.bfloat16)
    gain_piece = jnp.pad(gain_rows(half_sum[8]), ((0, PIECE - 2), (0, 0)))[None]
    pieces = [jnp.concatenate([half_rows[2 * k : 2 * k + 2], gain_piece], axis=0) for k in range(4)]
    line_sum = total(send_ring(pieces, shift_first))
    line_part = line_sum[:2].astype(jnp.bfloat16)
    line_part = line_part.reshape(2, 8, 2, HALF).transpose(1, 0, 2, 3).reshape(8, 4, HALF)
    gain_pair = gain_rows(line_sum[2])
    message = jnp.concatenate([line_part, jnp.broadcast_to(gain_pair[None], (8, 2, HALF))], axis=1)
    line_parts = lax.all_to_all(message, "z", 0, 0, tiled=True)
    line_sum = jnp.sum(line_parts.astype(jnp.float32), axis=0)
    gain_sum = line_sum[4:5] + line_sum[5:6]
    first_core, second_core = line_sum[0:2], line_sum[2:4]
    mine = jnp.concatenate([jnp.where(core == 0, first_core, second_core), gain_sum], axis=0)
    theirs = jnp.concatenate([jnp.where(core == 0, second_core, first_core), gain_sum], axis=0)
    whole = by_core(mine, swap_cores(theirs), 1)
    grad_normed = whole[:2]
    grad_gain = whole[2] / norm_gain

    total_exp, total_weighted, target_logit = stats
    log_total = cap_value + jnp.log(total_exp)
    mean_logit = total_weighted / total_exp
    every_loss = log_total - target_logit - entropy_weight * (log_total - mean_logit)
    token_loss = lax.dynamic_slice_in_dim(every_loss, position * 2, 2, 0)
    scaled = norm_gain * grad_normed
    grad_hidden = (
        scaled - unit_rows * jnp.mean(scaled * unit_rows, axis=-1, keepdims=True)
    ) * inverse
    return (token_loss, grad_hidden, grad_weight, grad_gain)


def solution(mesh):
    fine = Mesh(mesh.devices.reshape(2, 4, 2, 2, 8), AXES)
    rows = P(AXES, None)
    return jax.shard_map(
        on_device,
        mesh=fine,
        in_specs=(rows, P(), rows, P()),
        out_specs=(P(AXES), rows, rows, P()),
        check_vma=False,
    )
```

```python
import jax
import jax.numpy as jnp
from jax import lax
from jax.experimental import pallas as pl
from jax.experimental.pallas import tpu as pltpu
from jax.sharding import Mesh, PartitionSpec as P

epsilon = 1e-06
cap_value = 30.0
entropy_weight = 0.2

AXES = ("x_lo", "y", "core", "x_hi", "z")
PLANE = ("x_lo", "y", "x_hi")
WIDTH = 4608
HALF = WIDTH // 2
TOKENS = 512
VOCAB_ROWS = 512
PIECE = 16
STEP = 768
STEPS = WIDTH // STEP
HALF_STEPS = HALF // STEP

CROSS = ("x_lo", "y", "core", "x_hi")


def cross_pairs(step, x_core):
    index = lambda x, y, core: ((x % 2 * 4 + y) * 2 + core) * 2 + x // 2
    pairs = []
    for x in range(4):
        for y in range(4):
            for core in range(2):
                to = ((x + step) % 4, y) if core == x_core else (x, (y + step) % 4)
                pairs.append((index(x, y, core), index(*to, core)))
    return pairs


def shift_first(block, step):
    return lax.ppermute(block, CROSS, cross_pairs(step, 0))


def shift_second(block, step):
    return lax.ppermute(block, CROSS, cross_pairs(step, 1))


def swap_cores(block):
    return lax.ppermute(block, "core", [(0, 1), (1, 0)])


def gather_over(block, axes, size):
    copies = jnp.broadcast_to(block[None], (size,) + block.shape)
    return lax.all_to_all(copies, axes, 0, 0, tiled=True)


def sum_over(block, axes, size):
    return jnp.sum(gather_over(block, axes, size), axis=0)


def gather_ring(block, shift):
    across, up, down = shift(block, 2), shift(block, 3), shift(block, 1)
    return [block, up, across, down]


def send_ring(blocks, shift):
    across, up, down = shift(blocks[2], 2), shift(blocks[1], 1), shift(blocks[3], 3)
    return [blocks[0], up, across, down]


def total(blocks):
    return sum(block.astype(jnp.float32) for block in blocks)


def piece_row(core, y, x):
    piece = ((lax.rem(x, 2) * 4 + y) * 2 + core) * 2 + lax.div(x, 2)
    return pl.multiple_of(piece * PIECE, PIECE)


def step_columns(step):
    return pl.ds(pl.multiple_of(step * STEP, STEP), STEP)


def steps(body, first=0, last=STEPS):
    lax.fori_loop(first, last, lambda j, carry: (body(j), carry)[1], 0)


def forward_kernel(place, targets, weight, *rest):
    blocks = rest[:8]
    gathered, capped_out, stats_out, weight_held, rows_held, logits, weight_sems, row_sems, out_sem = rest[8:]
    core, y, x, position = place[0], place[1], place[2], place[3]

    def half_columns(half):
        return pl.ds(pl.multiple_of(half * HALF, HALF), HALF)

    def half_rows(half):
        return rows_held.at[:, half_columns(half)]

    def weight_copy(j):
        columns = step_columns(j)
        return pltpu.make_async_copy(weight.at[:, columns], weight_held.at[:, columns], weight_sems.at[j])

    def place_blocks(half, held):
        def pieces(inner, carry):
            for outer in range(4):
                up_y = jnp.where(half == 0, outer, inner)
                up_x = jnp.where(half == 0, inner, outer)
                for owner in range(2):
                    row = piece_row(owner, lax.rem(y + up_y, 4), lax.rem(x + up_x, 4))
                    pltpu.make_async_copy(
                        held[outer].at[inner, owner],
                        rows_held.at[pl.ds(row, PIECE), half_columns(half)],
                        row_sems.at[half],
                    ).start()
            return carry

        lax.fori_loop(0, 4, pieces, 0)

    def multiply(j):
        weight_copy(j).wait()
        columns = step_columns(j)
        logits[...] += lax.dot_general(
            weight_held[:, columns],
            rows_held[:, columns],
            (((1,), (1,)), ((), ())),
            preferred_element_type=jnp.float32,
        )

    steps(lambda j: weight_copy(j).start(), 0, HALF_STEPS)
    place_blocks(core, blocks[:4])
    steps(lambda j: weight_copy(j).start(), HALF_STEPS, STEPS)
    place_blocks(1 - core, blocks[4:])
    logits[...] = jnp.zeros_like(logits)
    pltpu.make_async_copy(half_rows(0), half_rows(0), row_sems.at[0]).wait()
    steps(multiply, 0, HALF_STEPS)
    pltpu.make_async_copy(half_rows(1), half_rows(1), row_sems.at[1]).wait()
    out_copy = pltpu.make_async_copy(rows_held, gathered, out_sem)
    out_copy.start()
    steps(multiply, HALF_STEPS, STEPS)

    def finish(k, carry):
        rows = pl.ds(pl.multiple_of(k * 64, 64), 64)
        capped = cap_value * jnp.tanh(logits[rows, :] / cap_value)
        capped_out[rows, :] = capped
        powers = jnp.exp(capped - cap_value)
        entry = position * VOCAB_ROWS + k * 64 + lax.broadcasted_iota(jnp.int32, capped.shape, 0)
        hit = targets[...] == entry
        return (
            carry[0] + jnp.sum(powers, axis=0, keepdims=True),
            carry[1] + jnp.sum(powers * capped, axis=0, keepdims=True),
            carry[2] + jnp.sum(jnp.where(hit, capped, 0.0), axis=0, keepdims=True),
        )

    sums = lax.fori_loop(0, VOCAB_ROWS // 64, finish, (jnp.zeros((1, TOKENS), jnp.float32),) * 3)
    for k in range(3):
        stats_out[k : k + 1, :] = sums[k]
    out_copy.wait()


SCALARS = pl.BlockSpec(memory_space=pltpu.SMEM)
IN_VMEM = pl.BlockSpec(memory_space=pltpu.VMEM)
IN_HBM = pl.BlockSpec(memory_space=pltpu.HBM)
ANYWHERE = pl.BlockSpec(memory_space=pl.ANY)


def forward(place, targets, weight, blocks):
    return pl.pallas_call(
        forward_kernel,
        out_shape=(
            jax.ShapeDtypeStruct((TOKENS, WIDTH), jnp.bfloat16),
            jax.ShapeDtypeStruct((VOCAB_ROWS, TOKENS), jnp.float32),
            jax.ShapeDtypeStruct((3, TOKENS), jnp.float32),
        ),
        in_specs=[SCALARS, IN_VMEM, IN_HBM] + [ANYWHERE] * 8,
        out_specs=(IN_HBM, IN_VMEM, IN_VMEM),
        scratch_shapes=[
            pltpu.VMEM((VOCAB_ROWS, WIDTH), jnp.bfloat16),
            pltpu.VMEM((TOKENS, WIDTH), jnp.bfloat16),
            pltpu.VMEM((VOCAB_ROWS, TOKENS), jnp.float32),
            pltpu.SemaphoreType.DMA((STEPS,)),
            pltpu.SemaphoreType.DMA((2,)),
            pltpu.SemaphoreType.DMA,
        ],
        compiler_params=pltpu.CompilerParams(vmem_limit_bytes=50 << 20),
        cost_estimate=pl.CostEstimate(
            flops=2 * VOCAB_ROWS * TOKENS * WIDTH, bytes_accessed=16 << 20, transcendentals=1 << 19
        ),
        name="forward",
    )(place, targets, weight, *blocks)


def far_kernel(
    place, targets, capped, totals, weight, grad_out, turned_out, far_out,
    weight_held, far_held, weight_sems, out_sems,
):
    core, position = place[0], place[3]

    def arrival(j):
        columns = step_columns((1 - core) * HALF_STEPS + j)
        return pltpu.make_async_copy(
            weight.at[:, columns], weight_held.at[:, step_columns(j)], weight_sems.at[j]
        )

    def leaving(j):
        columns = step_columns(j)
        return pltpu.make_async_copy(far_held.at[:, columns], far_out.at[:, columns], out_sems.at[j])

    steps(lambda j: arrival(j).start(), 0, HALF_STEPS)
    log_total = cap_value + jnp.log(totals[0:1, :])
    mean_logit = totals[1:2, :] / totals[0:1, :]

    def gradient(k):
        rows = pl.ds(pl.multiple_of(k * 128, 128), 128)
        values = capped[rows, :]
        probs = jnp.exp(values - log_total)
        entry = position * VOCAB_ROWS + k * 128 + lax.broadcasted_iota(jnp.int32, values.shape, 0)
        hit = (targets[...] == entry).astype(jnp.float32)
        raw_grad = probs - hit + entropy_weight * probs * (values - mean_logit)
        ratio = values / cap_value
        grad = raw_grad * (1.0 - ratio * ratio)
        grad_out[rows, :] = grad.astype(jnp.bfloat16)
        turned_out[:, rows] = grad.T.astype(jnp.bfloat16)

    steps(gradient, 0, VOCAB_ROWS // 128)

    def multiply(j):
        arrival(j).wait()
        columns = step_columns(j)
        far_held[:, columns] = jnp.dot(
            turned_out[...], weight_held[:, columns], preferred_element_type=jnp.float32
        ).astype(jnp.bfloat16)
        leaving(j).start()

    steps(multiply, 0, HALF_STEPS)
    steps(lambda j: leaving(j).wait(), 0, HALF_STEPS)


def far_gradient(place, targets, capped, totals, weight):
    return pl.pallas_call(
        far_kernel,
        out_shape=(
            jax.ShapeDtypeStruct((VOCAB_ROWS, TOKENS), jnp.bfloat16),
            jax.ShapeDtypeStruct((TOKENS, VOCAB_ROWS), jnp.bfloat16),
            jax.ShapeDtypeStruct((TOKENS, HALF), jnp.bfloat16),
        ),
        in_specs=[SCALARS, IN_VMEM, IN_VMEM, IN_VMEM, IN_HBM],
        out_specs=(IN_VMEM, IN_VMEM, ANYWHERE),
        scratch_shapes=[
            pltpu.VMEM((VOCAB_ROWS, HALF), jnp.bfloat16),
            pltpu.VMEM((TOKENS, HALF), jnp.bfloat16),
            pltpu.SemaphoreType.DMA((HALF_STEPS,)),
            pltpu.SemaphoreType.DMA((HALF_STEPS,)),
        ],
        compiler_params=pltpu.CompilerParams(vmem_limit_bytes=52 << 20),
        cost_estimate=pl.CostEstimate(
            flops=VOCAB_ROWS * TOKENS * WIDTH, bytes_accessed=9 << 20, transcendentals=1 << 18
        ),
        name="far_gradient",
    )(place, targets, capped, totals, weight)


def near_kernel(place, turned, weight, arrived, gathered, *rest):
    sends = rest[:4]
    weight_held, arrived_held, rows_held, held, in_sems, out_sems = rest[4:]
    core, y, x = place[0], place[1], place[2]

    def arrivals(j):
        columns, own = step_columns(core * HALF_STEPS + j), step_columns(j)
        return [
            pltpu.make_async_copy(weight.at[:, columns], weight_held.at[:, own], in_sems.at[0, j]),
            pltpu.make_async_copy(arrived.at[:, own], arrived_held.at[:, own], in_sems.at[1, j]),
            pltpu.make_async_copy(gathered.at[:, columns], rows_held.at[:, own], in_sems.at[2, j]),
        ]

    def begin(j):
        for copy in arrivals(j):
            copy.start()

    def multiply(j):
        for copy in arrivals(j):
            copy.wait()
        columns = step_columns(j)
        part = jnp.dot(turned[...], weight_held[:, columns], preferred_element_type=jnp.float32)
        part = part + arrived_held[:, columns].astype(jnp.float32)
        gain = jnp.sum(part * rows_held[:, columns].astype(jnp.float32), axis=0, keepdims=True)
        high = gain.astype(jnp.bfloat16).astype(jnp.float32)
        row = lax.broadcasted_iota(jnp.int32, (PIECE, STEP), 0)
        gain_piece = jnp.where(row == 0, high, jnp.where(row == 1, gain - high, 0.0)).astype(jnp.bfloat16)
        for k in range(4):
            held[k, 8, :, columns] = gain_piece
        rounded = part.astype(jnp.bfloat16)
        for to_y in range(4):
            for to_x in range(4):
                up_y, up_x = lax.rem(to_y + 4 - y, 4), lax.rem(to_x + 4 - x, 4)
                outer, inner = jnp.where(core == 0, up_y, up_x), jnp.where(core == 0, up_x, up_y)
                for owner in range(2):
                    row = (((to_x % 2 * 4 + to_y) * 2 + owner) * 2 + to_x // 2) * PIECE
                    held[outer, inner * 2 + owner, :, columns] = rounded[row : row + PIECE]

    steps(begin, 0, HALF_STEPS)
    steps(multiply, 0, HALF_STEPS)
    leaving = [pltpu.make_async_copy(held.at[k], sends[k], out_sems.at[k]) for k in range(4)]
    for copy in leaving:
        copy.start()
    for copy in leaving:
        copy.wait()


def near_gradient(place, turned, weight, arrived, gathered):
    return pl.pallas_call(
        near_kernel,
        out_shape=[jax.ShapeDtypeStruct((9, PIECE, HALF), jnp.bfloat16)] * 4,
        in_specs=[SCALARS, IN_VMEM, IN_HBM, ANYWHERE, IN_HBM],
        out_specs=[ANYWHERE] * 4,
        scratch_shapes=[
            pltpu.VMEM((VOCAB_ROWS, HALF), jnp.bfloat16),
            pltpu.VMEM((TOKENS, HALF), jnp.bfloat16),
            pltpu.VMEM((TOKENS, HALF), jnp.bfloat16),
            pltpu.VMEM((4, 9, PIECE, HALF), jnp.bfloat16),
            pltpu.SemaphoreType.DMA((3, HALF_STEPS)),
            pltpu.SemaphoreType.DMA((4,)),
        ],
        compiler_params=pltpu.CompilerParams(vmem_limit_bytes=45 << 20),
        cost_estimate=pl.CostEstimate(
            flops=VOCAB_ROWS * TOKENS * WIDTH, bytes_accessed=12 << 20, transcendentals=0
        ),
        name="near_gradient",
    )(place, turned, weight, arrived, gathered)


def weight_kernel(grad, gathered, out, rows_held, out_held, in_sems, out_sems):
    def arrival(j):
        columns = step_columns(j)
        return pltpu.make_async_copy(gathered.at[:, columns], rows_held.at[:, columns], in_sems.at[j])

    def leaving(j):
        columns = step_columns(j)
        return pltpu.make_async_copy(out_held.at[:, columns], out.at[:, columns], out_sems.at[j])

    def multiply(j):
        arrival(j).wait()
        columns = step_columns(j)
        out_held[:, columns] = jnp.dot(
            grad[...], rows_held[:, columns], preferred_element_type=jnp.float32
        ).astype(jnp.bfloat16)
        leaving(j).start()

    steps(lambda j: arrival(j).start())
    steps(multiply)
    steps(lambda j: leaving(j).wait())


def weight_gradient(grad, gathered):
    return pl.pallas_call(
        weight_kernel,
        out_shape=jax.ShapeDtypeStruct((VOCAB_ROWS, WIDTH), jnp.bfloat16),
        in_specs=[IN_VMEM, IN_HBM],
        out_specs=IN_HBM,
        scratch_shapes=[
            pltpu.VMEM((TOKENS, WIDTH), jnp.bfloat16),
            pltpu.VMEM((VOCAB_ROWS, WIDTH), jnp.bfloat16),
            pltpu.SemaphoreType.DMA((STEPS,)),
            pltpu.SemaphoreType.DMA((STEPS,)),
        ],
        compiler_params=pltpu.CompilerParams(vmem_limit_bytes=50 << 20),
        cost_estimate=pl.CostEstimate(
            flops=2 * VOCAB_ROWS * TOKENS * WIDTH, bytes_accessed=10 << 20, transcendentals=0
        ),
        name="weight_gradient",
    )(grad, gathered)


def on_device(hidden, norm_gain, weight, targets):
    core, y, position = lax.axis_index("core"), lax.axis_index("y"), lax.axis_index(AXES)
    x = lax.axis_index("x_hi") * 2 + lax.axis_index("x_lo")
    place = jnp.stack([core, y, x, position]).astype(jnp.int32)
    ids = targets.reshape(1, TOKENS)

    values = hidden.astype(jnp.float32)
    inverse = lax.rsqrt(jnp.mean(values * values, axis=-1, keepdims=True) + epsilon)
    unit_rows = values * inverse
    normed = (unit_rows * norm_gain).astype(jnp.bfloat16)

    halves = normed.reshape(2, 2, HALF).transpose(1, 0, 2)
    halves = jnp.broadcast_to(halves[:, None], (2, 8, 2, HALF)).reshape(16, 2, HALF)
    line = lax.all_to_all(halves, ("core", "z"), 0, 0, tiled=True).reshape(2, PIECE, HALF)
    blocks = gather_ring(jnp.stack(gather_ring(line, shift_first)), shift_second)
    blocks = blocks + [swap_cores(block) for block in blocks]

    gathered, capped, stats = forward(place, ids, weight, blocks)
    stats = sum_over(stats, PLANE, 16)
    stats = sum_over(stats, ("core", "z"), 16)

    grad, turned, far_part = far_gradient(place, ids, capped, stats, weight)
    arrived = swap_cores(far_part)
    sends = near_gradient(place, turned, weight, arrived, gathered)

    def gain_rows(piece):
        gain = piece[0:1] + piece[1:2]
        high = lax.reduce_precision(gain, 8, 7)
        return jnp.concatenate([high, gain - high], axis=0).astype(jnp.bfloat16)

    parts = send_ring(sends, shift_second)
    grad, parts[1] = lax.optimization_barrier((grad, parts[1]))
    grad_weight = weight_gradient(grad, gathered)
    grad_weight, *parts = lax.optimization_barrier((grad_weight, *parts))
    half_sum = total(parts)
    half_rows = half_sum[:8].astype(jnp.bfloat16)
    gain_piece = jnp.pad(gain_rows(half_sum[8]), ((0, PIECE - 2), (0, 0)))[None]
    pieces = [jnp.concatenate([half_rows[2 * k : 2 * k + 2], gain_piece], axis=0) for k in range(4)]
    line_sum = total(send_ring(pieces, shift_first))
    line_part = line_sum[:2].astype(jnp.bfloat16)
    gain_pair = gain_rows(line_sum[2])
    message = jnp.concatenate(
        [line_part.reshape(16, 2, HALF), jnp.broadcast_to(gain_pair[None], (16, 2, HALF))], axis=1
    )
    line_parts = lax.all_to_all(message, ("core", "z"), 0, 0, tiled=True)
    sums = jnp.sum(line_parts.astype(jnp.float32).reshape(2, 8, 4, HALF), axis=1)
    grad_normed = jnp.concatenate([sums[0, :2], sums[1, :2]], axis=1)
    grad_gain = (sums[:, 2] + sums[:, 3]).reshape(WIDTH) / norm_gain

    total_exp, total_weighted, target_logit = stats
    log_total = cap_value + jnp.log(total_exp)
    mean_logit = total_weighted / total_exp
    every_loss = log_total - target_logit - entropy_weight * (log_total - mean_logit)
    token_loss = lax.dynamic_slice_in_dim(every_loss, position * 2, 2, 0)
    scaled = norm_gain * grad_normed
    grad_hidden = (
        scaled - unit_rows * jnp.mean(scaled * unit_rows, axis=-1, keepdims=True)
    ) * inverse
    return (token_loss, grad_hidden, grad_weight, grad_gain)


def solution(mesh):
    fine = Mesh(mesh.devices.reshape(2, 4, 2, 2, 8), AXES)
    rows = P(AXES, None)
    return jax.shard_map(
        on_device,
        mesh=fine,
        in_specs=(rows, P(), rows, P()),
        out_specs=(P(AXES), rows, rows, P()),
        check_vma=False,
    )
```

```python
import jax
import jax.numpy as jnp
from jax import lax
from jax.experimental import pallas as pl
from jax.experimental.pallas import tpu as pltpu
from jax.sharding import Mesh, PartitionSpec as P

epsilon = 1e-06
cap_value = 30.0
entropy_weight = 0.2

AXES = ("x_lo", "y", "core", "x_hi", "z")
PLANE = ("x_lo", "y", "x_hi")
WIDTH = 4608
HALF = WIDTH // 2
TOKENS = 512
VOCAB_ROWS = 512
PIECE = 16
STEP = 768
STEPS = WIDTH // STEP
HALF_STEPS = HALF // STEP

CROSS = ("x_lo", "y", "core", "x_hi")


def cross_pairs(step, x_core):
    index = lambda x, y, core: ((x % 2 * 4 + y) * 2 + core) * 2 + x // 2
    pairs = []
    for x in range(4):
        for y in range(4):
            for core in range(2):
                to = ((x + step) % 4, y) if core == x_core else (x, (y + step) % 4)
                pairs.append((index(x, y, core), index(*to, core)))
    return pairs


def shift_first(block, step):
    return lax.ppermute(block, CROSS, cross_pairs(step, 0))


def shift_second(block, step):
    return lax.ppermute(block, CROSS, cross_pairs(step, 1))


def swap_cores(block):
    return lax.ppermute(block, "core", [(0, 1), (1, 0)])


def gather_over(block, axes, size):
    copies = jnp.broadcast_to(block[None], (size,) + block.shape)
    return lax.all_to_all(copies, axes, 0, 0, tiled=True)


def sum_over(block, axes, size):
    return jnp.sum(gather_over(block, axes, size), axis=0)


def gather_ring(block, shift):
    across, up, down = shift(block, 2), shift(block, 3), shift(block, 1)
    return [block, up, across, down]


def send_ring(blocks, shift):
    across, up, down = shift(blocks[2], 2), shift(blocks[1], 1), shift(blocks[3], 3)
    return [blocks[0], up, across, down]


def total(blocks):
    return sum(block.astype(jnp.float32) for block in blocks)


def piece_row(core, y, x):
    piece = ((lax.rem(x, 2) * 4 + y) * 2 + core) * 2 + lax.div(x, 2)
    return pl.multiple_of(piece * PIECE, PIECE)


def step_columns(step):
    return pl.ds(pl.multiple_of(step * STEP, STEP), STEP)


def steps(body, first=0, last=STEPS, unroll=False):
    lax.fori_loop(first, last, lambda j, carry: (body(j), carry)[1], 0, unroll=unroll)


def forward_kernel(place, targets, weight, *rest):
    blocks = rest[:8]
    gathered, capped_out, stats_out, weight_held, rows_held, logits, weight_sems, row_sems, out_sem = rest[8:]
    core, y, x, position = place[0], place[1], place[2], place[3]

    def half_columns(half):
        return pl.ds(pl.multiple_of(half * HALF, HALF), HALF)

    def half_rows(half):
        return rows_held.at[:, half_columns(half)]

    def weight_copy(j):
        columns = step_columns(j)
        return pltpu.make_async_copy(weight.at[:, columns], weight_held.at[:, columns], weight_sems.at[j])

    def place_blocks(half, held):
        def pieces(inner, carry):
            for outer in range(4):
                up_y = jnp.where(half == 0, outer, inner)
                up_x = jnp.where(half == 0, inner, outer)
                for owner in range(2):
                    row = piece_row(owner, lax.rem(y + up_y, 4), lax.rem(x + up_x, 4))
                    pltpu.make_async_copy(
                        held[outer].at[inner, owner],
                        rows_held.at[pl.ds(row, PIECE), half_columns(half)],
                        row_sems.at[half],
                    ).start()
            return carry

        lax.fori_loop(0, 4, pieces, 0)

    def multiply(j):
        weight_copy(j).wait()
        columns = step_columns(j)
        logits[...] += lax.dot_general(
            weight_held[:, columns],
            rows_held[:, columns],
            (((1,), (1,)), ((), ())),
            preferred_element_type=jnp.float32,
        )

    steps(lambda j: weight_copy(j).start(), 0, HALF_STEPS)
    place_blocks(core, blocks[:4])
    steps(lambda j: weight_copy(j).start(), HALF_STEPS, STEPS)
    place_blocks(1 - core, blocks[4:])
    logits[...] = jnp.zeros_like(logits)
    pltpu.make_async_copy(half_rows(0), half_rows(0), row_sems.at[0]).wait()
    steps(multiply, 0, HALF_STEPS, True)
    pltpu.make_async_copy(half_rows(1), half_rows(1), row_sems.at[1]).wait()
    out_copy = pltpu.make_async_copy(rows_held, gathered, out_sem)
    out_copy.start()
    steps(multiply, HALF_STEPS, STEPS, True)

    def finish(k, carry):
        rows = pl.ds(pl.multiple_of(k * 64, 64), 64)
        capped = cap_value * jnp.tanh(logits[rows, :] / cap_value)
        capped_out[rows, :] = capped
        powers = jnp.exp(capped - cap_value)
        entry = position * VOCAB_ROWS + k * 64 + lax.broadcasted_iota(jnp.int32, capped.shape, 0)
        hit = targets[...] == entry
        return (
            carry[0] + jnp.sum(powers, axis=0, keepdims=True),
            carry[1] + jnp.sum(powers * capped, axis=0, keepdims=True),
            carry[2] + jnp.sum(jnp.where(hit, capped, 0.0), axis=0, keepdims=True),
        )

    sums = lax.fori_loop(0, VOCAB_ROWS // 64, finish, (jnp.zeros((1, TOKENS), jnp.float32),) * 3)
    for k in range(3):
        stats_out[k : k + 1, :] = sums[k]
    out_copy.wait()


SCALARS = pl.BlockSpec(memory_space=pltpu.SMEM)
IN_VMEM = pl.BlockSpec(memory_space=pltpu.VMEM)
IN_HBM = pl.BlockSpec(memory_space=pltpu.HBM)
ANYWHERE = pl.BlockSpec(memory_space=pl.ANY)


def forward(place, targets, weight, blocks):
    return pl.pallas_call(
        forward_kernel,
        out_shape=(
            jax.ShapeDtypeStruct((TOKENS, WIDTH), jnp.bfloat16),
            jax.ShapeDtypeStruct((VOCAB_ROWS, TOKENS), jnp.float32),
            jax.ShapeDtypeStruct((3, TOKENS), jnp.float32),
        ),
        in_specs=[SCALARS, IN_VMEM, IN_HBM] + [ANYWHERE] * 8,
        out_specs=(IN_HBM, IN_VMEM, IN_VMEM),
        scratch_shapes=[
            pltpu.VMEM((VOCAB_ROWS, WIDTH), jnp.bfloat16),
            pltpu.VMEM((TOKENS, WIDTH), jnp.bfloat16),
            pltpu.VMEM((VOCAB_ROWS, TOKENS), jnp.float32),
            pltpu.SemaphoreType.DMA((STEPS,)),
            pltpu.SemaphoreType.DMA((2,)),
            pltpu.SemaphoreType.DMA,
        ],
        compiler_params=pltpu.CompilerParams(vmem_limit_bytes=50 << 20),
        cost_estimate=pl.CostEstimate(
            flops=2 * VOCAB_ROWS * TOKENS * WIDTH, bytes_accessed=16 << 20, transcendentals=1 << 19
        ),
        name="forward",
    )(place, targets, weight, *blocks)


def far_kernel(
    place, targets, capped, totals, weight, grad_out, turned_out, far_out,
    weight_held, far_held, weight_sems, out_sems,
):
    core, position = place[0], place[3]

    def arrival(j):
        columns = step_columns((1 - core) * HALF_STEPS + j)
        return pltpu.make_async_copy(
            weight.at[:, columns], weight_held.at[:, step_columns(j)], weight_sems.at[j]
        )

    def leaving(j):
        columns = step_columns(j)
        return pltpu.make_async_copy(far_held.at[:, columns], far_out.at[:, columns], out_sems.at[j])

    steps(lambda j: arrival(j).start(), 0, HALF_STEPS)
    log_total = cap_value + jnp.log(totals[0:1, :])
    mean_logit = totals[1:2, :] / totals[0:1, :]

    def gradient(k):
        rows = pl.ds(pl.multiple_of(k * 128, 128), 128)
        values = capped[rows, :]
        probs = jnp.exp(values - log_total)
        entry = position * VOCAB_ROWS + k * 128 + lax.broadcasted_iota(jnp.int32, values.shape, 0)
        hit = (targets[...] == entry).astype(jnp.float32)
        raw_grad = probs - hit + entropy_weight * probs * (values - mean_logit)
        ratio = values / cap_value
        grad = raw_grad * (1.0 - ratio * ratio)
        grad_out[rows, :] = grad.astype(jnp.bfloat16)
        turned_out[:, rows] = grad.T.astype(jnp.bfloat16)

    steps(gradient, 0, VOCAB_ROWS // 128)

    def multiply(j):
        arrival(j).wait()
        columns = step_columns(j)
        far_held[:, columns] = jnp.dot(
            turned_out[...], weight_held[:, columns], preferred_element_type=jnp.float32
        ).astype(jnp.bfloat16)
        leaving(j).start()

    steps(multiply, 0, HALF_STEPS, True)
    steps(lambda j: leaving(j).wait(), 0, HALF_STEPS)


def far_gradient(place, targets, capped, totals, weight):
    return pl.pallas_call(
        far_kernel,
        out_shape=(
            jax.ShapeDtypeStruct((VOCAB_ROWS, TOKENS), jnp.bfloat16),
            jax.ShapeDtypeStruct((TOKENS, VOCAB_ROWS), jnp.bfloat16),
            jax.ShapeDtypeStruct((TOKENS, HALF), jnp.bfloat16),
        ),
        in_specs=[SCALARS, IN_VMEM, IN_VMEM, IN_VMEM, IN_HBM],
        out_specs=(IN_VMEM, IN_VMEM, ANYWHERE),
        scratch_shapes=[
            pltpu.VMEM((VOCAB_ROWS, HALF), jnp.bfloat16),
            pltpu.VMEM((TOKENS, HALF), jnp.bfloat16),
            pltpu.SemaphoreType.DMA((HALF_STEPS,)),
            pltpu.SemaphoreType.DMA((HALF_STEPS,)),
        ],
        compiler_params=pltpu.CompilerParams(vmem_limit_bytes=52 << 20),
        cost_estimate=pl.CostEstimate(
            flops=VOCAB_ROWS * TOKENS * WIDTH, bytes_accessed=9 << 20, transcendentals=1 << 18
        ),
        name="far_gradient",
    )(place, targets, capped, totals, weight)


def near_kernel(place, turned, weight, arrived, gathered, *rest):
    sends = rest[:4]
    weight_held, arrived_held, rows_held, held, in_sems, out_sems = rest[4:]
    core, y, x = place[0], place[1], place[2]

    def arrivals(j):
        columns, own = step_columns(core * HALF_STEPS + j), step_columns(j)
        return [
            pltpu.make_async_copy(weight.at[:, columns], weight_held.at[:, own], in_sems.at[0, j]),
            pltpu.make_async_copy(arrived.at[:, own], arrived_held.at[:, own], in_sems.at[1, j]),
            pltpu.make_async_copy(gathered.at[:, columns], rows_held.at[:, own], in_sems.at[2, j]),
        ]

    def begin(j):
        for copy in arrivals(j):
            copy.start()

    def multiply(j):
        for copy in arrivals(j):
            copy.wait()
        columns = step_columns(j)
        part = jnp.dot(turned[...], weight_held[:, columns], preferred_element_type=jnp.float32)
        part = part + arrived_held[:, columns].astype(jnp.float32)
        gain = jnp.sum(part * rows_held[:, columns].astype(jnp.float32), axis=0, keepdims=True)
        high = gain.astype(jnp.bfloat16).astype(jnp.float32)
        row = lax.broadcasted_iota(jnp.int32, (PIECE, STEP), 0)
        gain_piece = jnp.where(row == 0, high, jnp.where(row == 1, gain - high, 0.0)).astype(jnp.bfloat16)
        for k in range(4):
            held[k, 8, :, columns] = gain_piece
        rounded = part.astype(jnp.bfloat16)
        for to_y in range(4):
            for to_x in range(4):
                up_y, up_x = lax.rem(to_y + 4 - y, 4), lax.rem(to_x + 4 - x, 4)
                outer, inner = jnp.where(core == 0, up_y, up_x), jnp.where(core == 0, up_x, up_y)
                for owner in range(2):
                    row = (((to_x % 2 * 4 + to_y) * 2 + owner) * 2 + to_x // 2) * PIECE
                    held[outer, inner * 2 + owner, :, columns] = rounded[row : row + PIECE]

    steps(begin, 0, HALF_STEPS)
    steps(multiply, 0, HALF_STEPS, True)
    leaving = [pltpu.make_async_copy(held.at[k], sends[k], out_sems.at[k]) for k in range(4)]
    for copy in leaving:
        copy.start()
    for copy in leaving:
        copy.wait()


def near_gradient(place, turned, weight, arrived, gathered):
    return pl.pallas_call(
        near_kernel,
        out_shape=[jax.ShapeDtypeStruct((9, PIECE, HALF), jnp.bfloat16)] * 4,
        in_specs=[SCALARS, IN_VMEM, IN_HBM, ANYWHERE, IN_HBM],
        out_specs=[ANYWHERE] * 4,
        scratch_shapes=[
            pltpu.VMEM((VOCAB_ROWS, HALF), jnp.bfloat16),
            pltpu.VMEM((TOKENS, HALF), jnp.bfloat16),
            pltpu.VMEM((TOKENS, HALF), jnp.bfloat16),
            pltpu.VMEM((4, 9, PIECE, HALF), jnp.bfloat16),
            pltpu.SemaphoreType.DMA((3, HALF_STEPS)),
            pltpu.SemaphoreType.DMA((4,)),
        ],
        compiler_params=pltpu.CompilerParams(vmem_limit_bytes=45 << 20),
        cost_estimate=pl.CostEstimate(
            flops=VOCAB_ROWS * TOKENS * WIDTH, bytes_accessed=12 << 20, transcendentals=0
        ),
        name="near_gradient",
    )(place, turned, weight, arrived, gathered)


def weight_kernel(grad, gathered, out, rows_held, out_held, in_sems, out_sems):
    def arrival(j):
        columns = step_columns(j)
        return pltpu.make_async_copy(gathered.at[:, columns], rows_held.at[:, columns], in_sems.at[j])

    def leaving(j):
        columns = step_columns(j)
        return pltpu.make_async_copy(out_held.at[:, columns], out.at[:, columns], out_sems.at[j])

    def multiply(j):
        arrival(j).wait()
        columns = step_columns(j)
        out_held[:, columns] = jnp.dot(
            grad[...], rows_held[:, columns], preferred_element_type=jnp.float32
        ).astype(jnp.bfloat16)
        leaving(j).start()

    steps(lambda j: arrival(j).start())
    steps(multiply)
    steps(lambda j: leaving(j).wait())


def weight_gradient(grad, gathered):
    return pl.pallas_call(
        weight_kernel,
        out_shape=jax.ShapeDtypeStruct((VOCAB_ROWS, WIDTH), jnp.bfloat16),
        in_specs=[IN_VMEM, IN_HBM],
        out_specs=IN_HBM,
        scratch_shapes=[
            pltpu.VMEM((TOKENS, WIDTH), jnp.bfloat16),
            pltpu.VMEM((VOCAB_ROWS, WIDTH), jnp.bfloat16),
            pltpu.SemaphoreType.DMA((STEPS,)),
            pltpu.SemaphoreType.DMA((STEPS,)),
        ],
        compiler_params=pltpu.CompilerParams(vmem_limit_bytes=50 << 20),
        cost_estimate=pl.CostEstimate(
            flops=2 * VOCAB_ROWS * TOKENS * WIDTH, bytes_accessed=10 << 20, transcendentals=0
        ),
        name="weight_gradient",
    )(grad, gathered)


def on_device(hidden, norm_gain, weight, targets):
    core, y, position = lax.axis_index("core"), lax.axis_index("y"), lax.axis_index(AXES)
    x = lax.axis_index("x_hi") * 2 + lax.axis_index("x_lo")
    place = jnp.stack([core, y, x, position]).astype(jnp.int32)
    ids = targets.reshape(1, TOKENS)

    values = hidden.astype(jnp.float32)
    inverse = lax.rsqrt(jnp.mean(values * values, axis=-1, keepdims=True) + epsilon)
    unit_rows = values * inverse
    normed = (unit_rows * norm_gain).astype(jnp.bfloat16)

    halves = normed.reshape(2, 2, HALF).transpose(1, 0, 2)
    halves = jnp.broadcast_to(halves[:, None], (2, 8, 2, HALF)).reshape(16, 2, HALF)
    line = lax.all_to_all(halves, ("core", "z"), 0, 0, tiled=True).reshape(2, PIECE, HALF)
    blocks = gather_ring(jnp.stack(gather_ring(line, shift_first)), shift_second)
    blocks = blocks + [swap_cores(block) for block in blocks]

    gathered, capped, stats = forward(place, ids, weight, blocks)
    stats = sum_over(stats, PLANE, 16)
    stats = sum_over(stats, ("core", "z"), 16)

    grad, turned, far_part = far_gradient(place, ids, capped, stats, weight)
    arrived = swap_cores(far_part)
    sends = near_gradient(place, turned, weight, arrived, gathered)

    def gain_rows(piece):
        gain = piece[0:1] + piece[1:2]
        high = lax.reduce_precision(gain, 8, 7)
        return jnp.concatenate([high, gain - high], axis=0).astype(jnp.bfloat16)

    own, *others = sends
    grad, own = lax.optimization_barrier((grad, own))
    parts = send_ring([own, *others], shift_second)
    grad_weight = weight_gradient(grad, gathered)
    grad_weight, *parts = lax.optimization_barrier((grad_weight, *parts))
    half_sum = total(parts)
    half_rows = half_sum[:8].astype(jnp.bfloat16)
    gain_piece = jnp.pad(gain_rows(half_sum[8]), ((0, PIECE - 2), (0, 0)))[None]
    pieces = [jnp.concatenate([half_rows[2 * k : 2 * k + 2], gain_piece], axis=0) for k in range(4)]
    line_sum = total(send_ring(pieces, shift_first))
    line_part = line_sum[:2].astype(jnp.bfloat16)
    gain_pair = gain_rows(line_sum[2])
    message = jnp.concatenate(
        [line_part.reshape(16, 2, HALF), jnp.broadcast_to(gain_pair[None], (16, 2, HALF))], axis=1
    )
    line_parts = lax.all_to_all(message, ("core", "z"), 0, 0, tiled=True)
    sums = jnp.sum(line_parts.astype(jnp.float32).reshape(2, 8, 4, HALF), axis=1)
    grad_normed = jnp.concatenate([sums[0, :2], sums[1, :2]], axis=1)
    grad_gain = (sums[:, 2] + sums[:, 3]).reshape(WIDTH) / norm_gain

    total_exp, total_weighted, target_logit = stats
    log_total = cap_value + jnp.log(total_exp)
    mean_logit = total_weighted / total_exp
    every_loss = log_total - target_logit - entropy_weight * (log_total - mean_logit)
    token_loss = lax.dynamic_slice_in_dim(every_loss, position * 2, 2, 0)
    scaled = norm_gain * grad_normed
    grad_hidden = (
        scaled - unit_rows * jnp.mean(scaled * unit_rows, axis=-1, keepdims=True)
    ) * inverse
    return (token_loss, grad_hidden, grad_weight, grad_gain)


def solution(mesh):
    fine = Mesh(mesh.devices.reshape(2, 4, 2, 2, 8), AXES)
    rows = P(AXES, None)
    return jax.shard_map(
        on_device,
        mesh=fine,
        in_specs=(rows, P(), rows, P()),
        out_specs=(P(AXES), rows, rows, P()),
        check_vma=False,
    )
```

```python
import jax
import jax.numpy as jnp
from jax import lax
from jax.experimental import pallas as pl
from jax.experimental.pallas import tpu as pltpu
from jax.sharding import Mesh, PartitionSpec as P

epsilon = 1e-06
cap_value = 30.0
entropy_weight = 0.2

AXES = ("x_lo", "y", "core", "x_hi", "z")
PLANE = ("x_lo", "y", "x_hi")
WIDTH = 4608
HALF = WIDTH // 2
TOKENS = 512
VOCAB_ROWS = 512
PIECE = 16
STEP = 2304
STEPS = WIDTH // STEP
HALF_STEPS = HALF // STEP

CROSS = ("x_lo", "y", "core", "x_hi")


def cross_pairs(step, x_core):
    index = lambda x, y, core: ((x % 2 * 4 + y) * 2 + core) * 2 + x // 2
    pairs = []
    for x in range(4):
        for y in range(4):
            for core in range(2):
                to = ((x + step) % 4, y) if core == x_core else (x, (y + step) % 4)
                pairs.append((index(x, y, core), index(*to, core)))
    return pairs


def shift_first(block, step):
    return lax.ppermute(block, CROSS, cross_pairs(step, 0))


def shift_second(block, step):
    return lax.ppermute(block, CROSS, cross_pairs(step, 1))


def swap_cores(block):
    return lax.ppermute(block, "core", [(0, 1), (1, 0)])


def gather_over(block, axes, size):
    copies = jnp.broadcast_to(block[None], (size,) + block.shape)
    return lax.all_to_all(copies, axes, 0, 0, tiled=True)


def sum_over(block, axes, size):
    return jnp.sum(gather_over(block, axes, size), axis=0)


def gather_ring(block, shift):
    across, up, down = shift(block, 2), shift(block, 3), shift(block, 1)
    return [block, up, across, down]


def send_ring(blocks, shift):
    across, up, down = shift(blocks[2], 2), shift(blocks[1], 1), shift(blocks[3], 3)
    return [blocks[0], up, across, down]


def total(blocks):
    return sum(block.astype(jnp.float32) for block in blocks)


def piece_row(core, y, x):
    piece = ((lax.rem(x, 2) * 4 + y) * 2 + core) * 2 + lax.div(x, 2)
    return pl.multiple_of(piece * PIECE, PIECE)


def step_columns(step):
    return pl.ds(pl.multiple_of(step * STEP, STEP), STEP)


def steps(body, first=0, last=STEPS, unroll=False):
    lax.fori_loop(first, last, lambda j, carry: (body(j), carry)[1], 0, unroll=unroll)


def forward_kernel(place, targets, weight, *rest):
    blocks = rest[:8]
    gathered, capped_out, stats_out, weight_held, rows_held, logits, weight_sems, row_sems, out_sem = rest[8:]
    core, y, x, position = place[0], place[1], place[2], place[3]

    def half_columns(half):
        return pl.ds(pl.multiple_of(half * HALF, HALF), HALF)

    def half_rows(half):
        return rows_held.at[:, half_columns(half)]

    def weight_copy(j):
        columns = step_columns(j)
        return pltpu.make_async_copy(weight.at[:, columns], weight_held.at[:, columns], weight_sems.at[j])

    def place_blocks(half, held):
        def pieces(inner, carry):
            for outer in range(4):
                up_y = jnp.where(half == 0, outer, inner)
                up_x = jnp.where(half == 0, inner, outer)
                for owner in range(2):
                    row = piece_row(owner, lax.rem(y + up_y, 4), lax.rem(x + up_x, 4))
                    pltpu.make_async_copy(
                        held[outer].at[inner, owner],
                        rows_held.at[pl.ds(row, PIECE), half_columns(half)],
                        row_sems.at[half],
                    ).start()
            return carry

        lax.fori_loop(0, 4, pieces, 0)

    def multiply(j):
        weight_copy(j).wait()
        columns = step_columns(j)
        logits[...] += lax.dot_general(
            weight_held[:, columns],
            rows_held[:, columns],
            (((1,), (1,)), ((), ())),
            preferred_element_type=jnp.float32,
        )

    steps(lambda j: weight_copy(j).start(), 0, HALF_STEPS)
    place_blocks(core, blocks[:4])
    steps(lambda j: weight_copy(j).start(), HALF_STEPS, STEPS)
    place_blocks(1 - core, blocks[4:])
    logits[...] = jnp.zeros_like(logits)
    pltpu.make_async_copy(half_rows(0), half_rows(0), row_sems.at[0]).wait()
    steps(multiply, 0, HALF_STEPS, True)
    pltpu.make_async_copy(half_rows(1), half_rows(1), row_sems.at[1]).wait()
    out_copy = pltpu.make_async_copy(rows_held, gathered, out_sem)
    out_copy.start()
    steps(multiply, HALF_STEPS, STEPS, True)

    def finish(k, carry):
        rows = pl.ds(pl.multiple_of(k * 64, 64), 64)
        capped = cap_value * jnp.tanh(logits[rows, :] / cap_value)
        capped_out[rows, :] = capped
        powers = jnp.exp(capped - cap_value)
        entry = position * VOCAB_ROWS + k * 64 + lax.broadcasted_iota(jnp.int32, capped.shape, 0)
        hit = targets[...] == entry
        return (
            carry[0] + jnp.sum(powers, axis=0, keepdims=True),
            carry[1] + jnp.sum(powers * capped, axis=0, keepdims=True),
            carry[2] + jnp.sum(jnp.where(hit, capped, 0.0), axis=0, keepdims=True),
        )

    sums = lax.fori_loop(0, VOCAB_ROWS // 64, finish, (jnp.zeros((1, TOKENS), jnp.float32),) * 3)
    for k in range(3):
        stats_out[k : k + 1, :] = sums[k]
    out_copy.wait()


SCALARS = pl.BlockSpec(memory_space=pltpu.SMEM)
IN_VMEM = pl.BlockSpec(memory_space=pltpu.VMEM)
IN_HBM = pl.BlockSpec(memory_space=pltpu.HBM)
ANYWHERE = pl.BlockSpec(memory_space=pl.ANY)


def forward(place, targets, weight, blocks):
    return pl.pallas_call(
        forward_kernel,
        out_shape=(
            jax.ShapeDtypeStruct((TOKENS, WIDTH), jnp.bfloat16),
            jax.ShapeDtypeStruct((VOCAB_ROWS, TOKENS), jnp.float32),
            jax.ShapeDtypeStruct((3, TOKENS), jnp.float32),
        ),
        in_specs=[SCALARS, IN_VMEM, IN_HBM] + [ANYWHERE] * 8,
        out_specs=(IN_HBM, IN_VMEM, IN_VMEM),
        scratch_shapes=[
            pltpu.VMEM((VOCAB_ROWS, WIDTH), jnp.bfloat16),
            pltpu.VMEM((TOKENS, WIDTH), jnp.bfloat16),
            pltpu.VMEM((VOCAB_ROWS, TOKENS), jnp.float32),
            pltpu.SemaphoreType.DMA((STEPS,)),
            pltpu.SemaphoreType.DMA((2,)),
            pltpu.SemaphoreType.DMA,
        ],
        compiler_params=pltpu.CompilerParams(vmem_limit_bytes=50 << 20),
        cost_estimate=pl.CostEstimate(
            flops=2 * VOCAB_ROWS * TOKENS * WIDTH, bytes_accessed=16 << 20, transcendentals=1 << 19
        ),
        name="forward",
    )(place, targets, weight, *blocks)


def far_kernel(
    place, targets, capped, totals, weight, grad_out, turned_out, far_out,
    weight_held, far_held, weight_sems, out_sems,
):
    core, position = place[0], place[3]

    def arrival(j):
        columns = step_columns((1 - core) * HALF_STEPS + j)
        return pltpu.make_async_copy(
            weight.at[:, columns], weight_held.at[:, step_columns(j)], weight_sems.at[j]
        )

    def leaving(j):
        columns = step_columns(j)
        return pltpu.make_async_copy(far_held.at[:, columns], far_out.at[:, columns], out_sems.at[j])

    steps(lambda j: arrival(j).start(), 0, HALF_STEPS)
    log_total = cap_value + jnp.log(totals[0:1, :])
    mean_logit = totals[1:2, :] / totals[0:1, :]

    def gradient(k):
        rows = pl.ds(pl.multiple_of(k * 128, 128), 128)
        values = capped[rows, :]
        probs = jnp.exp(values - log_total)
        entry = position * VOCAB_ROWS + k * 128 + lax.broadcasted_iota(jnp.int32, values.shape, 0)
        hit = (targets[...] == entry).astype(jnp.float32)
        raw_grad = probs - hit + entropy_weight * probs * (values - mean_logit)
        ratio = values / cap_value
        grad = raw_grad * (1.0 - ratio * ratio)
        grad_out[rows, :] = grad.astype(jnp.bfloat16)
        turned_out[:, rows] = grad.T.astype(jnp.bfloat16)

    steps(gradient, 0, VOCAB_ROWS // 128)

    def multiply(j):
        arrival(j).wait()
        columns = step_columns(j)
        far_held[:, columns] = jnp.dot(
            turned_out[...], weight_held[:, columns], preferred_element_type=jnp.float32
        ).astype(jnp.bfloat16)
        leaving(j).start()

    steps(multiply, 0, HALF_STEPS, True)
    steps(lambda j: leaving(j).wait(), 0, HALF_STEPS)


def far_gradient(place, targets, capped, totals, weight):
    return pl.pallas_call(
        far_kernel,
        out_shape=(
            jax.ShapeDtypeStruct((VOCAB_ROWS, TOKENS), jnp.bfloat16),
            jax.ShapeDtypeStruct((TOKENS, VOCAB_ROWS), jnp.bfloat16),
            jax.ShapeDtypeStruct((TOKENS, HALF), jnp.bfloat16),
        ),
        in_specs=[SCALARS, IN_VMEM, IN_VMEM, IN_VMEM, IN_HBM],
        out_specs=(IN_VMEM, IN_VMEM, ANYWHERE),
        scratch_shapes=[
            pltpu.VMEM((VOCAB_ROWS, HALF), jnp.bfloat16),
            pltpu.VMEM((TOKENS, HALF), jnp.bfloat16),
            pltpu.SemaphoreType.DMA((HALF_STEPS,)),
            pltpu.SemaphoreType.DMA((HALF_STEPS,)),
        ],
        compiler_params=pltpu.CompilerParams(vmem_limit_bytes=52 << 20),
        cost_estimate=pl.CostEstimate(
            flops=VOCAB_ROWS * TOKENS * WIDTH, bytes_accessed=9 << 20, transcendentals=1 << 18
        ),
        name="far_gradient",
    )(place, targets, capped, totals, weight)


def near_kernel(place, turned, weight, arrived, gathered, *rest):
    sends = rest[:4]
    weight_held, arrived_held, rows_held, held, in_sems, out_sems = rest[4:]
    core, y, x = place[0], place[1], place[2]

    def arrivals(j):
        columns, own = step_columns(core * HALF_STEPS + j), step_columns(j)
        return [
            pltpu.make_async_copy(weight.at[:, columns], weight_held.at[:, own], in_sems.at[0, j]),
            pltpu.make_async_copy(arrived.at[:, own], arrived_held.at[:, own], in_sems.at[1, j]),
            pltpu.make_async_copy(gathered.at[:, columns], rows_held.at[:, own], in_sems.at[2, j]),
        ]

    def begin(j):
        for copy in arrivals(j):
            copy.start()

    def multiply(j):
        for copy in arrivals(j):
            copy.wait()
        columns = step_columns(j)
        part = jnp.dot(turned[...], weight_held[:, columns], preferred_element_type=jnp.float32)
        part = part + arrived_held[:, columns].astype(jnp.float32)
        gain = jnp.sum(part * rows_held[:, columns].astype(jnp.float32), axis=0, keepdims=True)
        high = gain.astype(jnp.bfloat16).astype(jnp.float32)
        row = lax.broadcasted_iota(jnp.int32, (PIECE, STEP), 0)
        gain_piece = jnp.where(row == 0, high, jnp.where(row == 1, gain - high, 0.0)).astype(jnp.bfloat16)
        for k in range(4):
            held[k, 8, :, columns] = gain_piece
        rounded = part.astype(jnp.bfloat16)
        for to_y in range(4):
            for to_x in range(4):
                up_y, up_x = lax.rem(to_y + 4 - y, 4), lax.rem(to_x + 4 - x, 4)
                outer, inner = jnp.where(core == 0, up_y, up_x), jnp.where(core == 0, up_x, up_y)
                for owner in range(2):
                    row = (((to_x % 2 * 4 + to_y) * 2 + owner) * 2 + to_x // 2) * PIECE
                    held[outer, inner * 2 + owner, :, columns] = rounded[row : row + PIECE]

    steps(begin, 0, HALF_STEPS)
    steps(multiply, 0, HALF_STEPS, True)
    leaving = [pltpu.make_async_copy(held.at[k], sends[k], out_sems.at[k]) for k in range(4)]
    for copy in leaving:
        copy.start()
    for copy in leaving:
        copy.wait()


def near_gradient(place, turned, weight, arrived, gathered):
    return pl.pallas_call(
        near_kernel,
        out_shape=[jax.ShapeDtypeStruct((9, PIECE, HALF), jnp.bfloat16)] * 4,
        in_specs=[SCALARS, IN_VMEM, IN_HBM, ANYWHERE, IN_HBM],
        out_specs=[ANYWHERE] * 4,
        scratch_shapes=[
            pltpu.VMEM((VOCAB_ROWS, HALF), jnp.bfloat16),
            pltpu.VMEM((TOKENS, HALF), jnp.bfloat16),
            pltpu.VMEM((TOKENS, HALF), jnp.bfloat16),
            pltpu.VMEM((4, 9, PIECE, HALF), jnp.bfloat16),
            pltpu.SemaphoreType.DMA((3, HALF_STEPS)),
            pltpu.SemaphoreType.DMA((4,)),
        ],
        compiler_params=pltpu.CompilerParams(vmem_limit_bytes=45 << 20),
        cost_estimate=pl.CostEstimate(
            flops=VOCAB_ROWS * TOKENS * WIDTH, bytes_accessed=12 << 20, transcendentals=0
        ),
        name="near_gradient",
    )(place, turned, weight, arrived, gathered)


def weight_kernel(grad, gathered, out, rows_held, out_held, in_sems, out_sems):
    def arrival(j):
        columns = step_columns(j)
        return pltpu.make_async_copy(gathered.at[:, columns], rows_held.at[:, columns], in_sems.at[j])

    def leaving(j):
        columns = step_columns(j)
        return pltpu.make_async_copy(out_held.at[:, columns], out.at[:, columns], out_sems.at[j])

    def multiply(j):
        arrival(j).wait()
        columns = step_columns(j)
        out_held[:, columns] = jnp.dot(
            grad[...], rows_held[:, columns], preferred_element_type=jnp.float32
        ).astype(jnp.bfloat16)
        leaving(j).start()

    steps(lambda j: arrival(j).start())
    steps(multiply)
    steps(lambda j: leaving(j).wait())


def weight_gradient(grad, gathered):
    return pl.pallas_call(
        weight_kernel,
        out_shape=jax.ShapeDtypeStruct((VOCAB_ROWS, WIDTH), jnp.bfloat16),
        in_specs=[IN_VMEM, IN_HBM],
        out_specs=IN_HBM,
        scratch_shapes=[
            pltpu.VMEM((TOKENS, WIDTH), jnp.bfloat16),
            pltpu.VMEM((VOCAB_ROWS, WIDTH), jnp.bfloat16),
            pltpu.SemaphoreType.DMA((STEPS,)),
            pltpu.SemaphoreType.DMA((STEPS,)),
        ],
        compiler_params=pltpu.CompilerParams(vmem_limit_bytes=50 << 20),
        cost_estimate=pl.CostEstimate(
            flops=2 * VOCAB_ROWS * TOKENS * WIDTH, bytes_accessed=10 << 20, transcendentals=0
        ),
        name="weight_gradient",
    )(grad, gathered)


def on_device(hidden, norm_gain, weight, targets):
    core, y, position = lax.axis_index("core"), lax.axis_index("y"), lax.axis_index(AXES)
    x = lax.axis_index("x_hi") * 2 + lax.axis_index("x_lo")
    place = jnp.stack([core, y, x, position]).astype(jnp.int32)
    ids = targets.reshape(1, TOKENS)

    values = hidden.astype(jnp.float32)
    inverse = lax.rsqrt(jnp.mean(values * values, axis=-1, keepdims=True) + epsilon)
    unit_rows = values * inverse
    normed = (unit_rows * norm_gain).astype(jnp.bfloat16)

    halves = normed.reshape(2, 2, HALF).transpose(1, 0, 2)
    halves = jnp.broadcast_to(halves[:, None], (2, 8, 2, HALF)).reshape(16, 2, HALF)
    line = lax.all_to_all(halves, ("core", "z"), 0, 0, tiled=True).reshape(2, PIECE, HALF)
    blocks = gather_ring(jnp.stack(gather_ring(line, shift_first)), shift_second)
    blocks = blocks + [swap_cores(block) for block in blocks]

    gathered, capped, stats = forward(place, ids, weight, blocks)
    stats = sum_over(stats, PLANE, 16)
    stats = sum_over(stats, ("core", "z"), 16)

    grad, turned, far_part = far_gradient(place, ids, capped, stats, weight)
    arrived = swap_cores(far_part)
    sends = near_gradient(place, turned, weight, arrived, gathered)

    def gain_rows(piece):
        gain = piece[0:1] + piece[1:2]
        high = lax.reduce_precision(gain, 8, 7)
        return jnp.concatenate([high, gain - high], axis=0).astype(jnp.bfloat16)

    own, *others = sends
    grad, own = lax.optimization_barrier((grad, own))
    parts = send_ring([own, *others], shift_second)
    grad_weight = weight_gradient(grad, gathered)
    grad_weight, *parts = lax.optimization_barrier((grad_weight, *parts))
    half_sum = total(parts)
    half_rows = half_sum[:8].astype(jnp.bfloat16)
    gain_piece = jnp.pad(gain_rows(half_sum[8]), ((0, PIECE - 2), (0, 0)))[None]
    pieces = [jnp.concatenate([half_rows[2 * k : 2 * k + 2], gain_piece], axis=0) for k in range(4)]
    line_sum = total(send_ring(pieces, shift_first))
    line_part = line_sum[:2].astype(jnp.bfloat16)
    gain_pair = gain_rows(line_sum[2])
    message = jnp.concatenate(
        [line_part.reshape(16, 2, HALF), jnp.broadcast_to(gain_pair[None], (16, 2, HALF))], axis=1
    )
    line_parts = lax.all_to_all(message, ("core", "z"), 0, 0, tiled=True)
    sums = jnp.sum(line_parts.astype(jnp.float32).reshape(2, 8, 4, HALF), axis=1)
    grad_normed = jnp.concatenate([sums[0, :2], sums[1, :2]], axis=1)
    grad_gain = (sums[:, 2] + sums[:, 3]).reshape(WIDTH) / norm_gain

    total_exp, total_weighted, target_logit = stats
    log_total = cap_value + jnp.log(total_exp)
    mean_logit = total_weighted / total_exp
    every_loss = log_total - target_logit - entropy_weight * (log_total - mean_logit)
    token_loss = lax.dynamic_slice_in_dim(every_loss, position * 2, 2, 0)
    scaled = norm_gain * grad_normed
    grad_hidden = (
        scaled - unit_rows * jnp.mean(scaled * unit_rows, axis=-1, keepdims=True)
    ) * inverse
    return (token_loss, grad_hidden, grad_weight, grad_gain)


def solution(mesh):
    fine = Mesh(mesh.devices.reshape(2, 4, 2, 2, 8), AXES)
    rows = P(AXES, None)
    return jax.shard_map(
        on_device,
        mesh=fine,
        in_specs=(rows, P(), rows, P()),
        out_specs=(P(AXES), rows, rows, P()),
        check_vma=False,
    )
```

```python
import jax
import jax.numpy as jnp
from jax import lax
from jax.experimental import pallas as pl
from jax.experimental.pallas import tpu as pltpu
from jax.sharding import Mesh, PartitionSpec as P

epsilon = 1e-06
cap_value = 30.0
entropy_weight = 0.2

AXES = ("x_lo", "y", "core", "x_hi", "z")
PLANE = ("x_lo", "y", "x_hi")
WIDTH = 4608
HALF = WIDTH // 2
TOKENS = 512
VOCAB_ROWS = 512
PIECE = 16
STEP = 768
STEPS = WIDTH // STEP
HALF_STEPS = HALF // STEP

CROSS = ("x_lo", "y", "core", "x_hi")


def cross_pairs(step, x_core):
    index = lambda x, y, core: ((x % 2 * 4 + y) * 2 + core) * 2 + x // 2
    pairs = []
    for x in range(4):
        for y in range(4):
            for core in range(2):
                to = ((x + step) % 4, y) if core == x_core else (x, (y + step) % 4)
                pairs.append((index(x, y, core), index(*to, core)))
    return pairs


def shift_first(block, step):
    return lax.ppermute(block, CROSS, cross_pairs(step, 0))


def shift_second(block, step):
    return lax.ppermute(block, CROSS, cross_pairs(step, 1))


def swap_cores(block):
    return lax.ppermute(block, "core", [(0, 1), (1, 0)])


def gather_over(block, axes, size):
    copies = jnp.broadcast_to(block[None], (size,) + block.shape)
    return lax.all_to_all(copies, axes, 0, 0, tiled=True)


def sum_over(block, axes, size):
    return jnp.sum(gather_over(block, axes, size), axis=0)


def gather_ring(block, shift):
    across, up, down = shift(block, 2), shift(block, 3), shift(block, 1)
    return [block, up, across, down]


def send_ring(blocks, shift):
    across, up, down = shift(blocks[2], 2), shift(blocks[1], 1), shift(blocks[3], 3)
    return [blocks[0], up, across, down]


def total(blocks):
    return sum(block.astype(jnp.float32) for block in blocks)


def piece_row(core, y, x):
    piece = ((lax.rem(x, 2) * 4 + y) * 2 + core) * 2 + lax.div(x, 2)
    return pl.multiple_of(piece * PIECE, PIECE)


def step_columns(step):
    return pl.ds(pl.multiple_of(step * STEP, STEP), STEP)


def steps(body, first=0, last=STEPS):
    lax.fori_loop(first, last, lambda j, carry: (body(j), carry)[1], 0)


def forward_kernel(place, targets, weight, *rest):
    blocks = rest[:8]
    gathered, capped_out, stats_out, weight_held, rows_held, logits, weight_sems, row_sems, out_sem = rest[8:]
    core, y, x, position = place[0], place[1], place[2], place[3]

    def half_columns(half):
        return pl.ds(pl.multiple_of(half * HALF, HALF), HALF)

    def half_rows(half):
        return rows_held.at[:, half_columns(half)]

    def weight_copy(j):
        columns = half_columns(j)
        return pltpu.make_async_copy(weight.at[:, columns], weight_held.at[:, columns], weight_sems.at[j])

    def place_blocks(half, held):
        def pieces(inner, carry):
            for outer in range(4):
                up_y = jnp.where(half == 0, outer, inner)
                up_x = jnp.where(half == 0, inner, outer)
                for owner in range(2):
                    row = piece_row(owner, lax.rem(y + up_y, 4), lax.rem(x + up_x, 4))
                    pltpu.make_async_copy(
                        held[outer].at[inner, owner],
                        rows_held.at[pl.ds(row, PIECE), half_columns(half)],
                        row_sems.at[half],
                    ).start()
            return carry

        lax.fori_loop(0, 4, pieces, 0)

    def multiply(j):
        weight_copy(j).wait()
        columns = half_columns(j)
        logits[...] += lax.dot_general(
            weight_held[:, columns],
            rows_held[:, columns],
            (((1,), (1,)), ((), ())),
            preferred_element_type=jnp.float32,
        )

    steps(lambda j: weight_copy(j).start(), 0, 1)
    place_blocks(core, blocks[:4])
    steps(lambda j: weight_copy(j).start(), 1, 2)
    place_blocks(1 - core, blocks[4:])
    logits[...] = jnp.zeros_like(logits)
    pltpu.make_async_copy(half_rows(0), half_rows(0), row_sems.at[0]).wait()
    steps(multiply, 0, 1)
    pltpu.make_async_copy(half_rows(1), half_rows(1), row_sems.at[1]).wait()
    out_copy = pltpu.make_async_copy(rows_held, gathered, out_sem)
    out_copy.start()
    steps(multiply, 1, 2)

    def finish(k, carry):
        rows = pl.ds(pl.multiple_of(k * 64, 64), 64)
        capped = cap_value * jnp.tanh(logits[rows, :] / cap_value)
        capped_out[rows, :] = capped
        powers = jnp.exp(capped - cap_value)
        entry = position * VOCAB_ROWS + k * 64 + lax.broadcasted_iota(jnp.int32, capped.shape, 0)
        hit = targets[...] == entry
        return (
            carry[0] + jnp.sum(powers, axis=0, keepdims=True),
            carry[1] + jnp.sum(powers * capped, axis=0, keepdims=True),
            carry[2] + jnp.sum(jnp.where(hit, capped, 0.0), axis=0, keepdims=True),
        )

    sums = lax.fori_loop(0, VOCAB_ROWS // 64, finish, (jnp.zeros((1, TOKENS), jnp.float32),) * 3)
    for k in range(3):
        stats_out[k : k + 1, :] = sums[k]
    out_copy.wait()


SCALARS = pl.BlockSpec(memory_space=pltpu.SMEM)
IN_VMEM = pl.BlockSpec(memory_space=pltpu.VMEM)
IN_HBM = pl.BlockSpec(memory_space=pltpu.HBM)
ANYWHERE = pl.BlockSpec(memory_space=pl.ANY)


def forward(place, targets, weight, blocks):
    return pl.pallas_call(
        forward_kernel,
        out_shape=(
            jax.ShapeDtypeStruct((TOKENS, WIDTH), jnp.bfloat16),
            jax.ShapeDtypeStruct((VOCAB_ROWS, TOKENS), jnp.float32),
            jax.ShapeDtypeStruct((3, TOKENS), jnp.float32),
        ),
        in_specs=[SCALARS, IN_VMEM, IN_HBM] + [ANYWHERE] * 8,
        out_specs=(IN_HBM, IN_VMEM, IN_VMEM),
        scratch_shapes=[
            pltpu.VMEM((VOCAB_ROWS, WIDTH), jnp.bfloat16),
            pltpu.VMEM((TOKENS, WIDTH), jnp.bfloat16),
            pltpu.VMEM((VOCAB_ROWS, TOKENS), jnp.float32),
            pltpu.SemaphoreType.DMA((STEPS,)),
            pltpu.SemaphoreType.DMA((2,)),
            pltpu.SemaphoreType.DMA,
        ],
        compiler_params=pltpu.CompilerParams(vmem_limit_bytes=50 << 20),
        cost_estimate=pl.CostEstimate(
            flops=2 * VOCAB_ROWS * TOKENS * WIDTH, bytes_accessed=16 << 20, transcendentals=1 << 19
        ),
        name="forward",
    )(place, targets, weight, *blocks)


def far_kernel(
    place, targets, capped, totals, weight, grad_out, turned_out, far_out,
    weight_held, far_held, weight_sems, out_sems,
):
    core, position = place[0], place[3]

    def arrival(j):
        columns = step_columns((1 - core) * HALF_STEPS + j)
        return pltpu.make_async_copy(
            weight.at[:, columns], weight_held.at[:, step_columns(j)], weight_sems.at[j]
        )

    def leaving(j):
        columns = step_columns(j)
        return pltpu.make_async_copy(far_held.at[:, columns], far_out.at[:, columns], out_sems.at[j])

    steps(lambda j: arrival(j).start(), 0, HALF_STEPS)
    log_total = cap_value + jnp.log(totals[0:1, :])
    mean_logit = totals[1:2, :] / totals[0:1, :]

    def gradient(k):
        rows = pl.ds(pl.multiple_of(k * 128, 128), 128)
        values = capped[rows, :]
        probs = jnp.exp(values - log_total)
        entry = position * VOCAB_ROWS + k * 128 + lax.broadcasted_iota(jnp.int32, values.shape, 0)
        hit = (targets[...] == entry).astype(jnp.float32)
        raw_grad = probs - hit + entropy_weight * probs * (values - mean_logit)
        ratio = values / cap_value
        grad = raw_grad * (1.0 - ratio * ratio)
        grad_out[rows, :] = grad.astype(jnp.bfloat16)
        turned_out[:, rows] = grad.T.astype(jnp.bfloat16)

    steps(gradient, 0, VOCAB_ROWS // 128)

    def multiply(j):
        arrival(j).wait()
        columns = step_columns(j)
        far_held[:, columns] = jnp.dot(
            turned_out[...], weight_held[:, columns], preferred_element_type=jnp.float32
        ).astype(jnp.bfloat16)
        leaving(j).start()

    steps(multiply, 0, HALF_STEPS)
    steps(lambda j: leaving(j).wait(), 0, HALF_STEPS)


def far_gradient(place, targets, capped, totals, weight):
    return pl.pallas_call(
        far_kernel,
        out_shape=(
            jax.ShapeDtypeStruct((VOCAB_ROWS, TOKENS), jnp.bfloat16),
            jax.ShapeDtypeStruct((TOKENS, VOCAB_ROWS), jnp.bfloat16),
            jax.ShapeDtypeStruct((TOKENS, HALF), jnp.bfloat16),
        ),
        in_specs=[SCALARS, IN_VMEM, IN_VMEM, IN_VMEM, IN_HBM],
        out_specs=(IN_VMEM, IN_VMEM, ANYWHERE),
        scratch_shapes=[
            pltpu.VMEM((VOCAB_ROWS, HALF), jnp.bfloat16),
            pltpu.VMEM((TOKENS, HALF), jnp.bfloat16),
            pltpu.SemaphoreType.DMA((HALF_STEPS,)),
            pltpu.SemaphoreType.DMA((HALF_STEPS,)),
        ],
        compiler_params=pltpu.CompilerParams(vmem_limit_bytes=52 << 20),
        cost_estimate=pl.CostEstimate(
            flops=VOCAB_ROWS * TOKENS * WIDTH, bytes_accessed=9 << 20, transcendentals=1 << 18
        ),
        name="far_gradient",
    )(place, targets, capped, totals, weight)


def near_kernel(place, turned, weight, arrived, gathered, *rest):
    sends = rest[:4]
    weight_held, arrived_held, rows_held, held, in_sems, out_sems = rest[4:]
    core, y, x = place[0], place[1], place[2]

    def arrivals(j):
        columns, own = step_columns(core * HALF_STEPS + j), step_columns(j)
        return [
            pltpu.make_async_copy(weight.at[:, columns], weight_held.at[:, own], in_sems.at[0, j]),
            pltpu.make_async_copy(arrived.at[:, own], arrived_held.at[:, own], in_sems.at[1, j]),
            pltpu.make_async_copy(gathered.at[:, columns], rows_held.at[:, own], in_sems.at[2, j]),
        ]

    def begin(j):
        for copy in arrivals(j):
            copy.start()

    def multiply(j):
        for copy in arrivals(j):
            copy.wait()
        columns = step_columns(j)
        part = jnp.dot(turned[...], weight_held[:, columns], preferred_element_type=jnp.float32)
        part = part + arrived_held[:, columns].astype(jnp.float32)
        gain = jnp.sum(part * rows_held[:, columns].astype(jnp.float32), axis=0, keepdims=True)
        high = gain.astype(jnp.bfloat16).astype(jnp.float32)
        row = lax.broadcasted_iota(jnp.int32, (PIECE, STEP), 0)
        gain_piece = jnp.where(row == 0, high, jnp.where(row == 1, gain - high, 0.0)).astype(jnp.bfloat16)
        for k in range(4):
            held[k, 8, :, columns] = gain_piece
        rounded = part.astype(jnp.bfloat16)
        for to_y in range(4):
            for to_x in range(4):
                up_y, up_x = lax.rem(to_y + 4 - y, 4), lax.rem(to_x + 4 - x, 4)
                outer, inner = jnp.where(core == 0, up_y, up_x), jnp.where(core == 0, up_x, up_y)
                for owner in range(2):
                    row = (((to_x % 2 * 4 + to_y) * 2 + owner) * 2 + to_x // 2) * PIECE
                    held[outer, inner * 2 + owner, :, columns] = rounded[row : row + PIECE]

    steps(begin, 0, HALF_STEPS)
    steps(multiply, 0, HALF_STEPS)
    leaving = [pltpu.make_async_copy(held.at[k], sends[k], out_sems.at[k]) for k in range(4)]
    for copy in leaving:
        copy.start()
    for copy in leaving:
        copy.wait()


def near_gradient(place, turned, weight, arrived, gathered):
    return pl.pallas_call(
        near_kernel,
        out_shape=[jax.ShapeDtypeStruct((9, PIECE, HALF), jnp.bfloat16)] * 4,
        in_specs=[SCALARS, IN_VMEM, IN_HBM, ANYWHERE, IN_HBM],
        out_specs=[ANYWHERE] * 4,
        scratch_shapes=[
            pltpu.VMEM((VOCAB_ROWS, HALF), jnp.bfloat16),
            pltpu.VMEM((TOKENS, HALF), jnp.bfloat16),
            pltpu.VMEM((TOKENS, HALF), jnp.bfloat16),
            pltpu.VMEM((4, 9, PIECE, HALF), jnp.bfloat16),
            pltpu.SemaphoreType.DMA((3, HALF_STEPS)),
            pltpu.SemaphoreType.DMA((4,)),
        ],
        compiler_params=pltpu.CompilerParams(vmem_limit_bytes=45 << 20),
        cost_estimate=pl.CostEstimate(
            flops=VOCAB_ROWS * TOKENS * WIDTH, bytes_accessed=12 << 20, transcendentals=0
        ),
        name="near_gradient",
    )(place, turned, weight, arrived, gathered)


def weight_kernel(grad, gathered, out, rows_held, out_held, in_sems, out_sems):
    def arrival(j):
        columns = step_columns(j)
        return pltpu.make_async_copy(gathered.at[:, columns], rows_held.at[:, columns], in_sems.at[j])

    def leaving(j):
        columns = step_columns(j)
        return pltpu.make_async_copy(out_held.at[:, columns], out.at[:, columns], out_sems.at[j])

    def multiply(j):
        arrival(j).wait()
        columns = step_columns(j)
        out_held[:, columns] = jnp.dot(
            grad[...], rows_held[:, columns], preferred_element_type=jnp.float32
        ).astype(jnp.bfloat16)
        leaving(j).start()

    steps(lambda j: arrival(j).start())
    steps(multiply)
    steps(lambda j: leaving(j).wait())


def weight_gradient(grad, gathered):
    return pl.pallas_call(
        weight_kernel,
        out_shape=jax.ShapeDtypeStruct((VOCAB_ROWS, WIDTH), jnp.bfloat16),
        in_specs=[IN_VMEM, IN_HBM],
        out_specs=IN_HBM,
        scratch_shapes=[
            pltpu.VMEM((TOKENS, WIDTH), jnp.bfloat16),
            pltpu.VMEM((VOCAB_ROWS, WIDTH), jnp.bfloat16),
            pltpu.SemaphoreType.DMA((STEPS,)),
            pltpu.SemaphoreType.DMA((STEPS,)),
        ],
        compiler_params=pltpu.CompilerParams(vmem_limit_bytes=50 << 20),
        cost_estimate=pl.CostEstimate(
            flops=2 * VOCAB_ROWS * TOKENS * WIDTH, bytes_accessed=10 << 20, transcendentals=0
        ),
        name="weight_gradient",
    )(grad, gathered)


def on_device(hidden, norm_gain, weight, targets):
    core, y, position = lax.axis_index("core"), lax.axis_index("y"), lax.axis_index(AXES)
    x = lax.axis_index("x_hi") * 2 + lax.axis_index("x_lo")
    place = jnp.stack([core, y, x, position]).astype(jnp.int32)
    ids = targets.reshape(1, TOKENS)

    values = hidden.astype(jnp.float32)
    inverse = lax.rsqrt(jnp.mean(values * values, axis=-1, keepdims=True) + epsilon)
    unit_rows = values * inverse
    normed = (unit_rows * norm_gain).astype(jnp.bfloat16)

    halves = normed.reshape(2, 2, HALF).transpose(1, 0, 2)
    halves = jnp.broadcast_to(halves[:, None], (2, 8, 2, HALF)).reshape(16, 2, HALF)
    line = lax.all_to_all(halves, ("core", "z"), 0, 0, tiled=True).reshape(2, PIECE, HALF)
    blocks = gather_ring(jnp.stack(gather_ring(line, shift_first)), shift_second)
    blocks = blocks + [swap_cores(block) for block in blocks]

    gathered, capped, stats = forward(place, ids, weight, blocks)
    stats = sum_over(stats, PLANE, 16)
    stats = sum_over(stats, ("core", "z"), 16)

    grad, turned, far_part = far_gradient(place, ids, capped, stats, weight)
    arrived = swap_cores(far_part)
    sends = near_gradient(place, turned, weight, arrived, gathered)

    def gain_rows(piece):
        gain = piece[0:1] + piece[1:2]
        high = lax.reduce_precision(gain, 8, 7)
        return jnp.concatenate([high, gain - high], axis=0).astype(jnp.bfloat16)

    own, *others = sends
    grad, own = lax.optimization_barrier((grad, own))
    parts = send_ring([own, *others], shift_second)
    grad_weight = weight_gradient(grad, gathered)
    grad_weight, *parts = lax.optimization_barrier((grad_weight, *parts))
    half_sum = total(parts)
    half_rows = half_sum[:8].astype(jnp.bfloat16)
    gain_piece = jnp.pad(gain_rows(half_sum[8]), ((0, PIECE - 2), (0, 0)))[None]
    pieces = [jnp.concatenate([half_rows[2 * k : 2 * k + 2], gain_piece], axis=0) for k in range(4)]
    line_sum = total(send_ring(pieces, shift_first))
    line_part = line_sum[:2].astype(jnp.bfloat16)
    gain_pair = gain_rows(line_sum[2])
    message = jnp.concatenate(
        [line_part.reshape(16, 2, HALF), jnp.broadcast_to(gain_pair[None], (16, 2, HALF))], axis=1
    )
    line_parts = lax.all_to_all(message, ("core", "z"), 0, 0, tiled=True)
    sums = jnp.sum(line_parts.astype(jnp.float32).reshape(2, 8, 4, HALF), axis=1)
    grad_normed = jnp.concatenate([sums[0, :2], sums[1, :2]], axis=1)
    grad_gain = (sums[:, 2] + sums[:, 3]).reshape(WIDTH) / norm_gain

    total_exp, total_weighted, target_logit = stats
    log_total = cap_value + jnp.log(total_exp)
    mean_logit = total_weighted / total_exp
    every_loss = log_total - target_logit - entropy_weight * (log_total - mean_logit)
    token_loss = lax.dynamic_slice_in_dim(every_loss, position * 2, 2, 0)
    scaled = norm_gain * grad_normed
    grad_hidden = (
        scaled - unit_rows * jnp.mean(scaled * unit_rows, axis=-1, keepdims=True)
    ) * inverse
    return (token_loss, grad_hidden, grad_weight, grad_gain)


def solution(mesh):
    fine = Mesh(mesh.devices.reshape(2, 4, 2, 2, 8), AXES)
    rows = P(AXES, None)
    return jax.shard_map(
        on_device,
        mesh=fine,
        in_specs=(rows, P(), rows, P()),
        out_specs=(P(AXES), rows, rows, P()),
        check_vma=False,
    )
```
